32 devices in a mesh: section: 4 (over z), dp: 8 (over y, x, core).
Axes of the slice: x: 2, y: 2, z: 4, core: 2. Of those that a mesh axis runs over, the one named last changes fastest.
Arguments:
- section_inputs: bfloat16 [4, 2048, 896], P('section', 'dp'), may hold values from -44 to 44
- cotangent: bfloat16 [2048, 896], P('dp'), may hold values from -6 to 6
- norm_gain: float32 [4, 896], P('section'), may hold values from 0.25 to 1.75
- quant_gate: bfloat16 [4, 896, 2432], P('section', 'dp'), may hold values from -1 to 1
- quant_up: bfloat16 [4, 896, 2432], P('section', 'dp'), may hold values from -1 to 1
- scales: float32 [4, 2], P('section'), may hold values from 0.04 to 0.08
- down_proj: bfloat16 [4, 2432, 896], P('section'), may hold values from -0.125 to 0.125
- master_gate: float32 [4, 896, 2432], P('section', 'dp'), may hold values from -0.3 to 0.3
- master_up: float32 [4, 896, 2432], P('section', 'dp'), may hold values from -0.3 to 0.3
- moment_gate: float32 [4, 896, 2432], P('section', 'dp'), may hold values from -3 to 3
- moment_up: float32 [4, 896, 2432], P('section', 'dp'), may hold values from -3 to 3
- second_gate: float32 [4, 896, 2432], P('section', 'dp'), may hold values from 0.05 to 1
- second_up: float32 [4, 896, 2432], P('section', 'dp'), may hold values from 0.05 to 1
- next_inputs: bfloat16 [4, 2048, 896], P('section', 'dp'), may hold values from -44 to 44
Outputs:
- input_grads: bfloat16 [4, 2048, 896], P('section', 'dp')
- master_gate_new: float32 [4, 896, 2432], P('section', 'dp')
- master_up_new: float32 [4, 896, 2432], P('section', 'dp')
- moment_gate_new: float32 [4, 896, 2432], P('section', 'dp')
- moment_up_new: float32 [4, 896, 2432], P('section', 'dp')
- second_gate_new: float32 [4, 896, 2432], P('section', 'dp')
- second_up_new: float32 [4, 896, 2432], P('section', 'dp')
- new_scales: float32 [4, 2], P('section')
- next_hidden: bfloat16 [4, 2048, 2432], P('section', 'dp')
The draws below stay inside these ranges and needn't reach their ends.
All inputs are finite; a program needn't handle non-finite values. Where the reference program divides by a largest or mean magnitude, that divisor is 1e-20 or more.
Results may differ from the reference program's by a relative error of at most 0.034.
Values may be sent and summed in bfloat16 or wider, within the bound.
No kernel may reach another device: no remote copies, remote signals or barrier semaphores. Data moves between devices by JAX's collectives and lax.ppermute only.
A program may use at most 128 MiB of HBM per device.

```python
import math
import jax
import jax.numpy as jnp
from jax import lax

D = 896
HID = 2432
TOK_DEV = 256
LAYERS = 4
TOKENS = 2048
N_DP = 8


def activation_law(key):
    subkeys = jax.random.split(key, 3)
    token_scale = jnp.exp(jax.random.uniform(subkeys[1], (LAYERS, TOKENS, 1), jnp.float32, 0.0, math.log(10.0)))
    feature_scale = jnp.exp(jax.random.uniform(subkeys[0], (LAYERS, 1, D), jnp.float32, 0.0, math.log(10.0)))
    values = jax.random.truncated_normal(subkeys[2], -4.0, 4.0, (LAYERS, TOKENS, D), jnp.float32)
    return (0.1 * values * feature_scale * token_scale).astype(jnp.bfloat16)


def master_law(key):
    subkeys = jax.random.split(key, 3)
    row_scale = jnp.exp(jax.random.uniform(subkeys[0], (LAYERS, D, 1), jnp.float32, 0.0, math.log(10.0)))
    column_scale = jnp.exp(jax.random.uniform(subkeys[1], (LAYERS, 1, HID), jnp.float32, 0.0, math.log(10.0)))
    rising = 1.0 + 2.0 * jnp.arange(D, dtype=jnp.float32).reshape(1, D, 1) / D
    values = jax.random.truncated_normal(subkeys[2], -4.0, 4.0, (LAYERS, D, HID), jnp.float32)
    return 0.00025 * values * row_scale * column_scale * rising


def draw_section_inputs(key, part):
    return activation_law(jax.random.fold_in(key, 11))


def draw_next_inputs(key, part):
    return activation_law(jax.random.fold_in(key, 12))


def draw_master_gate(key, part):
    return master_law(jax.random.fold_in(key, 13))


def draw_master_up(key, part):
    return master_law(jax.random.fold_in(key, 14))


def block_levels(key, extent, cuts, smallest, high):
    gain = 1.0
    for position, shards_of in cuts:
        draws = jax.random.uniform(jax.random.fold_in(jax.random.fold_in(key, 6), position), (shards_of,), jnp.float32, smallest / len(cuts), high / len(cuts))
        gain = gain * jnp.repeat(jnp.exp(draws), extent[position] // shards_of).reshape((-1,) + (1,) * (len(extent) - 1 - position))
    return gain


def scatter_about(own_key, extent, deviation, limit, cuts=(), kind=jnp.bfloat16):
    values = jax.random.normal(own_key, extent, jnp.float32) * deviation
    if len(cuts) > 0:
        values = block_levels(own_key, extent, cuts, -0.22, 0.18) * values
    return jnp.clip(values, min=-limit, max=limit).astype(kind)


def setup_inputs(seed: int = 0) -> dict:
    arg_keys = jax.random.split(jax.random.key(seed), 15)
    return {
        "section_inputs": draw_section_inputs(jax.random.fold_in(arg_keys[14], 71), 0),
        "cotangent": scatter_about(arg_keys[1], (TOKENS, D), 1.0, 6.0, ((0, 8),)),
        "norm_gain": jnp.clip(1.0 + 0.15 * jax.random.normal(arg_keys[2], (LAYERS, D), jnp.float32), 0.25, 1.75),
        "quant_gate": jnp.clip(jax.random.uniform(arg_keys[3], (LAYERS, D, HID), jnp.float32, -1.0, 1.0) * block_levels(arg_keys[3], (LAYERS, D, HID), ((0, 4), (1, 8)), -0.4, 0.0), -1.0, 1.0).astype(jnp.bfloat16),
        "quant_up": jnp.clip(jax.random.uniform(arg_keys[4], (LAYERS, D, HID), jnp.float32, -1.0, 1.0) * block_levels(arg_keys[4], (LAYERS, D, HID), ((0, 4), (1, 8)), -0.4, 0.0), -1.0, 1.0).astype(jnp.bfloat16),
        "scales": jnp.clip(jnp.exp(math.log(0.08) - 0.6931472 * jax.random.uniform(arg_keys[5], (LAYERS, 2), jnp.float32) ** block_levels(arg_keys[5], (LAYERS, 2), ((0, 4),), -0.2, 0.2)), 0.04, 0.08),
        "down_proj": scatter_about(arg_keys[6], (LAYERS, HID, D), HID ** -0.5, 0.125, ((0, 4),)),
        "master_gate": draw_master_gate(jax.random.fold_in(arg_keys[14], 71), 0),
        "master_up": draw_master_up(jax.random.fold_in(arg_keys[14], 71), 0),
        "moment_gate": scatter_about(arg_keys[9], (LAYERS, D, HID), 0.5, 3.0, ((0, 4), (1, 8)), jnp.float32),
        "moment_up": scatter_about(arg_keys[10], (LAYERS, D, HID), 0.5, 3.0, ((0, 4), (1, 8)), jnp.float32),
        "second_gate": jnp.clip(jnp.exp(math.log(1.0) - 2.9957323 * jax.random.uniform(arg_keys[11], (LAYERS, D, HID), jnp.float32) ** block_levels(arg_keys[11], (LAYERS, D, HID), ((0, 4), (1, 8)), -0.2, 0.2)), 0.05, 1.0),
        "second_up": jnp.clip(jnp.exp(math.log(1.0) - 2.9957323 * jax.random.uniform(arg_keys[12], (LAYERS, D, HID), jnp.float32) ** block_levels(arg_keys[12], (LAYERS, D, HID), ((0, 4), (1, 8)), -0.2, 0.2)), 0.05, 1.0),
        "next_inputs": draw_next_inputs(jax.random.fold_in(arg_keys[14], 71), 0),
    }


beta_one = 0.9
beta_two = 0.95
learn_rate = 0.002
decay_rate = 0.1
adam_steps = 100.0
norm_eps = 1e-06
adam_eps = 1e-08
scale_eps = 1e-06

def normalize(inputs, norm_gain):
    widened = inputs.astype(jnp.float32)
    inverse = lax.rsqrt(lax.optimization_barrier(jnp.mean(widened * widened, axis=-1, keepdims=True)) + norm_eps)
    return (widened, inverse, (widened * inverse * norm_gain).astype(jnp.bfloat16))

def silu_slope(preact):
    sigmoid = jax.nn.sigmoid(preact)
    return (preact * sigmoid, sigmoid * (1.0 + preact * (1.0 - sigmoid)))

def transposed(first_op, second_op):
    return lax.dot_general(first_op, second_op, (((1,), (1,)), ((), ())), preferred_element_type=jnp.float32)

def block_back(widened, inverse, normed, norm_gain, gate_full, up_full, scale_pair, down_full, upstream):
    gate_pre = jnp.dot(normed, gate_full, preferred_element_type=jnp.float32) * scale_pair[0]
    up_pre = jnp.dot(normed, up_full, preferred_element_type=jnp.float32) * scale_pair[1]
    hidden_grad = transposed(upstream, down_full)
    active, slopes = silu_slope(gate_pre)
    gate_grad = (hidden_grad * up_pre * slopes).astype(jnp.bfloat16)
    up_grad = (hidden_grad * active).astype(jnp.bfloat16)
    normed_grad = transposed(gate_grad, gate_full) * scale_pair[0] + transposed(up_grad, up_full) * scale_pair[1]
    gained = norm_gain * normed_grad
    mean_term = lax.optimization_barrier(jnp.mean(widened * gained, axis=-1, keepdims=True))
    result = upstream.astype(jnp.float32) + inverse * gained - widened * (inverse * inverse * inverse) * mean_term
    return (result.astype(jnp.bfloat16), jnp.concatenate([gate_grad, up_grad], axis=1))

def adam_update(master, moment_old, second_old, gradient):
    moment_one = beta_one * moment_old + (1.0 - beta_one) * gradient
    moment_two = beta_two * second_old + (1.0 - beta_two) * gradient * gradient
    unbiased_one = moment_one / (1.0 - beta_one ** adam_steps)
    unbiased_two = moment_two / (1.0 - beta_two ** adam_steps)
    updated = master - learn_rate * (unbiased_one / (jnp.sqrt(unbiased_two) + adam_eps) + decay_rate * master)
    return (updated, moment_one, moment_two)

def partner_sum(normed, grads_both):
    normed_parts = normed.reshape(N_DP, TOK_DEV, D)
    grad_parts = grads_both.reshape(N_DP, TOK_DEV, 2 * HID)

    def add_partner(running, pieces):
        partial_sum = lax.dot_general(pieces[0], pieces[1], (((0,), (0,)), ((), ())), preferred_element_type=jnp.float32).astype(jnp.bfloat16)
        partial_sum = lax.optimization_barrier(partial_sum)
        return (running + partial_sum.astype(jnp.float32), None)
    running, unused = lax.scan(add_partner, jnp.zeros((D, 2 * HID), jnp.float32), (normed_parts, grad_parts))
    return running

def reference(section_inputs, cotangent, norm_gain, quant_gate, quant_up, scales, down_proj, master_gate, master_up, moment_gate, moment_up, second_gate, second_up, next_inputs):
    upstream = cotangent
    collected = []
    for layer_index in range(LAYERS - 1, -1, -1):
        widened, inverse, normed = normalize(section_inputs[layer_index], norm_gain[layer_index])
        upstream, grads_both = block_back(widened, inverse, normed, norm_gain[layer_index], quant_gate[layer_index], quant_up[layer_index], scales[layer_index], down_proj[layer_index], upstream)
        summed = partner_sum(normed, grads_both)
        new_gate, mom_gate, sec_gate = adam_update(master_gate[layer_index], moment_gate[layer_index], second_gate[layer_index], summed[:, :HID])
        new_up, mom_up, sec_up = adam_update(master_up[layer_index], moment_up[layer_index], second_up[layer_index], summed[:, HID:])
        scale_gate = jnp.max(jnp.abs(new_gate)) + scale_eps
        scale_up = jnp.max(jnp.abs(new_up)) + scale_eps
        quant_next_gate = (new_gate / scale_gate).astype(jnp.bfloat16)
        quant_next_up = (new_up / scale_up).astype(jnp.bfloat16)
        unused_one, unused_two, next_normed = normalize(next_inputs[layer_index], norm_gain[layer_index])
        gate_next = jnp.dot(next_normed, quant_next_gate, preferred_element_type=jnp.float32) * scale_gate
        up_next = jnp.dot(next_normed, quant_next_up, preferred_element_type=jnp.float32) * scale_up
        hidden_next = (jax.nn.silu(gate_next) * up_next).astype(jnp.bfloat16)
        collected.insert(0, (upstream, new_gate, new_up, mom_gate, mom_up, sec_gate, sec_up, jnp.stack([scale_gate, scale_up]), hidden_next))
    return (jnp.stack([entry[0] for entry in collected]), jnp.stack([entry[1] for entry in collected]), jnp.stack([entry[2] for entry in collected]), jnp.stack([entry[3] for entry in collected]), jnp.stack([entry[4] for entry in collected]), jnp.stack([entry[5] for entry in collected]), jnp.stack([entry[6] for entry in collected]), jnp.stack([entry[7] for entry in collected]), jnp.stack([entry[8] for entry in collected]))
```

```python
import jax
import jax.numpy as jnp
from jax import lax
from jax.sharding import PartitionSpec as P

beta_one = 0.9
beta_two = 0.95
learn_rate = 0.002
decay_rate = 0.1
adam_steps = 100.0
norm_eps = 1e-06
adam_eps = 1e-08
scale_eps = 1e-06


def normalize(inputs, norm_gain):
    widened = inputs.astype(jnp.float32)
    inverse = lax.rsqrt(jnp.mean(widened * widened, axis=-1, keepdims=True) + norm_eps)
    return (widened, inverse, (widened * inverse * norm_gain).astype(jnp.bfloat16))


def transposed(first_op, second_op):
    return lax.dot_general(
        first_op, second_op, (((1,), (1,)), ((), ())), preferred_element_type=jnp.float32
    )


def adam_update(master, moment_old, second_old, gradient):
    moment_one = beta_one * moment_old + (1.0 - beta_one) * gradient
    moment_two = beta_two * second_old + (1.0 - beta_two) * gradient * gradient
    unbiased_one = moment_one / (1.0 - beta_one**adam_steps)
    unbiased_two = moment_two / (1.0 - beta_two**adam_steps)
    updated = master - learn_rate * (
        unbiased_one / (jnp.sqrt(unbiased_two) + adam_eps) + decay_rate * master
    )
    return (updated, moment_one, moment_two)


def ring_max(value, axis):
    count = lax.axis_size(axis)
    span = 1
    while span < count:
        pairs = [(source, (source + span) % count) for source in range(count)]
        value = jnp.maximum(value, lax.ppermute(value, axis, pairs))
        span *= 2
    return value


def shards(
    section_inputs,
    cotangent,
    norm_gain,
    quant_gate,
    quant_up,
    scales,
    down_proj,
    master_gate,
    master_up,
    moment_gate,
    moment_up,
    second_gate,
    second_up,
    next_inputs,
):
    gain_row = norm_gain[0]
    scale_pair = scales[0]
    down_local = down_proj[0]
    hidden_count = quant_gate.shape[2]
    sections = lax.axis_size("section")
    position = lax.axis_index("section")
    is_last = position == sections - 1
    both_full = lax.all_gather(
        jnp.concatenate([quant_gate[0], quant_up[0]], axis=1), "dp", axis=0, tiled=True
    )
    widened, inverse, normed = normalize(section_inputs[0], gain_row)
    both_pre = jnp.dot(normed, both_full, preferred_element_type=jnp.float32)
    gate_pre = both_pre[:, :hidden_count] * scale_pair[0]
    up_pre = both_pre[:, hidden_count:] * scale_pair[1]
    sigmoid = jax.nn.sigmoid(gate_pre)
    up_factor = gate_pre * sigmoid
    gate_factor = up_pre * (sigmoid * (1.0 + gate_pre * (1.0 - sigmoid)))
    cubed = inverse * inverse * inverse

    def stage(upstream):
        hidden_grad = transposed(upstream, down_local)
        gate_grad = (hidden_grad * gate_factor).astype(jnp.bfloat16)
        up_grad = (hidden_grad * up_factor).astype(jnp.bfloat16)
        normed_grad = (
            transposed(gate_grad, both_full[:, :hidden_count]) * scale_pair[0]
            + transposed(up_grad, both_full[:, hidden_count:]) * scale_pair[1]
        )
        gained = gain_row * normed_grad
        mean_term = jnp.mean(widened * gained, axis=-1, keepdims=True)
        result = upstream.astype(jnp.float32) + inverse * gained - widened * cubed * mean_term
        return (result.astype(jnp.bfloat16), gate_grad, up_grad)

    upstream = cotangent
    for turn in range(sections):
        result, gate_grad, up_grad = stage(upstream)
        if turn < sections - 1:
            incoming = lax.ppermute(
                result, "section", [(source, source - 1) for source in range(1, sections)]
            )
            upstream = jnp.where(is_last, cotangent, incoming)

    grads_all = jnp.concatenate([gate_grad, up_grad], axis=1)
    summed = lax.psum_scatter(
        lax.dot_general(
            normed, grads_all, (((0,), (0,)), ((), ())), preferred_element_type=jnp.float32
        ).astype(jnp.bfloat16),
        "dp",
        scatter_dimension=0,
        tiled=True,
    ).astype(jnp.float32)
    new_gate, mom_gate, sec_gate = adam_update(
        master_gate[0], moment_gate[0], second_gate[0], summed[:, :hidden_count]
    )
    new_up, mom_up, sec_up = adam_update(
        master_up[0], moment_up[0], second_up[0], summed[:, hidden_count:]
    )
    peaks = jnp.stack([jnp.max(jnp.abs(new_gate)), jnp.max(jnp.abs(new_up))])
    new_scales = ring_max(peaks, "dp") + scale_eps
    unused_one, unused_two, next_normed = normalize(next_inputs[0], gain_row)
    stacked = jnp.concatenate([new_gate, new_up], axis=1).astype(jnp.bfloat16)
    both_next = jnp.dot(
        next_normed,
        lax.all_gather(stacked, "dp", axis=0, tiled=True),
        preferred_element_type=jnp.float32,
    )
    next_hidden = (
        jax.nn.silu(both_next[:, :hidden_count]) * both_next[:, hidden_count:]
    ).astype(jnp.bfloat16)
    return (
        result[None],
        new_gate[None],
        new_up[None],
        mom_gate[None],
        mom_up[None],
        sec_gate[None],
        sec_up[None],
        new_scales[None, :],
        next_hidden[None],
    )


def solution(mesh):
    placed = (
        P("section", "dp", None),
        P("dp", None),
        P("section", None),
        P("section", "dp", None),
        P("section", "dp", None),
        P("section", None),
        P("section", None, None),
        P("section", "dp", None),
        P("section", "dp", None),
        P("section", "dp", None),
        P("section", "dp", None),
        P("section", "dp", None),
        P("section", "dp", None),
        P("section", "dp", None),
    )
    return jax.shard_map(
        shards,
        mesh=mesh,
        in_specs=placed,
        out_specs=(
            P("section", "dp", None),
            P("section", "dp", None),
            P("section", "dp", None),
            P("section", "dp", None),
            P("section", "dp", None),
            P("section", "dp", None),
            P("section", "dp", None),
            P("section", None),
            P("section", "dp", None),
        ),
        check_vma=False,
    )
```

```python
import jax
import jax.numpy as jnp
from jax import lax
from jax.sharding import PartitionSpec as P

beta_one = 0.9
beta_two = 0.95
learn_rate = 0.002
decay_rate = 0.1
adam_steps = 100.0
norm_eps = 1e-06
adam_eps = 1e-08
scale_eps = 1e-06


def normalize(inputs, norm_gain):
    widened = inputs.astype(jnp.float32)
    inverse = lax.rsqrt(jnp.mean(widened * widened, axis=-1, keepdims=True) + norm_eps)
    return (widened, inverse, (widened * inverse * norm_gain).astype(jnp.bfloat16))


def transposed(first_op, second_op):
    return lax.dot_general(
        first_op, second_op, (((1,), (1,)), ((), ())), preferred_element_type=jnp.float32
    )


def adam_update(master, moment_old, second_old, gradient):
    moment_one = beta_one * moment_old + (1.0 - beta_one) * gradient
    moment_two = beta_two * second_old + (1.0 - beta_two) * gradient * gradient
    unbiased_one = moment_one / (1.0 - beta_one**adam_steps)
    unbiased_two = moment_two / (1.0 - beta_two**adam_steps)
    updated = master - learn_rate * (
        unbiased_one / (jnp.sqrt(unbiased_two) + adam_eps) + decay_rate * master
    )
    return (updated, moment_one, moment_two)


def factors(gate_pre, up_pre):
    sigmoid = jax.nn.sigmoid(gate_pre)
    return (up_pre * (sigmoid * (1.0 + gate_pre * (1.0 - sigmoid))), gate_pre * sigmoid)


def exchange(blocks):
    return lax.all_to_all(blocks, "dp", split_axis=0, concat_axis=0, tiled=True)


def ring_max(value, axis):
    count = lax.axis_size(axis)
    span = 1
    while span < count:
        pairs = [(source, (source + span) % count) for source in range(count)]
        value = jnp.maximum(value, lax.ppermute(value, axis, pairs))
        span *= 2
    return value


def shards(
    section_inputs,
    cotangent,
    norm_gain,
    quant_gate,
    quant_up,
    scales,
    down_proj,
    master_gate,
    master_up,
    moment_gate,
    moment_up,
    second_gate,
    second_up,
    next_inputs,
):
    gain_row = norm_gain[0]
    scale_pair = scales[0]
    down_local = down_proj[0]
    tok_rows = section_inputs.shape[1]
    hidden_count = quant_gate.shape[2]
    own_rows = quant_gate.shape[1]
    partners = lax.axis_size("dp")
    own_cols = hidden_count // partners
    sections = lax.axis_size("section")
    position = lax.axis_index("section")
    is_last = position == sections - 1
    both_full = lax.all_gather(
        jnp.concatenate([quant_gate[0], quant_up[0]], axis=1), "dp", axis=0, tiled=True
    )
    widened, inverse, normed = normalize(section_inputs[0], gain_row)
    both_pre = jnp.dot(normed, both_full, preferred_element_type=jnp.float32)
    gate_factor, up_factor = factors(
        both_pre[:, :hidden_count] * scale_pair[0], both_pre[:, hidden_count:] * scale_pair[1]
    )
    cubed = inverse * inverse * inverse

    def stage(upstream):
        hidden_grad = transposed(upstream, down_local)
        gate_grad = (hidden_grad * gate_factor).astype(jnp.bfloat16)
        up_grad = (hidden_grad * up_factor).astype(jnp.bfloat16)
        normed_grad = (
            transposed(gate_grad, both_full[:, :hidden_count]) * scale_pair[0]
            + transposed(up_grad, both_full[:, hidden_count:]) * scale_pair[1]
        )
        gained = gain_row * normed_grad
        mean_term = jnp.mean(widened * gained, axis=-1, keepdims=True)
        result = upstream.astype(jnp.float32) + inverse * gained - widened * cubed * mean_term
        return result.astype(jnp.bfloat16)

    unused_one, unused_two, next_normed = normalize(next_inputs[0], gain_row)
    normed_all = lax.all_gather(normed, "dp", axis=0, tiled=True)
    next_all = lax.all_gather(next_normed, "dp", axis=0, tiled=True)
    first_col = lax.axis_index("dp") * own_cols
    gate_cols = lax.dynamic_slice_in_dim(both_full, first_col, own_cols, axis=1)
    up_cols = lax.dynamic_slice_in_dim(both_full, hidden_count + first_col, own_cols, axis=1)
    down_cols = lax.dynamic_slice_in_dim(down_local, first_col, own_cols, axis=0)
    gate_factor_cols, up_factor_cols = factors(
        jnp.dot(normed_all, gate_cols, preferred_element_type=jnp.float32) * scale_pair[0],
        jnp.dot(normed_all, up_cols, preferred_element_type=jnp.float32) * scale_pair[1],
    )

    upstream = cotangent
    for turn in range(sections):
        result = stage(upstream)
        if turn < sections - 1:
            incoming = lax.ppermute(
                result, "section", [(source, source - 1) for source in range(1, sections)]
            )
            upstream = jnp.where(is_last, cotangent, incoming)

    upstream_all = lax.all_gather(upstream, "dp", axis=0, tiled=True)
    hidden_cols = transposed(upstream_all, down_cols)
    grads_cols = jnp.concatenate(
        [
            (hidden_cols * gate_factor_cols).astype(jnp.bfloat16),
            (hidden_cols * up_factor_cols).astype(jnp.bfloat16),
        ],
        axis=1,
    )
    weight_cols = lax.dot_general(
        normed_all, grads_cols, (((0,), (0,)), ((), ())), preferred_element_type=jnp.float32
    ).astype(jnp.bfloat16)
    weight_blocks = exchange(weight_cols.reshape(partners, own_rows, 2 * own_cols))
    gradient = weight_blocks.astype(jnp.float32).reshape(partners, own_rows, 2, own_cols)
    gradient = gradient.transpose(2, 1, 0, 3).reshape(2, own_rows, hidden_count)
    new_gate, mom_gate, sec_gate = adam_update(
        master_gate[0], moment_gate[0], second_gate[0], gradient[0]
    )
    new_up, mom_up, sec_up = adam_update(master_up[0], moment_up[0], second_up[0], gradient[1])
    peaks = jnp.stack([jnp.max(jnp.abs(new_gate)), jnp.max(jnp.abs(new_up))])
    new_scales = ring_max(peaks, "dp") + scale_eps
    stacked = jnp.stack([new_gate, new_up]).astype(jnp.bfloat16)
    stacked = stacked.reshape(2, own_rows, partners, own_cols).transpose(2, 1, 0, 3)
    new_cols = exchange(stacked.reshape(partners, own_rows, 2 * own_cols))
    new_cols = new_cols.reshape(partners * own_rows, 2 * own_cols)
    both_next = lax.dot_general(
        new_cols, next_all, (((0,), (1,)), ((), ())), preferred_element_type=jnp.float32
    )
    hidden_turned = (jax.nn.silu(both_next[:own_cols]) * both_next[own_cols:]).astype(jnp.bfloat16)
    token_blocks = hidden_turned.reshape(own_cols, partners, tok_rows).transpose(1, 0, 2)
    next_hidden = exchange(token_blocks).reshape(hidden_count, tok_rows).T
    return (
        result[None],
        new_gate[None],
        new_up[None],
        mom_gate[None],
        mom_up[None],
        sec_gate[None],
        sec_up[None],
        new_scales[None, :],
        next_hidden[None],
    )


def solution(mesh):
    placed = (
        P("section", "dp", None),
        P("dp", None),
        P("section", None),
        P("section", "dp", None),
        P("section", "dp", None),
        P("section", None),
        P("section", None, None),
        P("section", "dp", None),
        P("section", "dp", None),
        P("section", "dp", None),
        P("section", "dp", None),
        P("section", "dp", None),
        P("section", "dp", None),
        P("section", "dp", None),
    )
    return jax.shard_map(
        shards,
        mesh=mesh,
        in_specs=placed,
        out_specs=(
            P("section", "dp", None),
            P("section", "dp", None),
            P("section", "dp", None),
            P("section", "dp", None),
            P("section", "dp", None),
            P("section", "dp", None),
            P("section", "dp", None),
            P("section", None),
            P("section", "dp", None),
        ),
        check_vma=False,
    )
```

```python
import jax
import jax.numpy as jnp
from jax import lax
from jax.sharding import PartitionSpec as P

beta_one = 0.9
beta_two = 0.95
learn_rate = 0.002
decay_rate = 0.1
adam_steps = 100.0
norm_eps = 1e-06
adam_eps = 1e-08
scale_eps = 1e-06


def normalize(inputs, norm_gain):
    widened = inputs.astype(jnp.float32)
    inverse = lax.rsqrt(jnp.mean(widened * widened, axis=-1, keepdims=True) + norm_eps)
    return (widened, inverse, (widened * inverse * norm_gain).astype(jnp.bfloat16))


def transposed(first_op, second_op):
    return lax.dot_general(
        first_op, second_op, (((1,), (1,)), ((), ())), preferred_element_type=jnp.float32
    )


def adam_update(master, moment_old, second_old, gradient):
    moment_one = beta_one * moment_old + (1.0 - beta_one) * gradient
    moment_two = beta_two * second_old + (1.0 - beta_two) * gradient * gradient
    unbiased_one = moment_one / (1.0 - beta_one**adam_steps)
    unbiased_two = moment_two / (1.0 - beta_two**adam_steps)
    updated = master - learn_rate * (
        unbiased_one / (jnp.sqrt(unbiased_two) + adam_eps) + decay_rate * master
    )
    return (updated, moment_one, moment_two)


def factors(gate_pre, up_pre):
    sigmoid = jax.nn.sigmoid(gate_pre)
    return (up_pre * (sigmoid * (1.0 + gate_pre * (1.0 - sigmoid))), gate_pre * sigmoid)


def exchange(blocks):
    return lax.all_to_all(blocks, "dp", split_axis=0, concat_axis=0, tiled=True)


def swap(value, distance):
    pairs = [(source, source ^ distance) for source in range(lax.axis_size("dp"))]
    return lax.ppermute(value, "dp", pairs)


def spread(first, second):
    across_x = (swap(first, 2), swap(second, 2))
    across_y = (swap(first, 4), swap(second, 4))
    diagonal = (swap(across_y[0], 2), swap(across_x[1], 4))
    even = [(first, second), across_x, across_y, diagonal]
    odd = [(swap(pair[0], 1), swap(pair[1], 1)) for pair in even]
    return [even[0], odd[0], even[1], odd[1], even[2], odd[2], even[3], odd[3]]


def gather_weights(gate, up):
    partners = lax.axis_size("dp")
    if partners != 8:
        return tuple(lax.all_gather(part, "dp", axis=0, tiled=True) for part in (gate, up))
    rows, columns = gate.shape
    own = lax.axis_index("dp")
    gate_full = jnp.zeros((partners * rows, columns), gate.dtype)
    up_full = jnp.zeros((partners * rows, columns), up.dtype)
    for distance, pair in enumerate(spread(gate, up)):
        start = (own ^ distance) * rows
        gate_full = lax.dynamic_update_slice_in_dim(gate_full, pair[0], start, axis=0)
        up_full = lax.dynamic_update_slice_in_dim(up_full, pair[1], start, axis=0)
    return (gate_full, up_full)


def gather_tokens(value):
    if lax.axis_size("dp") != 8:
        return lax.all_gather(value, "dp", axis=0, tiled=True)
    half = value.shape[0] // 2
    blocks = spread(value[:half], value[half:])
    return jnp.concatenate([part for pair in blocks for part in pair], axis=0)


def token_order(value):
    partners = lax.axis_size("dp")
    if partners != 8:
        return value
    blocks = value.reshape(partners, value.shape[0] // partners, value.shape[1])
    own = lax.axis_index("dp")
    picked = [lax.dynamic_index_in_dim(blocks, own ^ k, 0, keepdims=False) for k in range(partners)]
    return jnp.concatenate(picked, axis=0)


def to_column_blocks(value, partners):
    columns = value.shape[1] // partners
    return jnp.stack([value[:, k * columns : (k + 1) * columns] for k in range(partners)])


def from_column_blocks(blocks):
    return jnp.concatenate([blocks[k] for k in range(blocks.shape[0])], axis=1)


def ring_max(value, axis):
    count = lax.axis_size(axis)
    span = 1
    while span < count:
        pairs = [(source, (source + span) % count) for source in range(count)]
        value = jnp.maximum(value, lax.ppermute(value, axis, pairs))
        span *= 2
    return value


def shards(
    section_inputs,
    cotangent,
    norm_gain,
    quant_gate,
    quant_up,
    scales,
    down_proj,
    master_gate,
    master_up,
    moment_gate,
    moment_up,
    second_gate,
    second_up,
    next_inputs,
):
    gain_row = norm_gain[0]
    scale_pair = scales[0]
    down_local = down_proj[0]
    tok_rows = section_inputs.shape[1]
    feature_count = section_inputs.shape[2]
    hidden_count = quant_gate.shape[2]
    own_rows = quant_gate.shape[1]
    partners = lax.axis_size("dp")
    own_cols = hidden_count // partners
    sections = lax.axis_size("section")
    position = lax.axis_index("section")
    is_last = position == sections - 1
    gate_full, up_full = gather_weights(quant_gate[0], quant_up[0])
    widened, inverse, normed = normalize(section_inputs[0], gain_row)
    unused_one, unused_two, next_normed = normalize(next_inputs[0], gain_row)
    state_blocks = jnp.stack(
        [
            jnp.concatenate(
                [
                    to_column_blocks(gate_part[0].astype(jnp.bfloat16), partners),
                    to_column_blocks(up_part[0].astype(jnp.bfloat16), partners),
                ],
                axis=2,
            )
            for gate_part, up_part in (
                (master_gate, master_up),
                (moment_gate, moment_up),
                (second_gate, second_up),
            )
        ],
        axis=1,
    )
    gate_factor, up_factor = factors(
        jnp.dot(normed, gate_full, preferred_element_type=jnp.float32) * scale_pair[0],
        jnp.dot(normed, up_full, preferred_element_type=jnp.float32) * scale_pair[1],
    )
    cubed = inverse * inverse * inverse

    def stage(upstream):
        hidden_grad = transposed(upstream, down_local)
        gate_grad = (hidden_grad * gate_factor).astype(jnp.bfloat16)
        up_grad = (hidden_grad * up_factor).astype(jnp.bfloat16)
        normed_grad = (
            transposed(gate_grad, gate_full) * scale_pair[0]
            + transposed(up_grad, up_full) * scale_pair[1]
        )
        gained = gain_row * normed_grad
        mean_term = jnp.mean(widened * gained, axis=-1, keepdims=True)
        result = upstream.astype(jnp.float32) + inverse * gained - widened * cubed * mean_term
        return result.astype(jnp.bfloat16)

    both_normed = lax.all_gather(
        jnp.concatenate([normed, next_normed], axis=1), "dp", axis=0, tiled=True
    )
    normed_all = token_order(both_normed[:, :feature_count])
    next_all = both_normed[:, feature_count:]
    first_col = lax.axis_index("dp") * own_cols
    gate_cols = lax.dynamic_slice_in_dim(gate_full, first_col, own_cols, axis=1)
    up_cols = lax.dynamic_slice_in_dim(up_full, first_col, own_cols, axis=1)
    down_cols = lax.dynamic_slice_in_dim(down_local, first_col, own_cols, axis=0)
    gate_factor_cols, up_factor_cols = factors(
        jnp.dot(normed_all, gate_cols, preferred_element_type=jnp.float32) * scale_pair[0],
        jnp.dot(normed_all, up_cols, preferred_element_type=jnp.float32) * scale_pair[1],
    )

    upstream = cotangent
    for turn in range(sections):
        result = stage(upstream)
        if turn == 0:
            result, state_blocks = lax.optimization_barrier((result, state_blocks))
            state_cols = exchange(state_blocks)
        if turn < sections - 1:
            incoming = lax.ppermute(
                result, "section", [(source, source - 1) for source in range(1, sections)]
            )
            upstream = jnp.where(is_last, cotangent, incoming)

    upstream_all = gather_tokens(upstream)
    hidden_cols = transposed(upstream_all, down_cols)
    grads_cols = jnp.concatenate(
        [
            (hidden_cols * gate_factor_cols).astype(jnp.bfloat16),
            (hidden_cols * up_factor_cols).astype(jnp.bfloat16),
        ],
        axis=1,
    )
    weight_cols = lax.dot_general(
        normed_all, grads_cols, (((0,), (0,)), ((), ())), preferred_element_type=jnp.float32
    )
    weight_cols = weight_cols.astype(jnp.bfloat16).reshape(partners, own_rows, 2 * own_cols)
    weight_blocks = exchange(weight_cols)

    new_cols, unused_three, unused_four = adam_update(
        state_cols[:, 0].astype(jnp.float32),
        state_cols[:, 1].astype(jnp.float32),
        state_cols[:, 2].astype(jnp.float32),
        weight_cols.astype(jnp.float32),
    )
    new_cols = new_cols.astype(jnp.bfloat16).reshape(partners * own_rows, 2 * own_cols)
    both_next = lax.dot_general(
        new_cols, next_all, (((0,), (1,)), ((), ())), preferred_element_type=jnp.float32
    )
    hidden_turned = (jax.nn.silu(both_next[:own_cols]) * both_next[own_cols:]).astype(jnp.bfloat16)
    token_blocks = jnp.stack(
        [hidden_turned[:, k * tok_rows : (k + 1) * tok_rows] for k in range(partners)]
    )
    next_hidden = exchange(token_blocks).reshape(hidden_count, tok_rows).T

    new_gate, mom_gate, sec_gate = adam_update(
        master_gate[0],
        moment_gate[0],
        second_gate[0],
        from_column_blocks(weight_blocks[:, :, :own_cols]).astype(jnp.float32),
    )
    new_up, mom_up, sec_up = adam_update(
        master_up[0],
        moment_up[0],
        second_up[0],
        from_column_blocks(weight_blocks[:, :, own_cols:]).astype(jnp.float32),
    )
    peaks = jnp.stack([jnp.max(jnp.abs(new_gate)), jnp.max(jnp.abs(new_up))])
    new_scales = ring_max(peaks, "dp") + scale_eps
    return (
        result[None],
        new_gate[None],
        new_up[None],
        mom_gate[None],
        mom_up[None],
        sec_gate[None],
        sec_up[None],
        new_scales[None, :],
        next_hidden[None],
    )


def solution(mesh):
    placed = (
        P("section", "dp", None),
        P("dp", None),
        P("section", None),
        P("section", "dp", None),
        P("section", "dp", None),
        P("section", None),
        P("section", None, None),
        P("section", "dp", None),
        P("section", "dp", None),
        P("section", "dp", None),
        P("section", "dp", None),
        P("section", "dp", None),
        P("section", "dp", None),
        P("section", "dp", None),
    )
    return jax.shard_map(
        shards,
        mesh=mesh,
        in_specs=placed,
        out_specs=(
            P("section", "dp", None),
            P("section", "dp", None),
            P("section", "dp", None),
            P("section", "dp", None),
            P("section", "dp", None),
            P("section", "dp", None),
            P("section", "dp", None),
            P("section", None),
            P("section", "dp", None),
        ),
        check_vma=False,
    )
```

```python
import functools

import jax
import jax.numpy as jnp
from jax import lax
from jax.experimental import pallas as pl
from jax.experimental.pallas import tpu as pltpu
from jax.sharding import PartitionSpec as P

beta_one = 0.9
beta_two = 0.95
learn_rate = 0.002
decay_rate = 0.1
adam_steps = 100.0
norm_eps = 1e-06
adam_eps = 1e-08
scale_eps = 1e-06
vmem_bytes = 56 * 1024 * 1024
bf16 = jnp.bfloat16
f32 = jnp.float32


def normalize(inputs, norm_gain):
    widened = inputs.astype(jnp.float32)
    inverse = lax.rsqrt(jnp.mean(widened * widened, axis=-1, keepdims=True) + norm_eps)
    return (widened, inverse, (widened * inverse * norm_gain).astype(jnp.bfloat16))


def matmul(first_op, second_op):
    return jnp.dot(first_op, second_op, preferred_element_type=jnp.float32)


def transposed(first_op, second_op):
    return lax.dot_general(
        first_op, second_op, (((1,), (1,)), ((), ())), preferred_element_type=jnp.float32
    )


def adam_update(master, moment_old, second_old, gradient):
    moment_one = beta_one * moment_old + (1.0 - beta_one) * gradient
    moment_two = beta_two * second_old + (1.0 - beta_two) * gradient * gradient
    unbiased_one = moment_one / (1.0 - beta_one**adam_steps)
    unbiased_two = moment_two / (1.0 - beta_two**adam_steps)
    updated = master - learn_rate * (
        unbiased_one / (jnp.sqrt(unbiased_two) + adam_eps) + decay_rate * master
    )
    return (updated, moment_one, moment_two)


def factors(gate_pre, up_pre):
    sigmoid = jax.nn.sigmoid(gate_pre)
    return (up_pre * (sigmoid * (1.0 + gate_pre * (1.0 - sigmoid))), gate_pre * sigmoid)


def exchange(blocks):
    return lax.all_to_all(blocks, "dp", split_axis=0, concat_axis=0, tiled=True)


def swap(value, distance):
    pairs = [(source, source ^ distance) for source in range(lax.axis_size("dp"))]
    return lax.ppermute(value, "dp", pairs)


def spread(first, second):
    across_x = (swap(first, 2), swap(second, 2))
    across_y = (swap(first, 4), swap(second, 4))
    diagonal = (swap(across_y[0], 2), swap(across_x[1], 4))
    even = [(first, second), across_x, across_y, diagonal]
    odd = [(swap(pair[0], 1), swap(pair[1], 1)) for pair in even]
    return [even[0], odd[0], even[1], odd[1], even[2], odd[2], even[3], odd[3]]


def ring_max(value, axis):
    count = lax.axis_size(axis)
    span = 1
    while span < count:
        pairs = [(source, (source + span) % count) for source in range(count)]
        value = jnp.maximum(value, lax.ppermute(value, axis, pairs))
        span *= 2
    return value


def column_chunks(total, width=512):
    return [(start, min(width, total - start)) for start in range(0, total, width)]


def finish_stage(upstream, normed_grad, widened, gain_row):
    inverse = lax.rsqrt(jnp.mean(widened * widened, axis=-1, keepdims=True) + norm_eps)
    gained = gain_row * normed_grad
    mean_term = jnp.mean(widened * gained, axis=-1, keepdims=True)
    cubed = inverse * inverse * inverse
    return (upstream.astype(f32) + inverse * gained - widened * cubed * mean_term).astype(bf16)


def first_kernel(
    own_ref, scale_ref, upstream_ref, inputs_ref, normed_ref, gain_ref, down_hbm, *refs, partners
):
    shards_in = refs[: 2 * partners]
    result_ref, gate_factor_ref, up_factor_ref, gate_hbm, up_hbm = refs[
        2 * partners : 2 * partners + 5
    ]
    gate_full, up_full, down, in_sems, down_sems, out_sems = refs[2 * partners + 5 :]
    rows = shards_in[0].shape[0]
    own = own_ref[0]
    chunks = column_chunks(gate_full.shape[1])
    loads = []
    for index in range(2 * partners):
        place = pl.ds(pl.multiple_of((own ^ (index // 2)) * rows, 16), rows)
        full = gate_full if index % 2 == 0 else up_full
        copy = pltpu.make_async_copy(shards_in[index], full.at[place, :], in_sems.at[index])
        copy.start()
        loads.append(copy)
    downs = []
    for index, (start, width) in enumerate(chunks):
        part = pl.ds(start, width)
        copy = pltpu.make_async_copy(down_hbm.at[part, :], down.at[part, :], down_sems.at[index])
        copy.start()
        downs.append(copy)
    for copy in loads:
        copy.wait()
    stores = [
        pltpu.make_async_copy(gate_full, gate_hbm, out_sems.at[0]),
        pltpu.make_async_copy(up_full, up_hbm, out_sems.at[1]),
    ]
    for copy in stores:
        copy.start()
    upstream = upstream_ref[...]
    normed = normed_ref[...]
    normed_grad = jnp.zeros(upstream.shape, f32)
    for index, (start, width) in enumerate(chunks):
        part = slice(start, start + width)
        gate_part, up_part = gate_full[:, part], up_full[:, part]
        gate_factor, up_factor = factors(
            matmul(normed, gate_part) * scale_ref[0], matmul(normed, up_part) * scale_ref[1]
        )
        gate_factor = (gate_factor * scale_ref[0]).astype(bf16)
        up_factor = (up_factor * scale_ref[1]).astype(bf16)
        gate_factor_ref[:, part] = gate_factor
        up_factor_ref[:, part] = up_factor
        downs[index].wait()
        hidden_grad = transposed(upstream, down[part, :])
        normed_grad += transposed((hidden_grad * gate_factor).astype(bf16), gate_part)
        normed_grad += transposed((hidden_grad * up_factor).astype(bf16), up_part)
    result_ref[...] = finish_stage(
        upstream, normed_grad, inputs_ref[...].astype(f32), gain_ref[...]
    )
    for copy in stores:
        copy.wait()


def stage_kernel(
    upstream_ref,
    inputs_ref,
    gain_ref,
    down_hbm,
    gate_hbm,
    up_hbm,
    gate_factor_hbm,
    up_factor_hbm,
    result_ref,
    down,
    gate_full,
    up_full,
    gate_factor,
    up_factor,
    sems,
):
    chunks = column_chunks(gate_full.shape[1])
    copies = []
    for index, (start, width) in enumerate(chunks):
        part = pl.ds(start, width)
        batch = [
            pltpu.make_async_copy(down_hbm.at[part, :], down.at[part, :], sems.at[0, index]),
            pltpu.make_async_copy(
                gate_factor_hbm.at[:, part], gate_factor.at[:, part], sems.at[1, index]
            ),
            pltpu.make_async_copy(
                up_factor_hbm.at[:, part], up_factor.at[:, part], sems.at[2, index]
            ),
            pltpu.make_async_copy(gate_hbm.at[:, part], gate_full.at[:, part], sems.at[3, index]),
            pltpu.make_async_copy(up_hbm.at[:, part], up_full.at[:, part], sems.at[4, index]),
        ]
        for copy in batch:
            copy.start()
        copies.append(batch)
    upstream = upstream_ref[...]
    normed_grad = jnp.zeros(upstream.shape, f32)
    for index, (start, width) in enumerate(chunks):
        part = slice(start, start + width)
        for copy in copies[index]:
            copy.wait()
        hidden_grad = transposed(upstream, down[part, :])
        gate_grad = (hidden_grad * gate_factor[:, part]).astype(bf16)
        up_grad = (hidden_grad * up_factor[:, part]).astype(bf16)
        normed_grad += transposed(gate_grad, gate_full[:, part])
        normed_grad += transposed(up_grad, up_full[:, part])
    result_ref[...] = finish_stage(
        upstream, normed_grad, inputs_ref[...].astype(f32), gain_ref[...]
    )


def blocks_kernel(*refs):
    sources, targets = refs[:6], refs[6:]
    for kind in range(3):
        gate = sources[2 * kind][...].astype(bf16)
        up = sources[2 * kind + 1][...].astype(bf16)
        partners, unused, both = targets[kind].shape
        columns = both // 2
        for k in range(partners):
            part = slice(k * columns, (k + 1) * columns)
            targets[kind][k, :, :columns] = gate[:, part]
            targets[kind][k, :, columns:] = up[:, part]


def factors_kernel(own_ref, scale_ref, normed_ref, gate_ref, up_ref, out_gate, out_up, gate, up):
    columns = gate.shape[1]
    partners = gate_ref.shape[1] // columns

    @pl.when(pl.program_id(0) == 0)
    def pick():
        for k in range(partners):
            @pl.when(own_ref[0] == k)
            def pick_one():
                part = slice(k * columns, (k + 1) * columns)
                gate[...] = gate_ref[:, part]
                up[...] = up_ref[:, part]

    normed = normed_ref[0].T
    gate_factor, up_factor = factors(
        matmul(normed, gate[...]) * scale_ref[0], matmul(normed, up[...]) * scale_ref[1]
    )
    out_gate[...] = gate_factor.astype(bf16)
    out_up[...] = up_factor.astype(bf16)


def weight_kernel(
    own_ref, down_ref, normed_hbm, gate_factor_hbm, up_factor_hbm, *refs, partners
):
    pieces = refs[: 2 * partners]
    out_ref = refs[2 * partners]
    upstream, normed, gate_factor, up_factor, total, sems = refs[2 * partners + 1 :]
    own = own_ref[0]
    half = pieces[0].shape[0]
    rows = 2 * half
    columns = gate_factor.shape[1]
    copies = []
    for k in range(partners):
        block = pl.ds(k * rows, rows)
        batch = [
            pltpu.make_async_copy(
                pieces[2 * k + side],
                upstream.at[pl.ds(k * rows + side * half, half), :],
                sems.at[side, k],
            )
            for side in range(2)
        ]
        batch += [
            pltpu.make_async_copy(
                gate_factor_hbm.at[block, :], gate_factor.at[block, :], sems.at[2, k]
            ),
            pltpu.make_async_copy(up_factor_hbm.at[block, :], up_factor.at[block, :], sems.at[3, k]),
            pltpu.make_async_copy(normed_hbm.at[own ^ k], normed.at[k], sems.at[4, k]),
        ]
        for copy in batch:
            copy.start()
        copies.append(batch)
    for k in range(partners):
        block = slice(k * rows, (k + 1) * rows)
        for copy in copies[k]:
            copy.wait()
        hidden_grad = transposed(upstream[block, :], down_ref[...])
        grads = jnp.concatenate(
            [hidden_grad * gate_factor[block, :], hidden_grad * up_factor[block, :]], axis=1
        ).astype(bf16)
        product = matmul(normed[k], grads)
        if k == 0:
            total[...] = product
        else:
            total[...] += product
    out_ref[...] = total[...].astype(bf16)


def next_kernel(gradient_ref, master_ref, moment_ref, second_ref, next_ref, out_ref, peak_ref, turned):
    columns = turned.shape[0] // 2

    @pl.when(pl.program_id(0) == 0)
    def update():
        updated, unused_one, unused_two = adam_update(
            master_ref[...].astype(f32),
            moment_ref[...].astype(f32),
            second_ref[...].astype(f32),
            gradient_ref[...].astype(f32),
        )
        flipped = updated.T
        turned[...] = flipped.astype(bf16)
        sizes = jnp.abs(flipped)
        peak_ref[0:1, :] = jnp.full((1, 128), jnp.max(sizes[:columns]), f32)
        peak_ref[1:2, :] = jnp.full((1, 128), jnp.max(sizes[columns:]), f32)

    both = matmul(turned[...], next_ref[0])
    gate, up = both[:columns], both[columns:]
    out_ref[0] = (gate * jax.nn.sigmoid(gate) * up).astype(bf16)


def rows_kernel(
    blocks_ref, *refs
):
    sources, targets, gradient = refs[:6], refs[6:12], refs[12]
    partners, unused, both = blocks_ref.shape
    columns = both // 2
    for side in range(2):
        for k in range(partners):
            gradient[:, k * columns : (k + 1) * columns] = blocks_ref[k].astype(f32)[
                :, side * columns : (side + 1) * columns
            ]
        results = adam_update(
            sources[side][...], sources[2 + side][...], sources[4 + side][...], gradient[...]
        )
        for kind in range(3):
            targets[2 * kind + side][...] = results[kind]


def any_space():
    return pl.BlockSpec(memory_space=pl.ANY)


def smem_space():
    return pl.BlockSpec(memory_space=pltpu.SMEM)


def params():
    return pltpu.CompilerParams(vmem_limit_bytes=vmem_bytes)


def whole(shape):
    return pl.BlockSpec(shape, lambda *unused: (0,) * len(shape))


def run_first(own, scale_pair, upstream, inputs, normed, gain, down, pieces):
    tokens, features = upstream.shape
    hidden = down.shape[0]
    partners = len(pieces)
    chunk_count = len(column_chunks(hidden))
    flat = [part for pair in pieces for part in pair]
    vmem = pl.BlockSpec(memory_space=pltpu.VMEM)
    return pl.pallas_call(
        functools.partial(first_kernel, partners=partners),
        out_shape=(
            jax.ShapeDtypeStruct((tokens, features), bf16),
            jax.ShapeDtypeStruct((tokens, hidden), bf16),
            jax.ShapeDtypeStruct((tokens, hidden), bf16),
            jax.ShapeDtypeStruct((features, hidden), bf16),
            jax.ShapeDtypeStruct((features, hidden), bf16),
        ),
        in_specs=[smem_space(), smem_space()] + [vmem] * 4 + [any_space()] * (1 + len(flat)),
        out_specs=(vmem, vmem, vmem, any_space(), any_space()),
        scratch_shapes=[
            pltpu.VMEM((features, hidden), bf16),
            pltpu.VMEM((features, hidden), bf16),
            pltpu.VMEM((hidden, features), bf16),
            pltpu.SemaphoreType.DMA((len(flat),)),
            pltpu.SemaphoreType.DMA((chunk_count,)),
            pltpu.SemaphoreType.DMA((2,)),
        ],
        compiler_params=params(),
        name="first_stage",
    )(own, scale_pair, upstream, inputs, normed, gain, down, *flat)


def run_stage(upstream, inputs, gain, down, gate_full, up_full, gate_factor, up_factor):
    tokens, features = upstream.shape
    hidden = down.shape[0]
    vmem = pl.BlockSpec(memory_space=pltpu.VMEM)
    return pl.pallas_call(
        stage_kernel,
        out_shape=jax.ShapeDtypeStruct((tokens, features), bf16),
        in_specs=[vmem] * 3 + [any_space()] * 5,
        out_specs=vmem,
        scratch_shapes=[
            pltpu.VMEM((hidden, features), bf16),
            pltpu.VMEM((features, hidden), bf16),
            pltpu.VMEM((features, hidden), bf16),
            pltpu.VMEM((tokens, hidden), bf16),
            pltpu.VMEM((tokens, hidden), bf16),
            pltpu.SemaphoreType.DMA((5, len(column_chunks(hidden)))),
        ],
        compiler_params=params(),
        name="stage",
    )(upstream, inputs, gain, down, gate_full, up_full, gate_factor, up_factor)


def run_blocks(sources, partners):
    rows, hidden = sources[0].shape
    step = 16
    both = 2 * (hidden // partners)
    return pl.pallas_call(
        blocks_kernel,
        grid=(rows // step,),
        out_shape=tuple(jax.ShapeDtypeStruct((partners, rows, both), bf16) for _ in range(3)),
        in_specs=[pl.BlockSpec((step, hidden), lambda i: (i, 0))] * 6,
        out_specs=tuple(pl.BlockSpec((partners, step, both), lambda i: (0, i, 0)) for _ in range(3)),
        compiler_params=params(),
        name="state_blocks",
    )(*sources)


def run_factors(own, scale_pair, normed_all, gate_full, up_full):
    partners, features, tokens = normed_all.shape
    hidden = gate_full.shape[1]
    columns = hidden // partners
    shape = jax.ShapeDtypeStruct((partners * tokens, columns), bf16)
    return pl.pallas_call(
        factors_kernel,
        grid_spec=pltpu.PrefetchScalarGridSpec(
            num_scalar_prefetch=1,
            grid=(partners,),
            in_specs=[
                smem_space(),
                pl.BlockSpec((1, features, tokens), lambda k, own: (own[0] ^ k, 0, 0)),
                whole((features, hidden)),
                whole((features, hidden)),
            ],
            out_specs=(
                pl.BlockSpec((tokens, columns), lambda k, own: (k, 0)),
                pl.BlockSpec((tokens, columns), lambda k, own: (k, 0)),
            ),
            scratch_shapes=[pltpu.VMEM((features, columns), bf16)] * 2,
        ),
        out_shape=(shape, shape),
        compiler_params=params(),
        name="column_factors",
    )(own, scale_pair, normed_all, gate_full, up_full)


def run_weights(own, down_cols, normed_all, gate_factor, up_factor, pieces):
    partners, features, tokens = normed_all.shape
    columns = down_cols.shape[0]
    flat = [part for pair in pieces for part in pair]
    vmem = pl.BlockSpec(memory_space=pltpu.VMEM)
    return pl.pallas_call(
        functools.partial(weight_kernel, partners=partners),
        out_shape=jax.ShapeDtypeStruct((features, 2 * columns), bf16),
        in_specs=[smem_space(), vmem] + [any_space()] * (3 + len(flat)),
        out_specs=vmem,
        scratch_shapes=[
            pltpu.VMEM((partners * tokens, features), bf16),
            pltpu.VMEM((partners, features, tokens), bf16),
            pltpu.VMEM((partners * tokens, columns), bf16),
            pltpu.VMEM((partners * tokens, columns), bf16),
            pltpu.VMEM((features, 2 * columns), f32),
            pltpu.SemaphoreType.DMA((5, partners)),
        ],
        compiler_params=params(),
        name="column_gradients",
    )(own, down_cols, normed_all, gate_factor, up_factor, *flat)


def run_next(gradient, state, next_all):
    partners, features, tokens = next_all.shape
    both = gradient.shape[1]
    return pl.pallas_call(
        next_kernel,
        grid=(partners,),
        out_shape=(
            jax.ShapeDtypeStruct((partners, both // 2, tokens), bf16),
            jax.ShapeDtypeStruct((8, 128), f32),
        ),
        in_specs=[whole((features, both))] * 4
        + [pl.BlockSpec((1, features, tokens), lambda k: (k, 0, 0))],
        out_specs=(
            pl.BlockSpec((1, both // 2, tokens), lambda k: (k, 0, 0)),
            whole((8, 128)),
        ),
        scratch_shapes=[pltpu.VMEM((both, features), bf16)],
        compiler_params=params(),
        name="next_columns",
    )(gradient, *state, next_all)


def run_rows(blocks, sources):
    partners, rows, both = blocks.shape
    hidden = sources[0].shape[1]
    step = 16
    row_spec = pl.BlockSpec((step, hidden), lambda i: (i, 0))
    return pl.pallas_call(
        rows_kernel,
        grid=(rows // step,),
        out_shape=tuple(jax.ShapeDtypeStruct((rows, hidden), f32) for _ in range(6)),
        in_specs=[pl.BlockSpec((partners, step, both), lambda i: (0, i, 0))] + [row_spec] * 6,
        out_specs=(row_spec,) * 6,
        scratch_shapes=[pltpu.VMEM((step, hidden), f32)],
        compiler_params=params(),
        name="row_update",
    )(blocks, *sources)


def down_shift(value, sections):
    return lax.ppermute(value, "section", [(source, source - 1) for source in range(1, sections)])


def columns_plan(
    section_inputs,
    cotangent,
    norm_gain,
    quant_gate,
    quant_up,
    scales,
    down_proj,
    master_gate,
    master_up,
    moment_gate,
    moment_up,
    second_gate,
    second_up,
    next_inputs,
):
    gain_row = norm_gain[0]
    scale_pair = scales[0]
    down_local = down_proj[0]
    inputs = section_inputs[0]
    tok_rows, feature_count = inputs.shape
    own_rows, hidden_count = quant_gate.shape[1:]
    partners = lax.axis_size("dp")
    own_cols = hidden_count // partners
    sections = lax.axis_size("section")
    is_last = lax.axis_index("section") == sections - 1
    own_index = lax.axis_index("dp")
    own = own_index.astype(jnp.int32).reshape(1)
    barrier = lax.optimization_barrier

    weight_pieces = spread(quant_gate[0], quant_up[0])
    normed = normalize(inputs, gain_row)[2]
    normed_turned = normed.T
    next_turned = normalize(next_inputs[0], gain_row)[2].T
    sources = [
        master_gate[0],
        master_up[0],
        moment_gate[0],
        moment_up[0],
        second_gate[0],
        second_up[0],
    ]
    state_blocks = list(run_blocks(sources, partners))
    normed, normed_turned, next_turned, *state_blocks = barrier(
        (normed, normed_turned, next_turned, *state_blocks)
    )

    last_piece, normed_turned = barrier((weight_pieces[-1][1], normed_turned))
    weight_pieces[-1] = (weight_pieces[-1][0], last_piece)
    normed_all = lax.all_gather(normed_turned[None], "dp", axis=0, tiled=True)
    result, gate_factor, up_factor, gate_full, up_full = run_first(
        own, scale_pair, cotangent, inputs, normed, gain_row[None], down_local, weight_pieces
    )
    state_cols = []
    waiting = []
    next_all = None
    for turn in range(sections - 1):
        incoming = down_shift(result, sections)
        if turn < 3:
            result, block = barrier((result, state_blocks[turn]))
            state_cols.append(exchange(block))
        if turn == 1:
            result, next_turned = barrier((result, next_turned))
            next_all = lax.all_gather(next_turned[None], "dp", axis=0, tiled=True)
        upstream = jnp.where(is_last, cotangent, incoming)
        if turn == sections - 2:
            break
        if turn >= 1:
            upstream, state_cols[turn - 1] = barrier((upstream, state_cols[turn - 1]))
        result = run_stage(
            upstream, inputs, gain_row[None], down_local, gate_full, up_full, gate_factor, up_factor
        )
    gate_factor_cols, up_factor_cols = run_factors(own, scale_pair, normed_all, gate_full, up_full)
    down_cols = lax.dynamic_slice_in_dim(down_local, own_index * own_cols, own_cols, axis=0)
    upstream, gate_factor_cols, up_factor_cols, down_cols = barrier(
        (upstream, gate_factor_cols, up_factor_cols, down_cols)
    )
    half = tok_rows // 2
    pieces = spread(upstream[:half], upstream[half:])
    result = run_stage(
        upstream, inputs, gain_row[None], down_local, gate_full, up_full, gate_factor, up_factor
    )
    gradient = run_weights(own, down_cols, normed_all, gate_factor_cols, up_factor_cols, pieces)
    row_blocks = exchange(gradient.reshape(partners, own_rows, 2 * own_cols))
    state = [part.reshape(feature_count, 2 * own_cols) for part in state_cols]
    token_blocks, peaks = run_next(gradient, state, next_all)
    next_hidden = exchange(token_blocks).reshape(hidden_count, tok_rows).T
    new_scales = ring_max(peaks, "dp")[:2, 0] + scale_eps
    updated = run_rows(row_blocks, sources)
    return (
        result[None],
        *(part[None] for part in updated),
        new_scales[None, :],
        next_hidden[None],
    )


def plain_plan(
    section_inputs,
    cotangent,
    norm_gain,
    quant_gate,
    quant_up,
    scales,
    down_proj,
    master_gate,
    master_up,
    moment_gate,
    moment_up,
    second_gate,
    second_up,
    next_inputs,
):
    gain_row = norm_gain[0]
    scale_pair = scales[0]
    down_local = down_proj[0]
    hidden_count = quant_gate.shape[2]
    sections = lax.axis_size("section")
    position = lax.axis_index("section")
    is_last = position == sections - 1
    both_full = lax.all_gather(
        jnp.concatenate([quant_gate[0], quant_up[0]], axis=1), "dp", axis=0, tiled=True
    )
    widened, inverse, normed = normalize(section_inputs[0], gain_row)
    both_pre = jnp.dot(normed, both_full, preferred_element_type=jnp.float32)
    gate_pre = both_pre[:, :hidden_count] * scale_pair[0]
    up_pre = both_pre[:, hidden_count:] * scale_pair[1]
    sigmoid = jax.nn.sigmoid(gate_pre)
    up_factor = gate_pre * sigmoid
    gate_factor = up_pre * (sigmoid * (1.0 + gate_pre * (1.0 - sigmoid)))
    cubed = inverse * inverse * inverse

    def stage(upstream):
        hidden_grad = transposed(upstream, down_local)
        gate_grad = (hidden_grad * gate_factor).astype(jnp.bfloat16)
        up_grad = (hidden_grad * up_factor).astype(jnp.bfloat16)
        normed_grad = (
            transposed(gate_grad, both_full[:, :hidden_count]) * scale_pair[0]
            + transposed(up_grad, both_full[:, hidden_count:]) * scale_pair[1]
        )
        gained = gain_row * normed_grad
        mean_term = jnp.mean(widened * gained, axis=-1, keepdims=True)
        result = upstream.astype(jnp.float32) + inverse * gained - widened * cubed * mean_term
        return (result.astype(jnp.bfloat16), gate_grad, up_grad)

    upstream = cotangent
    for turn in range(sections):
        result, gate_grad, up_grad = stage(upstream)
        if turn < sections - 1:
            incoming = lax.ppermute(
                result, "section", [(source, source - 1) for source in range(1, sections)]
            )
            upstream = jnp.where(is_last, cotangent, incoming)

    grads_all = jnp.concatenate([gate_grad, up_grad], axis=1)
    summed = lax.psum_scatter(
        lax.dot_general(
            normed, grads_all, (((0,), (0,)), ((), ())), preferred_element_type=jnp.float32
        ).astype(jnp.bfloat16),
        "dp",
        scatter_dimension=0,
        tiled=True,
    ).astype(jnp.float32)
    new_gate, mom_gate, sec_gate = adam_update(
        master_gate[0], moment_gate[0], second_gate[0], summed[:, :hidden_count]
    )
    new_up, mom_up, sec_up = adam_update(
        master_up[0], moment_up[0], second_up[0], summed[:, hidden_count:]
    )
    peaks = jnp.stack([jnp.max(jnp.abs(new_gate)), jnp.max(jnp.abs(new_up))])
    new_scales = ring_max(peaks, "dp") + scale_eps
    unused_one, unused_two, next_normed = normalize(next_inputs[0], gain_row)
    stacked = jnp.concatenate([new_gate, new_up], axis=1).astype(jnp.bfloat16)
    both_next = jnp.dot(
        next_normed,
        lax.all_gather(stacked, "dp", axis=0, tiled=True),
        preferred_element_type=jnp.float32,
    )
    next_hidden = (
        jax.nn.silu(both_next[:, :hidden_count]) * both_next[:, hidden_count:]
    ).astype(jnp.bfloat16)
    return (
        result[None],
        new_gate[None],
        new_up[None],
        mom_gate[None],
        mom_up[None],
        sec_gate[None],
        sec_up[None],
        new_scales[None, :],
        next_hidden[None],
    )


def solution(mesh):
    placed = (
        P("section", "dp", None),
        P("dp", None),
        P("section", None),
        P("section", "dp", None),
        P("section", "dp", None),
        P("section", None),
        P("section", None, None),
        P("section", "dp", None),
        P("section", "dp", None),
        P("section", "dp", None),
        P("section", "dp", None),
        P("section", "dp", None),
        P("section", "dp", None),
        P("section", "dp", None),
    )
    return jax.shard_map(
        columns_plan if mesh.shape["dp"] == 8 and mesh.shape["section"] >= 4 else plain_plan,
        mesh=mesh,
        in_specs=placed,
        out_specs=(
            P("section", "dp", None),
            P("section", "dp", None),
            P("section", "dp", None),
            P("section", "dp", None),
            P("section", "dp", None),
            P("section", "dp", None),
            P("section", "dp", None),
            P("section", None),
            P("section", "dp", None),
        ),
        check_vma=False,
    )
```

```python
import functools

import jax
import jax.numpy as jnp
from jax import lax
from jax.experimental import pallas as pl
from jax.experimental.pallas import tpu as pltpu
from jax.sharding import PartitionSpec as P

beta_one = 0.9
beta_two = 0.95
learn_rate = 0.002
decay_rate = 0.1
adam_steps = 100.0
norm_eps = 1e-06
adam_eps = 1e-08
scale_eps = 1e-06
vmem_bytes = 56 * 1024 * 1024
bf16 = jnp.bfloat16
f32 = jnp.float32


def normalize(inputs, norm_gain):
    widened = inputs.astype(jnp.float32)
    inverse = lax.rsqrt(jnp.mean(widened * widened, axis=-1, keepdims=True) + norm_eps)
    return (widened, inverse, (widened * inverse * norm_gain).astype(jnp.bfloat16))


def matmul(first_op, second_op):
    return jnp.dot(first_op, second_op, preferred_element_type=jnp.float32)


def transposed(first_op, second_op):
    return lax.dot_general(
        first_op, second_op, (((1,), (1,)), ((), ())), preferred_element_type=jnp.float32
    )


def adam_update(master, moment_old, second_old, gradient):
    moment_one = beta_one * moment_old + (1.0 - beta_one) * gradient
    moment_two = beta_two * second_old + (1.0 - beta_two) * gradient * gradient
    unbiased_one = moment_one / (1.0 - beta_one**adam_steps)
    unbiased_two = moment_two / (1.0 - beta_two**adam_steps)
    updated = master - learn_rate * (
        unbiased_one / (jnp.sqrt(unbiased_two) + adam_eps) + decay_rate * master
    )
    return (updated, moment_one, moment_two)


def factors(gate_pre, up_pre):
    sigmoid = jax.nn.sigmoid(gate_pre)
    return (up_pre * (sigmoid * (1.0 + gate_pre * (1.0 - sigmoid))), gate_pre * sigmoid)


def exchange(blocks):
    return lax.all_to_all(blocks, "dp", split_axis=0, concat_axis=0, tiled=True)


def swap(value, distance):
    pairs = [(source, source ^ distance) for source in range(lax.axis_size("dp"))]
    return lax.ppermute(value, "dp", pairs)


def swap_some(value, distance, core):
    pairs = [(k, k ^ distance) for k in range(lax.axis_size("dp")) if k % 2 == core]
    return lax.ppermute(value, "dp", pairs)


def spread_weights(gate, up):
    near = [swap(part, distance) for distance in (2, 4, 1) for part in (gate, up)]
    gate_x, up_x, gate_y, up_y, gate_c, up_c = lax.optimization_barrier(near)
    diagonal = [swap(gate_y, 2), swap(up_x, 4)]
    beside = [swap(part, 1) for part in (gate_x, up_x, gate_y, up_y)]
    gate_d, up_d, *beside = lax.optimization_barrier(diagonal + beside)
    return [
        (gate, up),
        (gate_c, up_c),
        (gate_x, up_x),
        (beside[0], beside[1]),
        (gate_y, up_y),
        (beside[2], beside[3]),
        (gate_d, up_d),
        (swap(gate_d, 1), swap(up_d, 1)),
    ]


def ring_max(value, axis):
    count = lax.axis_size(axis)
    span = 1
    while span < count:
        pairs = [(source, (source + span) % count) for source in range(count)]
        value = jnp.maximum(value, lax.ppermute(value, axis, pairs))
        span *= 2
    return value


def column_chunks(total, width=512):
    return [(start, min(width, total - start)) for start in range(0, total, width)]


def finish_stage(upstream, normed_grad, widened, gain_column):
    inverse = lax.rsqrt(jnp.mean(widened * widened, axis=0, keepdims=True) + norm_eps)
    gained = gain_column * normed_grad
    mean_term = jnp.mean(widened * gained, axis=0, keepdims=True)
    cubed = inverse * inverse * inverse
    return (upstream.astype(f32) + inverse * gained - widened * cubed * mean_term).astype(bf16)


def prep_kernel(
    inputs_ref, next_ref, cotangent_ref, gain_ref, normed_ref, turned_ref, next_out, inputs_out, cot_out
):
    gain_row = gain_ref[...]
    normed = normalize(inputs_ref[...], gain_row)[2]
    normed_ref[...] = normed
    turned_ref[...] = normed.T
    next_out[...] = normalize(next_ref[...], gain_row)[2].T
    inputs_out[...] = inputs_ref[...].T
    cot_out[...] = cotangent_ref[...].T


def first_kernel(
    own_ref, scale_ref, upstream_ref, inputs_ref, normed_ref, gain_ref, down_hbm, *refs, partners
):
    shards_in = refs[: 2 * partners]
    result_ref, gate_factor_ref, up_factor_ref, gate_hbm, up_hbm = refs[
        2 * partners : 2 * partners + 5
    ]
    gate_full, up_full, down, in_sems, down_sems, out_sems = refs[2 * partners + 5 :]
    rows = shards_in[0].shape[0]
    own = own_ref[0]
    chunks = column_chunks(gate_full.shape[1])
    loads = []
    for index in range(2 * partners):
        place = pl.ds(pl.multiple_of((own ^ (index // 2)) * rows, 16), rows)
        full = gate_full if index % 2 == 0 else up_full
        copy = pltpu.make_async_copy(shards_in[index], full.at[place, :], in_sems.at[index])
        copy.start()
        loads.append(copy)
    downs = []
    for index, (start, width) in enumerate(chunks):
        part = pl.ds(start, width)
        copy = pltpu.make_async_copy(down_hbm.at[part, :], down.at[part, :], down_sems.at[index])
        copy.start()
        downs.append(copy)
    for copy in loads:
        copy.wait()
    stores = [
        pltpu.make_async_copy(gate_full, gate_hbm, out_sems.at[0]),
        pltpu.make_async_copy(up_full, up_hbm, out_sems.at[1]),
    ]
    for copy in stores:
        copy.start()
    upstream = upstream_ref[...]
    normed = normed_ref[...]
    normed_grad = jnp.zeros(upstream.shape, f32)
    for index, (start, width) in enumerate(chunks):
        part = slice(start, start + width)
        gate_part, up_part = gate_full[:, part], up_full[:, part]
        gate_factor, up_factor = factors(
            matmul(normed, gate_part) * scale_ref[0], matmul(normed, up_part) * scale_ref[1]
        )
        gate_factor = (gate_factor * scale_ref[0]).astype(bf16).T
        up_factor = (up_factor * scale_ref[1]).astype(bf16).T
        gate_factor_ref[part, :] = gate_factor
        up_factor_ref[part, :] = up_factor
        downs[index].wait()
        hidden_grad = matmul(down[part, :], upstream)
        normed_grad += matmul(gate_part, (hidden_grad * gate_factor).astype(bf16))
        normed_grad += matmul(up_part, (hidden_grad * up_factor).astype(bf16))
    result_ref[...] = finish_stage(
        upstream, normed_grad, inputs_ref[...].astype(f32), gain_ref[...]
    )
    for copy in stores:
        copy.wait()


def stage_kernel(
    upstream_ref,
    inputs_ref,
    gain_ref,
    down_hbm,
    gate_hbm,
    up_hbm,
    gate_factor_hbm,
    up_factor_hbm,
    result_ref,
    down,
    gate_full,
    up_full,
    gate_factor,
    up_factor,
    sems,
):
    chunks = column_chunks(gate_full.shape[1])
    copies = []
    for index, (start, width) in enumerate(chunks):
        part = pl.ds(start, width)
        by_rows = ((down_hbm, down), (gate_factor_hbm, gate_factor), (up_factor_hbm, up_factor))
        by_columns = ((gate_hbm, gate_full), (up_hbm, up_full))
        batch = [
            pltpu.make_async_copy(source.at[part, :], target.at[part, :], sems.at[place, index])
            for place, (source, target) in enumerate(by_rows)
        ]
        batch += [
            pltpu.make_async_copy(source.at[:, part], target.at[:, part], sems.at[3 + place, index])
            for place, (source, target) in enumerate(by_columns)
        ]
        for copy in batch:
            copy.start()
        copies.append(batch)
    upstream = upstream_ref[...]
    normed_grad = jnp.zeros(upstream.shape, f32)
    for index, (start, width) in enumerate(chunks):
        part = slice(start, start + width)
        for copy in copies[index]:
            copy.wait()
        hidden_grad = matmul(down[part, :], upstream)
        gate_grad = (hidden_grad * gate_factor[part, :]).astype(bf16)
        up_grad = (hidden_grad * up_factor[part, :]).astype(bf16)
        normed_grad += matmul(gate_full[:, part], gate_grad)
        normed_grad += matmul(up_full[:, part], up_grad)
    result_ref[...] = finish_stage(
        upstream, normed_grad, inputs_ref[...].astype(f32), gain_ref[...]
    )


def blocks_kernel(*refs):
    sources, targets = refs[:6], refs[6:]
    for kind in range(3):
        gate = sources[2 * kind][...].astype(bf16)
        up = sources[2 * kind + 1][...].astype(bf16)
        partners, unused, both = targets[kind].shape
        columns = both // 2
        for k in range(partners):
            part = slice(k * columns, (k + 1) * columns)
            targets[kind][k, :, :columns] = gate[:, part]
            targets[kind][k, :, columns:] = up[:, part]


def factors_kernel(
    own_ref, scale_ref, normed_ref, gate_hbm, up_hbm, out_ref, gate, up, turned, sems
):
    columns = turned.shape[0] // 2
    partners = gate_hbm.shape[1] // columns

    @pl.when(pl.program_id(0) == 0)
    def pick():
        for k in range(partners):
            first = k * columns // 128 * 128
            last = -(-(k + 1) * columns // 128) * 128
            inside = slice(k * columns - first, (k + 1) * columns - first)

            @pl.when(own_ref[0] == k)
            def pick_one():
                copies = [
                    pltpu.make_async_copy(
                        source.at[:, first:last], target.at[:, : last - first], sems.at[place]
                    )
                    for place, (source, target) in enumerate(((gate_hbm, gate), (up_hbm, up)))
                ]
                for copy in copies:
                    copy.start()
                for copy in copies:
                    copy.wait()
                turned[:columns] = gate[:, inside].T
                turned[columns:] = up[:, inside].T

    both = matmul(turned[...], normed_ref[0])
    gate_factor, up_factor = factors(both[:columns] * scale_ref[0], both[columns:] * scale_ref[1])
    out_ref[0, :columns] = gate_factor.astype(bf16)
    out_ref[0, columns:] = up_factor.astype(bf16)


def weight_kernel(own_ref, down_ref, normed_hbm, factor_hbm, *refs, distances, has_start):
    count = len(distances)
    pieces = refs[:count]
    start_ref = refs[count] if has_start else None
    out_ref, upstream, normed, factor, sems = refs[count + has_start :]
    own = own_ref[0]
    columns = down_ref.shape[0]
    copies = []
    for place, distance in enumerate(distances):
        batch = [
            pltpu.make_async_copy(pieces[place], upstream.at[place], sems.at[0, place]),
            pltpu.make_async_copy(factor_hbm.at[distance], factor.at[place], sems.at[1, place]),
            pltpu.make_async_copy(normed_hbm.at[own ^ distance], normed.at[place], sems.at[2, place]),
        ]
        for copy in batch:
            copy.start()
        copies.append(batch)
    total = start_ref[...] if has_start else None
    for place in range(count):
        for copy in copies[place]:
            copy.wait()
        hidden_grad = matmul(down_ref[...], upstream[place])
        grads = jnp.concatenate(
            [
                (hidden_grad * factor[place, :columns]).astype(bf16),
                (hidden_grad * factor[place, columns:]).astype(bf16),
            ],
            axis=0,
        )
        product = transposed(normed[place], grads)
        total = product if total is None else total + product
    out_ref[...] = total.astype(out_ref.dtype)


def next_kernel(gradient_ref, master_ref, moment_ref, second_ref, next_ref, out_ref, peak_ref, turned):
    columns = turned.shape[0] // 2

    @pl.when(pl.program_id(0) == 0)
    def update():
        updated, unused_one, unused_two = adam_update(
            master_ref[...].astype(f32),
            moment_ref[...].astype(f32),
            second_ref[...].astype(f32),
            gradient_ref[...].astype(f32),
        )
        flipped = updated.T
        turned[...] = flipped.astype(bf16)
        sizes = jnp.max(jnp.abs(flipped), axis=1, keepdims=True)
        peak_ref[0:1, :] = jnp.full((1, 128), jnp.max(sizes[:columns]), f32)
        peak_ref[1:2, :] = jnp.full((1, 128), jnp.max(sizes[columns:]), f32)

    both = matmul(turned[...], next_ref[0])
    gate, up = both[:columns], both[columns:]
    out_ref[0] = (gate * jax.nn.sigmoid(gate) * up).astype(bf16)


def rows_kernel(
    blocks_ref, *refs
):
    sources, targets, gradient = refs[:6], refs[6:12], refs[12]
    partners, unused, both = blocks_ref.shape
    columns = both // 2
    for side in range(2):
        for k in range(partners):
            gradient[:, k * columns : (k + 1) * columns] = blocks_ref[k].astype(f32)[
                :, side * columns : (side + 1) * columns
            ]
        results = adam_update(
            sources[side][...], sources[2 + side][...], sources[4 + side][...], gradient[...]
        )
        for kind in range(3):
            targets[2 * kind + side][...] = results[kind]


def cost(flops, accessed):
    return pl.CostEstimate(flops=flops, bytes_accessed=accessed, transcendentals=0)


def any_space():
    return pl.BlockSpec(memory_space=pl.ANY)


def smem_space():
    return pl.BlockSpec(memory_space=pltpu.SMEM)


def params():
    return pltpu.CompilerParams(vmem_limit_bytes=vmem_bytes)


def whole(shape):
    return pl.BlockSpec(shape, lambda *unused: (0,) * len(shape))


def run_prep(inputs, next_part, cotangent, gain_row):
    tokens, features = inputs.shape
    turned = jax.ShapeDtypeStruct((features, tokens), bf16)
    return pl.pallas_call(
        prep_kernel,
        out_shape=(jax.ShapeDtypeStruct((tokens, features), bf16),) + (turned,) * 4,
        compiler_params=params(),
        name="prep",
    )(inputs, next_part, cotangent, gain_row)


def run_first(own, scale_pair, upstream, inputs, normed, gain, down, pieces):
    features, tokens = upstream.shape
    hidden = down.shape[0]
    partners = len(pieces)
    chunk_count = len(column_chunks(hidden))
    flat = [part for pair in pieces for part in pair]
    vmem = pl.BlockSpec(memory_space=pltpu.VMEM)
    return pl.pallas_call(
        functools.partial(first_kernel, partners=partners),
        out_shape=(
            jax.ShapeDtypeStruct((features, tokens), bf16),
            jax.ShapeDtypeStruct((hidden, tokens), bf16),
            jax.ShapeDtypeStruct((hidden, tokens), bf16),
            jax.ShapeDtypeStruct((features, hidden), bf16),
            jax.ShapeDtypeStruct((features, hidden), bf16),
        ),
        in_specs=[smem_space(), smem_space()] + [vmem] * 4 + [any_space()] * (1 + len(flat)),
        out_specs=(vmem, vmem, vmem, any_space(), any_space()),
        scratch_shapes=[
            pltpu.VMEM((features, hidden), bf16),
            pltpu.VMEM((features, hidden), bf16),
            pltpu.VMEM((hidden, features), bf16),
            pltpu.SemaphoreType.DMA((len(flat),)),
            pltpu.SemaphoreType.DMA((chunk_count,)),
            pltpu.SemaphoreType.DMA((2,)),
        ],
        compiler_params=params(),
        cost_estimate=cost(9 * tokens * features * hidden * 2 // 2, 26 * features * hidden),
        name="first_stage",
    )(own, scale_pair, upstream, inputs, normed, gain, down, *flat)


def run_stage(upstream, inputs, gain, down, gate_full, up_full, gate_factor, up_factor):
    features, tokens = upstream.shape
    hidden = down.shape[0]
    vmem = pl.BlockSpec(memory_space=pltpu.VMEM)
    return pl.pallas_call(
        stage_kernel,
        out_shape=jax.ShapeDtypeStruct((features, tokens), bf16),
        in_specs=[vmem] * 3 + [any_space()] * 5,
        out_specs=vmem,
        scratch_shapes=[
            pltpu.VMEM((hidden, features), bf16),
            pltpu.VMEM((features, hidden), bf16),
            pltpu.VMEM((features, hidden), bf16),
            pltpu.VMEM((hidden, tokens), bf16),
            pltpu.VMEM((hidden, tokens), bf16),
            pltpu.SemaphoreType.DMA((5, len(column_chunks(hidden)))),
        ],
        compiler_params=params(),
        cost_estimate=cost(6 * tokens * features * hidden, 8 * features * hidden),
        name="stage",
    )(upstream, inputs, gain, down, gate_full, up_full, gate_factor, up_factor)


def run_blocks(sources, partners):
    rows, hidden = sources[0].shape
    step = 16
    both = 2 * (hidden // partners)
    return pl.pallas_call(
        blocks_kernel,
        grid=(rows // step,),
        out_shape=tuple(jax.ShapeDtypeStruct((partners, rows, both), bf16) for _ in range(3)),
        in_specs=[pl.BlockSpec((step, hidden), lambda i: (i, 0))] * 6,
        out_specs=tuple(pl.BlockSpec((partners, step, both), lambda i: (0, i, 0)) for _ in range(3)),
        compiler_params=params(),
        name="state_blocks",
    )(*sources)


def run_factors(own, scale_pair, normed_all, gate_full, up_full):
    partners, features, tokens = normed_all.shape
    both = 2 * (gate_full.shape[1] // partners)
    return pl.pallas_call(
        factors_kernel,
        grid_spec=pltpu.PrefetchScalarGridSpec(
            num_scalar_prefetch=1,
            grid=(partners,),
            in_specs=[
                smem_space(),
                pl.BlockSpec((1, features, tokens), lambda k, own: (own[0] ^ k, 0, 0)),
                any_space(),
                any_space(),
            ],
            out_specs=pl.BlockSpec((1, both, tokens), lambda k, own: (k, 0, 0)),
            scratch_shapes=[
                pltpu.VMEM((features, 512), bf16),
                pltpu.VMEM((features, 512), bf16),
                pltpu.VMEM((both, features), bf16),
                pltpu.SemaphoreType.DMA((2,)),
            ],
        ),
        out_shape=jax.ShapeDtypeStruct((partners, both, tokens), bf16),
        compiler_params=params(),
        cost_estimate=cost(2 * partners * tokens * features * both, 8 * features * both),
        name="column_factors",
    )(own, scale_pair, normed_all, gate_full, up_full)


def run_weights(own, down_cols, normed_all, factor_cols, pieces, distances, start=None):
    partners, features, tokens = normed_all.shape
    columns = down_cols.shape[0]
    count = len(distances)
    vmem = pl.BlockSpec(memory_space=pltpu.VMEM)
    starts = [] if start is None else [start]
    return pl.pallas_call(
        functools.partial(weight_kernel, distances=distances, has_start=len(starts)),
        out_shape=jax.ShapeDtypeStruct((features, 2 * columns), f32 if start is None else bf16),
        in_specs=[smem_space(), vmem] + [any_space()] * (2 + count) + [vmem] * len(starts),
        out_specs=vmem,
        scratch_shapes=[
            pltpu.VMEM((count, features, tokens), bf16),
            pltpu.VMEM((count, features, tokens), bf16),
            pltpu.VMEM((count, 2 * columns, tokens), bf16),
            pltpu.SemaphoreType.DMA((3, count)),
        ],
        compiler_params=params(),
        cost_estimate=cost(6 * count * tokens * features * columns, 12 * features * columns),
        name="column_gradients",
    )(own, down_cols, normed_all, factor_cols, *pieces, *starts)


def run_next(gradient, state, next_all):
    partners, features, tokens = next_all.shape
    both = gradient.shape[1]
    return pl.pallas_call(
        next_kernel,
        grid=(partners,),
        out_shape=(
            jax.ShapeDtypeStruct((partners, both // 2, tokens), bf16),
            jax.ShapeDtypeStruct((8, 128), f32),
        ),
        in_specs=[whole((features, both))] * 4
        + [pl.BlockSpec((1, features, tokens), lambda k: (k, 0, 0))],
        out_specs=(
            pl.BlockSpec((1, both // 2, tokens), lambda k: (k, 0, 0)),
            whole((8, 128)),
        ),
        scratch_shapes=[pltpu.VMEM((both, features), bf16)],
        compiler_params=params(),
        name="next_columns",
    )(gradient, *state, next_all)


def run_rows(blocks, sources):
    partners, rows, both = blocks.shape
    hidden = sources[0].shape[1]
    step = 16
    row_spec = pl.BlockSpec((step, hidden), lambda i: (i, 0))
    return pl.pallas_call(
        rows_kernel,
        grid=(rows // step,),
        out_shape=tuple(jax.ShapeDtypeStruct((rows, hidden), f32) for _ in range(6)),
        in_specs=[pl.BlockSpec((partners, step, both), lambda i: (0, i, 0))] + [row_spec] * 6,
        out_specs=(row_spec,) * 6,
        scratch_shapes=[pltpu.VMEM((step, hidden), f32)],
        compiler_params=params(),
        name="row_update",
    )(blocks, *sources)


def down_shift(value, sections):
    return lax.ppermute(value, "section", [(source, source - 1) for source in range(1, sections)])


def columns_plan(
    section_inputs,
    cotangent,
    norm_gain,
    quant_gate,
    quant_up,
    scales,
    down_proj,
    master_gate,
    master_up,
    moment_gate,
    moment_up,
    second_gate,
    second_up,
    next_inputs,
):
    gain_row = norm_gain[0]
    scale_pair = scales[0]
    down_local = down_proj[0]
    inputs = section_inputs[0]
    tok_rows, feature_count = inputs.shape
    own_rows, hidden_count = quant_gate.shape[1:]
    partners = lax.axis_size("dp")
    own_cols = hidden_count // partners
    sections = lax.axis_size("section")
    is_last = lax.axis_index("section") == sections - 1
    own_index = lax.axis_index("dp")
    own = own_index.astype(jnp.int32).reshape(1)
    barrier = lax.optimization_barrier

    weight_pieces = spread_weights(quant_gate[0], quant_up[0])
    normed, normed_turned, next_turned, inputs_turned, cotangent_turned = run_prep(
        inputs, next_inputs[0], cotangent, gain_row[None]
    )
    gain_column = gain_row[:, None]
    sources = [
        master_gate[0],
        master_up[0],
        moment_gate[0],
        moment_up[0],
        second_gate[0],
        second_up[0],
    ]
    state_blocks = list(run_blocks(sources, partners))

    *diagonal, normed_turned, next_turned, state_blocks = barrier(
        (*weight_pieces[6], normed_turned, next_turned, state_blocks)
    )
    weight_pieces[6] = tuple(diagonal)
    state_cols = [exchange(state_blocks[0])]
    normed_all = lax.all_gather(normed_turned[None], "dp", axis=0, tiled=True)
    result, gate_factor, up_factor, gate_full, up_full = run_first(
        own,
        scale_pair,
        cotangent_turned,
        inputs_turned,
        normed,
        gain_column,
        down_local,
        weight_pieces,
    )

    def next_stage(upstream):
        return run_stage(
            upstream,
            inputs_turned,
            gain_column,
            down_local,
            gate_full,
            up_full,
            gate_factor,
            up_factor,
        )

    down_cols = lax.dynamic_slice_in_dim(down_local, own_index * own_cols, own_cols, axis=0)
    for turn in range(sections - 1):
        if turn == sections - 2:
            result, normed_all, down_cols = barrier((result, normed_all, down_cols))
        incoming = down_shift(result, sections)
        if turn < 2:
            result, block = barrier((result, state_blocks[turn + 1]))
            state_cols.append(exchange(block))
        if turn == 1:
            result, next_turned = barrier((result, next_turned))
            next_all = lax.all_gather(next_turned[None], "dp", axis=0, tiled=True)
        if turn == sections - 2:
            factor_cols = run_factors(own, scale_pair, normed_all, gate_full, up_full)
            incoming, factor_cols, state_cols = barrier((incoming, factor_cols, state_cols))
        upstream = jnp.where(is_last, cotangent_turned, incoming)
        if turn < sections - 2:
            result = next_stage(upstream)

    near = [swap(upstream, distance) for distance in (1, 2, 4)]
    result = next_stage(upstream)
    result, *near = barrier([result] + near)
    across_c, across_x, across_y = near
    on_first_core = own_index % 2 == 0
    diagonal = (swap_some(across_y, 2, 0), swap_some(across_x, 4, 1))
    beside = [swap(across_x, 1), swap(across_y, 1)]
    gradient = run_weights(
        own,
        down_cols,
        normed_all,
        factor_cols,
        [upstream, across_c, across_x, across_y],
        (0, 1, 2, 4),
    )
    across_d = jnp.where(on_first_core, *diagonal)
    gradient, across_d, *beside = barrier([gradient, across_d] + beside)
    gradient = run_weights(
        own,
        down_cols,
        normed_all,
        factor_cols,
        beside + [across_d, swap(across_d, 1)],
        (3, 5, 6, 7),
        gradient,
    )
    row_blocks = exchange(gradient.reshape(partners, own_rows, 2 * own_cols))
    state = [part.reshape(feature_count, 2 * own_cols) for part in state_cols]
    token_blocks, peaks = run_next(gradient, state, next_all)
    next_hidden = exchange(token_blocks).reshape(hidden_count, tok_rows).T
    peaks = jnp.maximum(peaks, swap(peaks, 1))
    updated = run_rows(row_blocks, sources)
    peaks, *updated = barrier([peaks, *updated])
    peaks = jnp.maximum(peaks, swap(peaks, 2))
    peaks = jnp.maximum(peaks, swap(peaks, 4))
    new_scales = peaks[:2, 0] + scale_eps
    return (
        result.T[None],
        *(part[None] for part in updated),
        new_scales[None, :],
        next_hidden[None],
    )


def plain_plan(
    section_inputs,
    cotangent,
    norm_gain,
    quant_gate,
    quant_up,
    scales,
    down_proj,
    master_gate,
    master_up,
    moment_gate,
    moment_up,
    second_gate,
    second_up,
    next_inputs,
):
    gain_row = norm_gain[0]
    scale_pair = scales[0]
    down_local = down_proj[0]
    hidden_count = quant_gate.shape[2]
    sections = lax.axis_size("section")
    position = lax.axis_index("section")
    is_last = position == sections - 1
    both_full = lax.all_gather(
        jnp.concatenate([quant_gate[0], quant_up[0]], axis=1), "dp", axis=0, tiled=True
    )
    widened, inverse, normed = normalize(section_inputs[0], gain_row)
    both_pre = jnp.dot(normed, both_full, preferred_element_type=jnp.float32)
    gate_pre = both_pre[:, :hidden_count] * scale_pair[0]
    up_pre = both_pre[:, hidden_count:] * scale_pair[1]
    sigmoid = jax.nn.sigmoid(gate_pre)
    up_factor = gate_pre * sigmoid
    gate_factor = up_pre * (sigmoid * (1.0 + gate_pre * (1.0 - sigmoid)))
    cubed = inverse * inverse * inverse

    def stage(upstream):
        hidden_grad = transposed(upstream, down_local)
        gate_grad = (hidden_grad * gate_factor).astype(jnp.bfloat16)
        up_grad = (hidden_grad * up_factor).astype(jnp.bfloat16)
        normed_grad = (
            transposed(gate_grad, both_full[:, :hidden_count]) * scale_pair[0]
            + transposed(up_grad, both_full[:, hidden_count:]) * scale_pair[1]
        )
        gained = gain_row * normed_grad
        mean_term = jnp.mean(widened * gained, axis=-1, keepdims=True)
        result = upstream.astype(jnp.float32) + inverse * gained - widened * cubed * mean_term
        return (result.astype(jnp.bfloat16), gate_grad, up_grad)

    upstream = cotangent
    for turn in range(sections):
        result, gate_grad, up_grad = stage(upstream)
        if turn < sections - 1:
            incoming = lax.ppermute(
                result, "section", [(source, source - 1) for source in range(1, sections)]
            )
            upstream = jnp.where(is_last, cotangent, incoming)

    grads_all = jnp.concatenate([gate_grad, up_grad], axis=1)
    summed = lax.psum_scatter(
        lax.dot_general(
            normed, grads_all, (((0,), (0,)), ((), ())), preferred_element_type=jnp.float32
        ).astype(jnp.bfloat16),
        "dp",
        scatter_dimension=0,
        tiled=True,
    ).astype(jnp.float32)
    new_gate, mom_gate, sec_gate = adam_update(
        master_gate[0], moment_gate[0], second_gate[0], summed[:, :hidden_count]
    )
    new_up, mom_up, sec_up = adam_update(
        master_up[0], moment_up[0], second_up[0], summed[:, hidden_count:]
    )
    peaks = jnp.stack([jnp.max(jnp.abs(new_gate)), jnp.max(jnp.abs(new_up))])
    new_scales = ring_max(peaks, "dp") + scale_eps
    unused_one, unused_two, next_normed = normalize(next_inputs[0], gain_row)
    stacked = jnp.concatenate([new_gate, new_up], axis=1).astype(jnp.bfloat16)
    both_next = jnp.dot(
        next_normed,
        lax.all_gather(stacked, "dp", axis=0, tiled=True),
        preferred_element_type=jnp.float32,
    )
    next_hidden = (
        jax.nn.silu(both_next[:, :hidden_count]) * both_next[:, hidden_count:]
    ).astype(jnp.bfloat16)
    return (
        result[None],
        new_gate[None],
        new_up[None],
        mom_gate[None],
        mom_up[None],
        sec_gate[None],
        sec_up[None],
        new_scales[None, :],
        next_hidden[None],
    )


def solution(mesh):
    placed = (
        P("section", "dp", None),
        P("dp", None),
        P("section", None),
        P("section", "dp", None),
        P("section", "dp", None),
        P("section", None),
        P("section", None, None),
        P("section", "dp", None),
        P("section", "dp", None),
        P("section", "dp", None),
        P("section", "dp", None),
        P("section", "dp", None),
        P("section", "dp", None),
        P("section", "dp", None),
    )
    fits = mesh.shape["dp"] == 8 and mesh.shape["section"] >= 4
    return jax.shard_map(
        columns_plan if fits else plain_plan,
        mesh=mesh,
        in_specs=placed,
        out_specs=(
            P("section", "dp", None),
            P("section", "dp", None),
            P("section", "dp", None),
            P("section", "dp", None),
            P("section", "dp", None),
            P("section", "dp", None),
            P("section", "dp", None),
            P("section", None),
            P("section", "dp", None),
        ),
        check_vma=False,
    )
```

```python
import functools

import jax
import jax.numpy as jnp
from jax import lax
from jax.experimental import pallas as pl
from jax.experimental.pallas import tpu as pltpu
from jax.sharding import PartitionSpec as P

beta_one = 0.9
beta_two = 0.95
learn_rate = 0.002
decay_rate = 0.1
adam_steps = 100.0
norm_eps = 1e-06
adam_eps = 1e-08
scale_eps = 1e-06
mib = 1024 * 1024
bf16 = jnp.bfloat16
f32 = jnp.float32


def normalize(inputs, norm_gain):
    widened = inputs.astype(jnp.float32)
    inverse = lax.rsqrt(jnp.mean(widened * widened, axis=-1, keepdims=True) + norm_eps)
    return (widened, inverse, (widened * inverse * norm_gain).astype(jnp.bfloat16))


def matmul(first_op, second_op):
    return jnp.dot(first_op, second_op, preferred_element_type=jnp.float32)


def transposed(first_op, second_op):
    return lax.dot_general(
        first_op, second_op, (((1,), (1,)), ((), ())), preferred_element_type=jnp.float32
    )


def adam_update(master, moment_old, second_old, gradient):
    moment_one = beta_one * moment_old + (1.0 - beta_one) * gradient
    moment_two = beta_two * second_old + (1.0 - beta_two) * gradient * gradient
    unbiased_one = moment_one / (1.0 - beta_one**adam_steps)
    unbiased_two = moment_two / (1.0 - beta_two**adam_steps)
    updated = master - learn_rate * (
        unbiased_one / (jnp.sqrt(unbiased_two) + adam_eps) + decay_rate * master
    )
    return (updated, moment_one, moment_two)


def factors(gate_pre, up_pre):
    sigmoid = jax.nn.sigmoid(gate_pre)
    return (up_pre * (sigmoid * (1.0 + gate_pre * (1.0 - sigmoid))), gate_pre * sigmoid)


def exchange(blocks):
    return lax.all_to_all(blocks, "dp", split_axis=0, concat_axis=0, tiled=True)


def swap(value, distance):
    pairs = [(source, source ^ distance) for source in range(lax.axis_size("dp"))]
    return lax.ppermute(value, "dp", pairs)


def swap_some(value, distance, core):
    pairs = [(k, k ^ distance) for k in range(lax.axis_size("dp")) if k % 2 == core]
    return lax.ppermute(value, "dp", pairs)


def spread_weights(gate, up, near):
    gate_x, up_x, gate_y, up_y, gate_c, up_c = near
    diagonal = [swap(gate_y, 2), swap(up_x, 4)]
    beside = [swap(part, 1) for part in (gate_x, up_x, gate_y, up_y)]
    gate_d, up_d, *beside = lax.optimization_barrier(diagonal + beside)
    return [
        (gate, up),
        (gate_c, up_c),
        (gate_x, up_x),
        (beside[0], beside[1]),
        (gate_y, up_y),
        (beside[2], beside[3]),
        (gate_d, up_d),
        (swap(gate_d, 1), swap(up_d, 1)),
    ]


def ring_max(value, axis):
    count = lax.axis_size(axis)
    span = 1
    while span < count:
        pairs = [(source, (source + span) % count) for source in range(count)]
        value = jnp.maximum(value, lax.ppermute(value, axis, pairs))
        span *= 2
    return value


def column_chunks(total, width=512):
    return [(start, min(width, total - start)) for start in range(0, total, width)]


def finish_stage(upstream, normed_grad, widened, gain_row):
    inverse = lax.rsqrt(jnp.mean(widened * widened, axis=1, keepdims=True) + norm_eps)
    gained = gain_row * normed_grad
    mean_term = jnp.mean(widened * gained, axis=1, keepdims=True)
    cubed = inverse * inverse * inverse
    return (upstream.astype(f32) + inverse * gained - widened * cubed * mean_term).astype(bf16)


def prep_kernel(inputs_ref, next_ref, gain_ref, normed_ref, turned_ref, next_out):
    gain_row = gain_ref[...]
    normed = normalize(inputs_ref[...], gain_row)[2]
    normed_ref[...] = normed
    turned_ref[...] = normed.T
    next_out[...] = normalize(next_ref[...], gain_row)[2].T


def first_kernel(
    own_ref, scale_ref, upstream_ref, inputs_ref, normed_ref, gain_ref, down, *refs, partners
):
    pieces = refs[: 2 * partners]
    result_ref, gate_factor_ref, up_factor_ref, gate_full, up_full = refs[2 * partners :]
    rows = pieces[0].shape[0]
    own = own_ref[0]
    for index in range(2 * partners):
        place = pl.ds(pl.multiple_of((own ^ (index // 2)) * rows, 16), rows)
        full = gate_full if index % 2 == 0 else up_full
        full[place, :] = pieces[index][...]
    upstream = upstream_ref[...]
    normed = normed_ref[...]
    normed_grad = jnp.zeros(upstream.shape, f32)
    for start, width in column_chunks(gate_full.shape[1]):
        part = slice(start, start + width)
        gate_part, up_part = gate_full[:, part], up_full[:, part]
        gate_factor, up_factor = factors(
            matmul(normed, gate_part) * scale_ref[0], matmul(normed, up_part) * scale_ref[1]
        )
        gate_factor = (gate_factor * scale_ref[0]).astype(bf16)
        up_factor = (up_factor * scale_ref[1]).astype(bf16)
        gate_factor_ref[:, part] = gate_factor
        up_factor_ref[:, part] = up_factor
        hidden_grad = transposed(upstream, down[part, :])
        normed_grad += transposed((hidden_grad * gate_factor).astype(bf16), gate_part)
        normed_grad += transposed((hidden_grad * up_factor).astype(bf16), up_part)
    result_ref[...] = finish_stage(
        upstream, normed_grad, inputs_ref[...].astype(f32), gain_ref[...]
    )


def stage_kernel(
    upstream_ref, inputs_ref, gain_ref, down, gate_full, up_full, gate_factor, up_factor, result_ref
):
    upstream = upstream_ref[...]
    normed_grad = jnp.zeros(upstream.shape, f32)
    for start, width in column_chunks(gate_full.shape[1]):
        part = slice(start, start + width)
        hidden_grad = transposed(upstream, down[part, :])
        gate_grad = (hidden_grad * gate_factor[:, part]).astype(bf16)
        up_grad = (hidden_grad * up_factor[:, part]).astype(bf16)
        normed_grad += transposed(gate_grad, gate_full[:, part])
        normed_grad += transposed(up_grad, up_full[:, part])
    result_ref[...] = finish_stage(
        upstream, normed_grad, inputs_ref[...].astype(f32), gain_ref[...]
    )


def blocks_kernel(*refs):
    sources, targets = refs[:6], refs[6:]
    for kind in range(3):
        gate = sources[2 * kind][...].astype(bf16)
        up = sources[2 * kind + 1][...].astype(bf16)
        partners, unused, both = targets[kind].shape
        columns = both // 2
        for k in range(partners):
            part = slice(k * columns, (k + 1) * columns)
            targets[kind][k, :, :columns] = gate[:, part]
            targets[kind][k, :, columns:] = up[:, part]


def factors_kernel(
    own_ref, scale_ref, normed_ref, gate_full, up_full, out_gate, out_up, gate, up, normed
):
    partners, features, tokens = normed_ref.shape
    columns = gate.shape[1]
    group = normed.shape[0] // tokens
    own = own_ref[0]
    for k in range(partners):
        part = slice(k * columns, (k + 1) * columns)

        @pl.when(own == k)
        def pick():
            gate[...] = gate_full[:, part]
            up[...] = up_full[:, part]

    for first in range(0, partners, group):
        for k in range(group):
            normed[k * tokens : (k + 1) * tokens, :] = normed_ref[own ^ (first + k)].T
        rows = slice(first * tokens, (first + group) * tokens)
        gate_factor, up_factor = factors(
            matmul(normed[...], gate[...]) * scale_ref[0],
            matmul(normed[...], up[...]) * scale_ref[1],
        )
        out_gate[rows, :] = gate_factor.astype(bf16)
        out_up[rows, :] = up_factor.astype(bf16)


def weight_kernel(own_ref, down_ref, normed_ref, gate_factor, up_factor, *refs, distances, first):
    count = len(distances)
    pieces = refs[:count]
    if first:
        (out_ref,) = refs[count : count + 1]
    else:
        start_ref = refs[count]
        outs = refs[count + 1 : -3]
    upstream, normed, total = refs[-3:]
    own = own_ref[0]
    tokens = pieces[0].shape[0]
    factor_rows = []
    for place, distance in enumerate(distances):
        block = slice(place * tokens, (place + 1) * tokens)
        upstream[block, :] = pieces[place][...]
        normed[:, block] = normed_ref[own ^ distance]
        factor_rows.append(slice(distance * tokens, (distance + 1) * tokens))
    hidden_grad = transposed(upstream[...], down_ref[...])
    gate_grad = hidden_grad * jnp.concatenate([gate_factor[rows, :] for rows in factor_rows], axis=0)
    up_grad = hidden_grad * jnp.concatenate([up_factor[rows, :] for rows in factor_rows], axis=0)
    grads = jnp.concatenate([gate_grad, up_grad], axis=1).astype(bf16)
    product = matmul(normed[...], grads)
    if first:
        out_ref[...] = product
        return
    total[...] = (start_ref[...] + product).astype(bf16)
    outs[0][...] = total[...]
    rows = outs[1].shape[0]
    for distance in range(len(outs) - 1):
        place = pl.ds(pl.multiple_of((own ^ distance) * rows, 16), rows)
        outs[1 + distance][...] = total[place, :]


def next_kernel(
    gradient_ref, master_ref, moment_ref, second_ref, next_ref, out_ref, peak_ref, turned, joined
):
    partners, features, tokens = next_ref.shape
    columns = turned.shape[0] // 2
    group = joined.shape[1] // tokens
    peaks = jnp.zeros((1, 2 * columns), f32)
    for start in range(0, features, 128):
        rows = slice(start, min(start + 128, features))
        updated, unused_one, unused_two = adam_update(
            master_ref[rows, :].astype(f32),
            moment_ref[rows, :].astype(f32),
            second_ref[rows, :].astype(f32),
            gradient_ref[rows, :].astype(f32),
        )
        peaks = jnp.maximum(peaks, jnp.max(jnp.abs(updated), axis=0, keepdims=True))
        turned[:, rows] = updated.astype(bf16).T
    is_gate = lax.broadcasted_iota(jnp.int32, peaks.shape, 1) < columns
    peak_ref[0:1, :] = jnp.full((1, 128), jnp.max(jnp.where(is_gate, peaks, 0.0)), f32)
    peak_ref[1:2, :] = jnp.full((1, 128), jnp.max(jnp.where(is_gate, 0.0, peaks)), f32)
    for first in range(0, partners, group):
        for k in range(group):
            joined[:, k * tokens : (k + 1) * tokens] = next_ref[first + k]
        both = matmul(turned[...], joined[...])
        gate, up = both[:columns], both[columns:]
        hidden = (gate * jax.nn.sigmoid(gate) * up).astype(bf16)
        for k in range(group):
            out_ref[first + k] = hidden[:, k * tokens : (k + 1) * tokens]


def rows_kernel(own_ref, *refs, partners, side):
    pieces = refs[:partners]
    sources, targets = refs[partners : partners + 3], refs[partners + 3 : partners + 6]
    blocks, gradient = refs[partners + 6 :]
    own = own_ref[0]
    columns = pieces[0].shape[1] // 2
    for distance in range(partners):
        blocks[own ^ distance] = pieces[distance][...].astype(f32)
    for k in range(partners):
        gradient[:, k * columns : (k + 1) * columns] = blocks[
            k, :, side * columns : (side + 1) * columns
        ]
    results = adam_update(sources[0][...], sources[1][...], sources[2][...], gradient[...])
    for kind in range(3):
        targets[kind][...] = results[kind]


def cost(flops, accessed):
    return pl.CostEstimate(flops=flops, bytes_accessed=accessed, transcendentals=0)


def smem_space():
    return pl.BlockSpec(memory_space=pltpu.SMEM)


def params(limit):
    return pltpu.CompilerParams(vmem_limit_bytes=limit * mib)


def in_vmem(count):
    return [pl.BlockSpec(memory_space=pltpu.VMEM)] * count


def run_prep(inputs, next_part, gain_row):
    tokens, features = inputs.shape
    turned = jax.ShapeDtypeStruct((features, tokens), bf16)
    return pl.pallas_call(
        prep_kernel,
        out_shape=(jax.ShapeDtypeStruct((tokens, features), bf16), turned, turned),
        compiler_params=params(8),
        name="prep",
    )(inputs, next_part, gain_row)


def run_first(own, scale_pair, upstream, inputs, normed, gain, down, pieces):
    tokens, features = upstream.shape
    hidden = down.shape[0]
    partners = len(pieces)
    flat = [part for pair in pieces for part in pair]
    return pl.pallas_call(
        functools.partial(first_kernel, partners=partners),
        out_shape=(
            jax.ShapeDtypeStruct((tokens, features), bf16),
            jax.ShapeDtypeStruct((tokens, hidden), bf16),
            jax.ShapeDtypeStruct((tokens, hidden), bf16),
            jax.ShapeDtypeStruct((features, hidden), bf16),
            jax.ShapeDtypeStruct((features, hidden), bf16),
        ),
        in_specs=[smem_space(), smem_space()] + in_vmem(5 + len(flat)),
        out_specs=tuple(in_vmem(5)),
        compiler_params=params(34),
        cost_estimate=cost(10 * tokens * features * hidden, 26 * features * hidden),
        name="first_stage",
    )(own, scale_pair, upstream, inputs, normed, gain, down, *flat)


def run_stage(upstream, inputs, gain, down, gate_full, up_full, gate_factor, up_factor):
    tokens, features = upstream.shape
    hidden = down.shape[0]
    return pl.pallas_call(
        stage_kernel,
        out_shape=jax.ShapeDtypeStruct((tokens, features), bf16),
        in_specs=in_vmem(8),
        out_specs=in_vmem(1)[0],
        compiler_params=params(23),
        cost_estimate=cost(6 * tokens * features * hidden, 8 * features * hidden),
        name="stage",
    )(upstream, inputs, gain, down, gate_full, up_full, gate_factor, up_factor)


def run_blocks(sources, partners):
    rows, hidden = sources[0].shape
    step = 16
    both = 2 * (hidden // partners)
    return pl.pallas_call(
        blocks_kernel,
        grid=(rows // step,),
        out_shape=tuple(jax.ShapeDtypeStruct((partners, rows, both), bf16) for _ in range(3)),
        in_specs=[pl.BlockSpec((step, hidden), lambda i: (i, 0))] * 6,
        out_specs=tuple(pl.BlockSpec((partners, step, both), lambda i: (0, i, 0)) for _ in range(3)),
        compiler_params=params(12),
        name="state_blocks",
    )(*sources)


def run_factors(own, scale_pair, normed_all, gate_full, up_full):
    partners, features, tokens = normed_all.shape
    columns = gate_full.shape[1] // partners
    shape = jax.ShapeDtypeStruct((partners * tokens, columns), bf16)
    return pl.pallas_call(
        factors_kernel,
        out_shape=(shape, shape),
        in_specs=[smem_space(), smem_space()] + in_vmem(3),
        out_specs=tuple(in_vmem(2)),
        scratch_shapes=[
            pltpu.VMEM((features, columns), bf16),
            pltpu.VMEM((features, columns), bf16),
            pltpu.VMEM((partners * tokens // 2, features), bf16),
        ],
        compiler_params=params(28),
        cost_estimate=cost(4 * partners * tokens * features * columns, 8 * features * columns),
        name="column_factors",
    )(own, scale_pair, normed_all, gate_full, up_full)


def run_weights(own, down_cols, normed_all, factor_cols, pieces, distances, start=None):
    partners, features, tokens = normed_all.shape
    columns = down_cols.shape[0]
    count = len(distances)
    first = start is None
    if first:
        shapes = jax.ShapeDtypeStruct((features, 2 * columns), f32)
        starts = []
    else:
        block = jax.ShapeDtypeStruct((features // partners, 2 * columns), bf16)
        shapes = (jax.ShapeDtypeStruct((features, 2 * columns), bf16),) + (block,) * partners
        starts = [start]
    return pl.pallas_call(
        functools.partial(weight_kernel, distances=distances, first=first),
        out_shape=shapes,
        in_specs=[smem_space()] + in_vmem(4 + count + len(starts)),
        out_specs=in_vmem(1)[0] if first else tuple(in_vmem(1 + partners)),
        scratch_shapes=[
            pltpu.VMEM((count * tokens, features), bf16),
            pltpu.VMEM((features, count * tokens), bf16),
            pltpu.VMEM((features, 2 * columns), bf16),
        ],
        compiler_params=params(30),
        cost_estimate=cost(6 * count * tokens * features * columns, 12 * features * columns),
        name="column_gradients",
    )(own, down_cols, normed_all, *factor_cols, *pieces, *starts)


def run_next(gradient, state, next_all):
    partners, features, tokens = next_all.shape
    both = gradient.shape[1]
    return pl.pallas_call(
        next_kernel,
        out_shape=(
            jax.ShapeDtypeStruct((partners, both // 2, tokens), bf16),
            jax.ShapeDtypeStruct((8, 128), f32),
        ),
        in_specs=in_vmem(5),
        out_specs=tuple(in_vmem(2)),
        scratch_shapes=[
            pltpu.VMEM((both, features), bf16),
            pltpu.VMEM((features, partners * tokens // 2), bf16),
        ],
        compiler_params=params(28),
        cost_estimate=cost(2 * partners * tokens * features * both, 16 * features * both),
        name="next_columns",
    )(gradient, *state, next_all)


def run_rows(own, pieces, sources, side):
    partners = len(pieces)
    rows, hidden = sources[0].shape
    both = pieces[0].shape[1]
    step = 16
    row_spec = pl.BlockSpec((step, hidden), lambda i: (i, 0))
    return pl.pallas_call(
        functools.partial(rows_kernel, partners=partners, side=side),
        grid=(rows // step,),
        out_shape=tuple(jax.ShapeDtypeStruct((rows, hidden), f32) for _ in range(3)),
        in_specs=[smem_space()]
        + [pl.BlockSpec((step, both), lambda i: (i, 0))] * partners
        + [row_spec] * 3,
        out_specs=(row_spec,) * 3,
        scratch_shapes=[
            pltpu.VMEM((partners, step, both), f32),
            pltpu.VMEM((step, hidden), f32),
        ],
        compiler_params=params(8),
        name="row_update",
    )(own, *pieces, *sources)


def down_shift(value, sections):
    return lax.ppermute(value, "section", [(source, source - 1) for source in range(1, sections)])


def columns_plan(
    section_inputs,
    cotangent,
    norm_gain,
    quant_gate,
    quant_up,
    scales,
    down_proj,
    master_gate,
    master_up,
    moment_gate,
    moment_up,
    second_gate,
    second_up,
    next_inputs,
):
    gain_row = norm_gain[0]
    scale_pair = scales[0]
    down_local = down_proj[0]
    inputs = section_inputs[0]
    tok_rows, feature_count = inputs.shape
    own_rows, hidden_count = quant_gate.shape[1:]
    partners = lax.axis_size("dp")
    own_cols = hidden_count // partners
    sections = lax.axis_size("section")
    is_last = lax.axis_index("section") == sections - 1
    own_index = lax.axis_index("dp")
    own = own_index.astype(jnp.int32).reshape(1)
    barrier = lax.optimization_barrier

    near = [swap(part, distance) for distance in (2, 4, 1) for part in (quant_gate[0], quant_up[0])]
    normed, normed_turned, next_turned = run_prep(inputs, next_inputs[0], gain_row[None])
    gate_sources = (master_gate[0], moment_gate[0], second_gate[0])
    up_sources = (master_up[0], moment_up[0], second_up[0])
    state_blocks = run_blocks(
        [part for pair in zip(gate_sources, up_sources) for part in pair], partners
    )
    *near, normed, normed_turned, next_turned, state_blocks = barrier(
        (*near, normed, normed_turned, next_turned, state_blocks)
    )
    normed_all = lax.all_gather(normed_turned[None], "dp", axis=0, tiled=True)
    weight_pieces = spread_weights(quant_gate[0], quant_up[0], near)
    result, gate_factor, up_factor, gate_full, up_full = run_first(
        own, scale_pair, cotangent, inputs, normed, gain_row[None], down_local, weight_pieces
    )

    def next_stage(upstream):
        return run_stage(
            upstream, inputs, gain_row[None], down_local, gate_full, up_full, gate_factor, up_factor
        )

    state_cols = []
    down_cols = lax.dynamic_slice_in_dim(down_local, own_index * own_cols, own_cols, axis=0)
    for turn in range(sections - 1):
        if turn == sections - 2:
            result, normed_all, down_cols = barrier((result, normed_all, down_cols))
        incoming = down_shift(result, sections)
        if turn < 3:
            result, block = barrier((result, state_blocks[turn]))
            state_cols.append(exchange(block))
        if turn == 1:
            result, next_turned = barrier((result, next_turned))
            next_all = lax.all_gather(next_turned[None], "dp", axis=0, tiled=True)
        if turn == sections - 2:
            factor_cols = run_factors(own, scale_pair, normed_all, gate_full, up_full)
            incoming, factor_cols, state_cols[:2] = barrier(
                (incoming, factor_cols, state_cols[:2])
            )
        upstream = jnp.where(is_last, cotangent, incoming)
        if turn < sections - 2:
            result = next_stage(upstream)

    near = [swap(upstream, distance) for distance in (1, 2, 4)]
    result = next_stage(upstream)
    result, *near = barrier([result] + near)
    across_c, across_x, across_y = near
    on_first_core = own_index % 2 == 0
    diagonal = (swap_some(across_y, 2, 0), swap_some(across_x, 4, 1))
    beside = [swap(across_x, 1), swap(across_y, 1)]
    gradient = run_weights(
        own,
        down_cols,
        normed_all,
        factor_cols,
        [upstream, across_c, across_x, across_y],
        (0, 1, 2, 4),
    )
    across_d = jnp.where(on_first_core, *diagonal)
    gradient, across_d, *beside = barrier([gradient, across_d] + beside)
    gradient, *row_blocks = run_weights(
        own,
        down_cols,
        normed_all,
        factor_cols,
        beside + [across_d, swap(across_d, 1)],
        (3, 5, 6, 7),
        gradient,
    )
    row_pieces = row_blocks[:1] + [
        swap(row_blocks[distance], distance) for distance in range(1, partners)
    ]
    state = [part.reshape(feature_count, 2 * own_cols) for part in state_cols]
    token_blocks, peaks = run_next(gradient, state, next_all)
    token_pieces = exchange(token_blocks)
    peaks, *row_pieces = barrier([jnp.maximum(peaks, swap(peaks, 1)), *row_pieces])
    new_gate, mom_gate, sec_gate = run_rows(own, row_pieces, gate_sources, 0)
    peaks, *row_pieces = barrier([jnp.maximum(peaks, swap(peaks, 2)), *row_pieces, new_gate])
    new_gate = row_pieces.pop()
    new_up, mom_up, sec_up = run_rows(own, row_pieces, up_sources, 1)
    peaks = jnp.maximum(peaks, swap(peaks, 4))
    new_scales = peaks[:2, 0] + scale_eps
    next_hidden = token_pieces.reshape(hidden_count, tok_rows).T
    updated = (new_gate, new_up, mom_gate, mom_up, sec_gate, sec_up)
    return (
        result[None],
        *(part[None] for part in updated),
        new_scales[None, :],
        next_hidden[None],
    )


def plain_plan(
    section_inputs,
    cotangent,
    norm_gain,
    quant_gate,
    quant_up,
    scales,
    down_proj,
    master_gate,
    master_up,
    moment_gate,
    moment_up,
    second_gate,
    second_up,
    next_inputs,
):
    gain_row = norm_gain[0]
    scale_pair = scales[0]
    down_local = down_proj[0]
    hidden_count = quant_gate.shape[2]
    sections = lax.axis_size("section")
    position = lax.axis_index("section")
    is_last = position == sections - 1
    both_full = lax.all_gather(
        jnp.concatenate([quant_gate[0], quant_up[0]], axis=1), "dp", axis=0, tiled=True
    )
    widened, inverse, normed = normalize(section_inputs[0], gain_row)
    both_pre = jnp.dot(normed, both_full, preferred_element_type=jnp.float32)
    gate_pre = both_pre[:, :hidden_count] * scale_pair[0]
    up_pre = both_pre[:, hidden_count:] * scale_pair[1]
    sigmoid = jax.nn.sigmoid(gate_pre)
    up_factor = gate_pre * sigmoid
    gate_factor = up_pre * (sigmoid * (1.0 + gate_pre * (1.0 - sigmoid)))
    cubed = inverse * inverse * inverse

    def stage(upstream):
        hidden_grad = transposed(upstream, down_local)
        gate_grad = (hidden_grad * gate_factor).astype(jnp.bfloat16)
        up_grad = (hidden_grad * up_factor).astype(jnp.bfloat16)
        normed_grad = (
            transposed(gate_grad, both_full[:, :hidden_count]) * scale_pair[0]
            + transposed(up_grad, both_full[:, hidden_count:]) * scale_pair[1]
        )
        gained = gain_row * normed_grad
        mean_term = jnp.mean(widened * gained, axis=-1, keepdims=True)
        result = upstream.astype(jnp.float32) + inverse * gained - widened * cubed * mean_term
        return (result.astype(jnp.bfloat16), gate_grad, up_grad)

    upstream = cotangent
    for turn in range(sections):
        result, gate_grad, up_grad = stage(upstream)
        if turn < sections - 1:
            incoming = lax.ppermute(
                result, "section", [(source, source - 1) for source in range(1, sections)]
            )
            upstream = jnp.where(is_last, cotangent, incoming)

    grads_all = jnp.concatenate([gate_grad, up_grad], axis=1)
    summed = lax.psum_scatter(
        lax.dot_general(
            normed, grads_all, (((0,), (0,)), ((), ())), preferred_element_type=jnp.float32
        ).astype(jnp.bfloat16),
        "dp",
        scatter_dimension=0,
        tiled=True,
    ).astype(jnp.float32)
    new_gate, mom_gate, sec_gate = adam_update(
        master_gate[0], moment_gate[0], second_gate[0], summed[:, :hidden_count]
    )
    new_up, mom_up, sec_up = adam_update(
        master_up[0], moment_up[0], second_up[0], summed[:, hidden_count:]
    )
    peaks = jnp.stack([jnp.max(jnp.abs(new_gate)), jnp.max(jnp.abs(new_up))])
    new_scales = ring_max(peaks, "dp") + scale_eps
    unused_one, unused_two, next_normed = normalize(next_inputs[0], gain_row)
    stacked = jnp.concatenate([new_gate, new_up], axis=1).astype(jnp.bfloat16)
    both_next = jnp.dot(
        next_normed,
        lax.all_gather(stacked, "dp", axis=0, tiled=True),
        preferred_element_type=jnp.float32,
    )
    next_hidden = (
        jax.nn.silu(both_next[:, :hidden_count]) * both_next[:, hidden_count:]
    ).astype(jnp.bfloat16)
    return (
        result[None],
        new_gate[None],
        new_up[None],
        mom_gate[None],
        mom_up[None],
        sec_gate[None],
        sec_up[None],
        new_scales[None, :],
        next_hidden[None],
    )


def solution(mesh):
    placed = (
        P("section", "dp", None),
        P("dp", None),
        P("section", None),
        P("section", "dp", None),
        P("section", "dp", None),
        P("section", None),
        P("section", None, None),
        P("section", "dp", None),
        P("section", "dp", None),
        P("section", "dp", None),
        P("section", "dp", None),
        P("section", "dp", None),
        P("section", "dp", None),
        P("section", "dp", None),
    )
    fits = mesh.shape["dp"] == 8 and mesh.shape["section"] >= 4
    return jax.shard_map(
        columns_plan if fits else plain_plan,
        mesh=mesh,
        in_specs=placed,
        out_specs=(
            P("section", "dp", None),
            P("section", "dp", None),
            P("section", "dp", None),
            P("section", "dp", None),
            P("section", "dp", None),
            P("section", "dp", None),
            P("section", "dp", None),
            P("section", None),
            P("section", "dp", None),
        ),
        check_vma=False,
    )
```

```python
import functools

import jax
import jax.numpy as jnp
from jax import lax
from jax.experimental import pallas as pl
from jax.experimental.pallas import tpu as pltpu
from jax.sharding import PartitionSpec as P

beta_one = 0.9
beta_two = 0.95
learn_rate = 0.002
decay_rate = 0.1
adam_steps = 100.0
norm_eps = 1e-06
adam_eps = 1e-08
scale_eps = 1e-06
mib = 1024 * 1024
bf16 = jnp.bfloat16
f32 = jnp.float32


def normalize(inputs, norm_gain):
    widened = inputs.astype(jnp.float32)
    inverse = lax.rsqrt(jnp.mean(widened * widened, axis=-1, keepdims=True) + norm_eps)
    return (widened, inverse, (widened * inverse * norm_gain).astype(jnp.bfloat16))


def matmul(first_op, second_op):
    return jnp.dot(first_op, second_op, preferred_element_type=jnp.float32)


def transposed(first_op, second_op):
    return lax.dot_general(
        first_op, second_op, (((1,), (1,)), ((), ())), preferred_element_type=jnp.float32
    )


def adam_update(master, moment_old, second_old, gradient):
    moment_one = beta_one * moment_old + (1.0 - beta_one) * gradient
    moment_two = beta_two * second_old + (1.0 - beta_two) * gradient * gradient
    unbiased_one = moment_one / (1.0 - beta_one**adam_steps)
    unbiased_two = moment_two / (1.0 - beta_two**adam_steps)
    updated = master - learn_rate * (
        unbiased_one / (jnp.sqrt(unbiased_two) + adam_eps) + decay_rate * master
    )
    return (updated, moment_one, moment_two)


def factors(gate_pre, up_pre):
    sigmoid = jax.nn.sigmoid(gate_pre)
    return (up_pre * (sigmoid * (1.0 + gate_pre * (1.0 - sigmoid))), gate_pre * sigmoid)


def exchange(blocks):
    return lax.all_to_all(blocks, "dp", split_axis=0, concat_axis=0, tiled=True)


def swap(value, distance):
    pairs = [(source, source ^ distance) for source in range(lax.axis_size("dp"))]
    return lax.ppermute(value, "dp", pairs)


def swap_some(value, distance, core):
    pairs = [(k, k ^ distance) for k in range(lax.axis_size("dp")) if k % 2 == core]
    return lax.ppermute(value, "dp", pairs)


def spread_weights(gate, up, near, beside_it):
    gate_x, up_x, gate_y, up_y, gate_c, up_c = near
    diagonal = [swap(gate_y, 2), swap(up_x, 4)]
    beside = [swap(part, 1) for part in (gate_x, up_x, gate_y, up_y)]
    (gate_d, up_d, *beside), beside_it = lax.optimization_barrier((diagonal + beside, beside_it))
    pieces = [
        (gate, up),
        (gate_c, up_c),
        (gate_x, up_x),
        (beside[0], beside[1]),
        (gate_y, up_y),
        (beside[2], beside[3]),
        (gate_d, up_d),
        (swap(gate_d, 1), swap(up_d, 1)),
    ]
    return (pieces, beside_it)


def ring_max(value, axis):
    count = lax.axis_size(axis)
    span = 1
    while span < count:
        pairs = [(source, (source + span) % count) for source in range(count)]
        value = jnp.maximum(value, lax.ppermute(value, axis, pairs))
        span *= 2
    return value


def column_chunks(total, width=512):
    return [(start, min(width, total - start)) for start in range(0, total, width)]


def finish_stage(upstream, normed_grad, widened, gain_row):
    inverse = lax.rsqrt(jnp.mean(widened * widened, axis=1, keepdims=True) + norm_eps)
    gained = gain_row * normed_grad
    mean_term = jnp.mean(widened * gained, axis=1, keepdims=True)
    cubed = inverse * inverse * inverse
    return (upstream.astype(f32) + inverse * gained - widened * cubed * mean_term).astype(bf16)


def prep_kernel(inputs_ref, next_ref, gain_ref, normed_ref, turned_ref, next_out):
    gain_row = gain_ref[...]
    normed = normalize(inputs_ref[...], gain_row)[2]
    normed_ref[...] = normed
    turned_ref[...] = normed.T
    next_out[...] = normalize(next_ref[...], gain_row)[2].T


def first_kernel(
    own_ref, scale_ref, upstream_ref, inputs_ref, normed_ref, gain_ref, down, *refs, partners
):
    pieces = refs[: 2 * partners]
    result_ref, gate_factor_ref, up_factor_ref, gate_full, up_full = refs[2 * partners :]
    rows = pieces[0].shape[0]
    own = own_ref[0]
    for index in range(2 * partners):
        place = pl.ds(pl.multiple_of((own ^ (index // 2)) * rows, 16), rows)
        full = gate_full if index % 2 == 0 else up_full
        full[place, :] = pieces[index][...]
    upstream = upstream_ref[...]
    normed = normed_ref[...]
    normed_grad = jnp.zeros(upstream.shape, f32)
    for start, width in column_chunks(gate_full.shape[1]):
        part = slice(start, start + width)
        gate_part, up_part = gate_full[:, part], up_full[:, part]
        gate_factor, up_factor = factors(
            matmul(normed, gate_part) * scale_ref[0], matmul(normed, up_part) * scale_ref[1]
        )
        gate_factor = (gate_factor * scale_ref[0]).astype(bf16)
        up_factor = (up_factor * scale_ref[1]).astype(bf16)
        gate_factor_ref[:, part] = gate_factor
        up_factor_ref[:, part] = up_factor
        hidden_grad = transposed(upstream, down[part, :])
        normed_grad += transposed((hidden_grad * gate_factor).astype(bf16), gate_part)
        normed_grad += transposed((hidden_grad * up_factor).astype(bf16), up_part)
    result_ref[...] = finish_stage(
        upstream, normed_grad, inputs_ref[...].astype(f32), gain_ref[...]
    )


def stage_kernel(
    upstream_ref, inputs_ref, gain_ref, down, gate_full, up_full, gate_factor, up_factor, result_ref
):
    upstream = upstream_ref[...]
    normed_grad = jnp.zeros(upstream.shape, f32)
    for start, width in column_chunks(gate_full.shape[1]):
        part = slice(start, start + width)
        hidden_grad = transposed(upstream, down[part, :])
        gate_grad = (hidden_grad * gate_factor[:, part]).astype(bf16)
        up_grad = (hidden_grad * up_factor[:, part]).astype(bf16)
        normed_grad += transposed(gate_grad, gate_full[:, part])
        normed_grad += transposed(up_grad, up_full[:, part])
    result_ref[...] = finish_stage(
        upstream, normed_grad, inputs_ref[...].astype(f32), gain_ref[...]
    )


def blocks_kernel(*refs):
    sources, targets = refs[:6], refs[6:]
    for kind in range(3):
        gate = sources[2 * kind][...].astype(bf16)
        up = sources[2 * kind + 1][...].astype(bf16)
        partners, unused, both = targets[kind].shape
        columns = both // 2
        for k in range(partners):
            part = slice(k * columns, (k + 1) * columns)
            targets[kind][k, :, :columns] = gate[:, part]
            targets[kind][k, :, columns:] = up[:, part]


def factors_kernel(
    own_ref, scale_ref, normed_ref, gate_full, up_full, out_gate, out_up, gate, up, normed
):
    partners, features, tokens = normed_ref.shape
    columns = gate.shape[1]
    group = normed.shape[0] // tokens
    own = own_ref[0]
    for k in range(partners):
        part = slice(k * columns, (k + 1) * columns)

        @pl.when(own == k)
        def pick():
            gate[...] = gate_full[:, part]
            up[...] = up_full[:, part]

    for first in range(0, partners, group):
        for k in range(group):
            normed[k * tokens : (k + 1) * tokens, :] = normed_ref[own ^ (first + k)].T
        rows = slice(first * tokens, (first + group) * tokens)
        gate_factor, up_factor = factors(
            matmul(normed[...], gate[...]) * scale_ref[0],
            matmul(normed[...], up[...]) * scale_ref[1],
        )
        out_gate[rows, :] = gate_factor.astype(bf16)
        out_up[rows, :] = up_factor.astype(bf16)


def weight_kernel(own_ref, down_ref, normed_ref, gate_factor, up_factor, *refs, distances, first):
    count = len(distances)
    pieces = refs[:count]
    if first:
        (out_ref,) = refs[count : count + 1]
    else:
        start_ref = refs[count]
        outs = refs[count + 1 : -3]
    upstream, normed, total = refs[-3:]
    own = own_ref[0]
    tokens = pieces[0].shape[0]
    factor_rows = []
    for place, distance in enumerate(distances):
        block = slice(place * tokens, (place + 1) * tokens)
        upstream[block, :] = pieces[place][...]
        normed[:, block] = normed_ref[own ^ distance]
        factor_rows.append(slice(distance * tokens, (distance + 1) * tokens))
    hidden_grad = transposed(upstream[...], down_ref[...])
    gate_grad = hidden_grad * jnp.concatenate([gate_factor[rows, :] for rows in factor_rows], axis=0)
    up_grad = hidden_grad * jnp.concatenate([up_factor[rows, :] for rows in factor_rows], axis=0)
    grads = jnp.concatenate([gate_grad, up_grad], axis=1).astype(bf16)
    product = matmul(normed[...], grads)
    if first:
        out_ref[...] = product
        return
    total[...] = (start_ref[...] + product).astype(bf16)
    outs[0][...] = total[...]
    rows = outs[1].shape[0]
    for distance in range(len(outs) - 1):
        place = pl.ds(pl.multiple_of((own ^ distance) * rows, 16), rows)
        outs[1 + distance][...] = total[place, :]


def next_kernel(
    gradient_ref, master_ref, moment_ref, second_ref, next_ref, out_ref, peak_ref, turned, joined
):
    partners, features, tokens = next_ref.shape
    columns = turned.shape[0] // 2
    group = joined.shape[1] // tokens
    peaks = jnp.zeros((1, 2 * columns), f32)
    for start in range(0, features, 128):
        rows = slice(start, min(start + 128, features))
        updated, unused_one, unused_two = adam_update(
            master_ref[rows, :].astype(f32),
            moment_ref[rows, :].astype(f32),
            second_ref[rows, :].astype(f32),
            gradient_ref[rows, :].astype(f32),
        )
        peaks = jnp.maximum(peaks, jnp.max(jnp.abs(updated), axis=0, keepdims=True))
        turned[:, rows] = updated.astype(bf16).T
    is_gate = lax.broadcasted_iota(jnp.int32, peaks.shape, 1) < columns
    peak_ref[0:1, :] = jnp.full((1, 128), jnp.max(jnp.where(is_gate, peaks, 0.0)), f32)
    peak_ref[1:2, :] = jnp.full((1, 128), jnp.max(jnp.where(is_gate, 0.0, peaks)), f32)
    for first in range(0, partners, group):
        for k in range(group):
            joined[:, k * tokens : (k + 1) * tokens] = next_ref[first + k]
        both = matmul(turned[...], joined[...])
        gate, up = both[:columns], both[columns:]
        hidden = (gate * jax.nn.sigmoid(gate) * up).astype(bf16)
        for k in range(group):
            out_ref[first + k] = hidden[:, k * tokens : (k + 1) * tokens]


def rows_kernel(own_ref, *refs, partners, side):
    pieces = refs[:partners]
    sources, targets = refs[partners : partners + 3], refs[partners + 3 : partners + 6]
    blocks, gradient = refs[partners + 6 :]
    own = own_ref[0]
    columns = pieces[0].shape[1] // 2
    for distance in range(partners):
        blocks[own ^ distance] = pieces[distance][...].astype(f32)
    for k in range(partners):
        gradient[:, k * columns : (k + 1) * columns] = blocks[
            k, :, side * columns : (side + 1) * columns
        ]
    results = adam_update(sources[0][...], sources[1][...], sources[2][...], gradient[...])
    for kind in range(3):
        targets[kind][...] = results[kind]


def cost(flops, accessed):
    return pl.CostEstimate(flops=flops, bytes_accessed=accessed, transcendentals=0)


def smem_space():
    return pl.BlockSpec(memory_space=pltpu.SMEM)


def params(limit):
    return pltpu.CompilerParams(vmem_limit_bytes=limit * mib)


def in_vmem(count):
    return [pl.BlockSpec(memory_space=pltpu.VMEM)] * count


def run_prep(inputs, next_part, gain_row):
    tokens, features = inputs.shape
    turned = jax.ShapeDtypeStruct((features, tokens), bf16)
    return pl.pallas_call(
        prep_kernel,
        out_shape=(jax.ShapeDtypeStruct((tokens, features), bf16), turned, turned),
        compiler_params=params(4),
        name="prep",
    )(inputs, next_part, gain_row)


def run_first(own, scale_pair, upstream, inputs, normed, gain, down, pieces):
    tokens, features = upstream.shape
    hidden = down.shape[0]
    partners = len(pieces)
    flat = [part for pair in pieces for part in pair]
    return pl.pallas_call(
        functools.partial(first_kernel, partners=partners),
        out_shape=(
            jax.ShapeDtypeStruct((tokens, features), bf16),
            jax.ShapeDtypeStruct((tokens, hidden), bf16),
            jax.ShapeDtypeStruct((tokens, hidden), bf16),
            jax.ShapeDtypeStruct((features, hidden), bf16),
            jax.ShapeDtypeStruct((features, hidden), bf16),
        ),
        in_specs=[smem_space(), smem_space()] + in_vmem(5 + len(flat)),
        out_specs=tuple(in_vmem(5)),
        compiler_params=params(14),
        cost_estimate=cost(10 * tokens * features * hidden, 26 * features * hidden),
        name="first_stage",
    )(own, scale_pair, upstream, inputs, normed, gain, down, *flat)


def run_stage(upstream, inputs, gain, down, gate_full, up_full, gate_factor, up_factor):
    tokens, features = upstream.shape
    hidden = down.shape[0]
    return pl.pallas_call(
        stage_kernel,
        out_shape=jax.ShapeDtypeStruct((tokens, features), bf16),
        in_specs=in_vmem(8),
        out_specs=in_vmem(1)[0],
        compiler_params=params(10),
        cost_estimate=cost(6 * tokens * features * hidden, 8 * features * hidden),
        name="stage",
    )(upstream, inputs, gain, down, gate_full, up_full, gate_factor, up_factor)


def run_blocks(sources, partners):
    rows, hidden = sources[0].shape
    step = 16
    both = 2 * (hidden // partners)
    return pl.pallas_call(
        blocks_kernel,
        grid=(rows // step,),
        out_shape=tuple(jax.ShapeDtypeStruct((partners, rows, both), bf16) for _ in range(3)),
        in_specs=[pl.BlockSpec((step, hidden), lambda i: (i, 0))] * 6,
        out_specs=tuple(pl.BlockSpec((partners, step, both), lambda i: (0, i, 0)) for _ in range(3)),
        compiler_params=params(12),
        name="state_blocks",
    )(*sources)


def run_factors(own, scale_pair, normed_all, gate_full, up_full):
    partners, features, tokens = normed_all.shape
    columns = gate_full.shape[1] // partners
    shape = jax.ShapeDtypeStruct((partners * tokens, columns), bf16)
    return pl.pallas_call(
        factors_kernel,
        out_shape=(shape, shape),
        in_specs=[smem_space(), smem_space()] + in_vmem(3),
        out_specs=tuple(in_vmem(2)),
        scratch_shapes=[
            pltpu.VMEM((features, columns), bf16),
            pltpu.VMEM((features, columns), bf16),
            pltpu.VMEM((partners * tokens // 2, features), bf16),
        ],
        compiler_params=params(14),
        cost_estimate=cost(4 * partners * tokens * features * columns, 8 * features * columns),
        name="column_factors",
    )(own, scale_pair, normed_all, gate_full, up_full)


def run_weights(own, down_cols, normed_all, factor_cols, pieces, distances, start=None):
    partners, features, tokens = normed_all.shape
    columns = down_cols.shape[0]
    count = len(distances)
    first = start is None
    if first:
        shapes = jax.ShapeDtypeStruct((features, 2 * columns), f32)
        starts = []
    else:
        block = jax.ShapeDtypeStruct((features // partners, 2 * columns), bf16)
        shapes = (jax.ShapeDtypeStruct((features, 2 * columns), bf16),) + (block,) * partners
        starts = [start]
    return pl.pallas_call(
        functools.partial(weight_kernel, distances=distances, first=first),
        out_shape=shapes,
        in_specs=[smem_space()] + in_vmem(4 + count + len(starts)),
        out_specs=in_vmem(1)[0] if first else tuple(in_vmem(1 + partners)),
        scratch_shapes=[
            pltpu.VMEM((count * tokens, features), bf16),
            pltpu.VMEM((features, count * tokens), bf16),
            pltpu.VMEM((features, 2 * columns), bf16),
        ],
        compiler_params=params(18),
        cost_estimate=cost(6 * count * tokens * features * columns, 12 * features * columns),
        name="column_gradients",
    )(own, down_cols, normed_all, *factor_cols, *pieces, *starts)


def run_next(gradient, state, next_all):
    partners, features, tokens = next_all.shape
    both = gradient.shape[1]
    return pl.pallas_call(
        next_kernel,
        out_shape=(
            jax.ShapeDtypeStruct((partners, both // 2, tokens), bf16),
            jax.ShapeDtypeStruct((8, 128), f32),
        ),
        in_specs=in_vmem(5),
        out_specs=tuple(in_vmem(2)),
        scratch_shapes=[
            pltpu.VMEM((both, features), bf16),
            pltpu.VMEM((features, partners * tokens // 2), bf16),
        ],
        compiler_params=params(18),
        cost_estimate=cost(2 * partners * tokens * features * both, 16 * features * both),
        name="next_columns",
    )(gradient, *state, next_all)


def run_rows(own, pieces, sources, side):
    partners = len(pieces)
    rows, hidden = sources[0].shape
    both = pieces[0].shape[1]
    step = 16
    row_spec = pl.BlockSpec((step, hidden), lambda i: (i, 0))
    return pl.pallas_call(
        functools.partial(rows_kernel, partners=partners, side=side),
        grid=(rows // step,),
        out_shape=tuple(jax.ShapeDtypeStruct((rows, hidden), f32) for _ in range(3)),
        in_specs=[smem_space()]
        + [pl.BlockSpec((step, both), lambda i: (i, 0))] * partners
        + [row_spec] * 3,
        out_specs=(row_spec,) * 3,
        scratch_shapes=[
            pltpu.VMEM((partners, step, both), f32),
            pltpu.VMEM((step, hidden), f32),
        ],
        compiler_params=params(8),
        name="row_update",
    )(own, *pieces, *sources)


def down_shift(value, sections):
    return lax.ppermute(value, "section", [(source, source - 1) for source in range(1, sections)])


def columns_plan(
    section_inputs,
    cotangent,
    norm_gain,
    quant_gate,
    quant_up,
    scales,
    down_proj,
    master_gate,
    master_up,
    moment_gate,
    moment_up,
    second_gate,
    second_up,
    next_inputs,
):
    gain_row = norm_gain[0]
    scale_pair = scales[0]
    down_local = down_proj[0]
    inputs = section_inputs[0]
    tok_rows, feature_count = inputs.shape
    own_rows, hidden_count = quant_gate.shape[1:]
    partners = lax.axis_size("dp")
    own_cols = hidden_count // partners
    sections = lax.axis_size("section")
    is_last = lax.axis_index("section") == sections - 1
    own_index = lax.axis_index("dp")
    own = own_index.astype(jnp.int32).reshape(1)
    barrier = lax.optimization_barrier

    near = [swap(part, distance) for distance in (2, 4, 1) for part in (quant_gate[0], quant_up[0])]
    normed, normed_turned, next_turned = run_prep(inputs, next_inputs[0], gain_row[None])
    gate_sources = (master_gate[0], moment_gate[0], second_gate[0])
    up_sources = (master_up[0], moment_up[0], second_up[0])
    state_blocks = run_blocks(
        [part for pair in zip(gate_sources, up_sources) for part in pair], partners
    )
    *near, normed, normed_turned, next_turned = barrier(
        (*near, normed, normed_turned, next_turned)
    )
    normed_all = lax.all_gather(normed_turned[None], "dp", axis=0, tiled=True)
    weight_pieces, state_blocks = spread_weights(quant_gate[0], quant_up[0], near, state_blocks)
    result, gate_factor, up_factor, gate_full, up_full = run_first(
        own, scale_pair, cotangent, inputs, normed, gain_row[None], down_local, weight_pieces
    )

    def next_stage(upstream):
        return run_stage(
            upstream, inputs, gain_row[None], down_local, gate_full, up_full, gate_factor, up_factor
        )

    state_cols = []
    down_cols = lax.dynamic_slice_in_dim(down_local, own_index * own_cols, own_cols, axis=0)
    for turn in range(sections - 1):
        if turn == sections - 2:
            result, normed_all, down_cols = barrier((result, normed_all, down_cols))
        incoming = down_shift(result, sections)
        if turn < 3:
            result, block = barrier((result, state_blocks[turn]))
            state_cols.append(exchange(block))
        if turn == 1:
            result, next_turned = barrier((result, next_turned))
            next_all = lax.all_gather(next_turned[None], "dp", axis=0, tiled=True)
        if turn == sections - 2:
            factor_cols = run_factors(own, scale_pair, normed_all, gate_full, up_full)
            incoming, factor_cols, state_cols[:2] = barrier(
                (incoming, factor_cols, state_cols[:2])
            )
        upstream = jnp.where(is_last, cotangent, incoming)
        if turn < sections - 2:
            result = next_stage(upstream)

    near = [swap(upstream, distance) for distance in (1, 2, 4)]
    result = next_stage(upstream)
    result, *near = barrier([result] + near)
    across_c, across_x, across_y = near
    on_first_core = own_index % 2 == 0
    diagonal = (swap_some(across_y, 2, 0), swap_some(across_x, 4, 1))
    beside = [swap(across_x, 1), swap(across_y, 1)]
    gradient = run_weights(
        own,
        down_cols,
        normed_all,
        factor_cols,
        [upstream, across_c, across_x, across_y],
        (0, 1, 2, 4),
    )
    across_d = jnp.where(on_first_core, *diagonal)
    gradient, across_d, *beside = barrier([gradient, across_d] + beside)
    gradient, *row_blocks = run_weights(
        own,
        down_cols,
        normed_all,
        factor_cols,
        beside + [across_d, swap(across_d, 1)],
        (3, 5, 6, 7),
        gradient,
    )
    row_pieces = row_blocks[:1] + [
        swap(row_blocks[distance], distance) for distance in range(1, partners)
    ]
    state = [part.reshape(feature_count, 2 * own_cols) for part in state_cols]
    token_blocks, peaks = run_next(gradient, state, next_all)
    token_pieces = exchange(token_blocks)
    peaks, *row_pieces = barrier([jnp.maximum(peaks, swap(peaks, 1)), *row_pieces])
    new_gate, mom_gate, sec_gate = run_rows(own, row_pieces, gate_sources, 0)
    peaks, *row_pieces = barrier([jnp.maximum(peaks, swap(peaks, 2)), *row_pieces, new_gate])
    new_gate = row_pieces.pop()
    new_up, mom_up, sec_up = run_rows(own, row_pieces, up_sources, 1)
    peaks = jnp.maximum(peaks, swap(peaks, 4))
    new_scales = peaks[:2, 0] + scale_eps
    next_hidden = token_pieces.reshape(hidden_count, tok_rows).T
    updated = (new_gate, new_up, mom_gate, mom_up, sec_gate, sec_up)
    return (
        result[None],
        *(part[None] for part in updated),
        new_scales[None, :],
        next_hidden[None],
    )


def plain_plan(
    section_inputs,
    cotangent,
    norm_gain,
    quant_gate,
    quant_up,
    scales,
    down_proj,
    master_gate,
    master_up,
    moment_gate,
    moment_up,
    second_gate,
    second_up,
    next_inputs,
):
    gain_row = norm_gain[0]
    scale_pair = scales[0]
    down_local = down_proj[0]
    hidden_count = quant_gate.shape[2]
    sections = lax.axis_size("section")
    position = lax.axis_index("section")
    is_last = position == sections - 1
    both_full = lax.all_gather(
        jnp.concatenate([quant_gate[0], quant_up[0]], axis=1), "dp", axis=0, tiled=True
    )
    widened, inverse, normed = normalize(section_inputs[0], gain_row)
    both_pre = jnp.dot(normed, both_full, preferred_element_type=jnp.float32)
    gate_pre = both_pre[:, :hidden_count] * scale_pair[0]
    up_pre = both_pre[:, hidden_count:] * scale_pair[1]
    sigmoid = jax.nn.sigmoid(gate_pre)
    up_factor = gate_pre * sigmoid
    gate_factor = up_pre * (sigmoid * (1.0 + gate_pre * (1.0 - sigmoid)))
    cubed = inverse * inverse * inverse

    def stage(upstream):
        hidden_grad = transposed(upstream, down_local)
        gate_grad = (hidden_grad * gate_factor).astype(jnp.bfloat16)
        up_grad = (hidden_grad * up_factor).astype(jnp.bfloat16)
        normed_grad = (
            transposed(gate_grad, both_full[:, :hidden_count]) * scale_pair[0]
            + transposed(up_grad, both_full[:, hidden_count:]) * scale_pair[1]
        )
        gained = gain_row * normed_grad
        mean_term = jnp.mean(widened * gained, axis=-1, keepdims=True)
        result = upstream.astype(jnp.float32) + inverse * gained - widened * cubed * mean_term
        return (result.astype(jnp.bfloat16), gate_grad, up_grad)

    upstream = cotangent
    for turn in range(sections):
        result, gate_grad, up_grad = stage(upstream)
        if turn < sections - 1:
            incoming = lax.ppermute(
                result, "section", [(source, source - 1) for source in range(1, sections)]
            )
            upstream = jnp.where(is_last, cotangent, incoming)

    grads_all = jnp.concatenate([gate_grad, up_grad], axis=1)
    summed = lax.psum_scatter(
        lax.dot_general(
            normed, grads_all, (((0,), (0,)), ((), ())), preferred_element_type=jnp.float32
        ).astype(jnp.bfloat16),
        "dp",
        scatter_dimension=0,
        tiled=True,
    ).astype(jnp.float32)
    new_gate, mom_gate, sec_gate = adam_update(
        master_gate[0], moment_gate[0], second_gate[0], summed[:, :hidden_count]
    )
    new_up, mom_up, sec_up = adam_update(
        master_up[0], moment_up[0], second_up[0], summed[:, hidden_count:]
    )
    peaks = jnp.stack([jnp.max(jnp.abs(new_gate)), jnp.max(jnp.abs(new_up))])
    new_scales = ring_max(peaks, "dp") + scale_eps
    unused_one, unused_two, next_normed = normalize(next_inputs[0], gain_row)
    stacked = jnp.concatenate([new_gate, new_up], axis=1).astype(jnp.bfloat16)
    both_next = jnp.dot(
        next_normed,
        lax.all_gather(stacked, "dp", axis=0, tiled=True),
        preferred_element_type=jnp.float32,
    )
    next_hidden = (
        jax.nn.silu(both_next[:, :hidden_count]) * both_next[:, hidden_count:]
    ).astype(jnp.bfloat16)
    return (
        result[None],
        new_gate[None],
        new_up[None],
        mom_gate[None],
        mom_up[None],
        sec_gate[None],
        sec_up[None],
        new_scales[None, :],
        next_hidden[None],
    )


def solution(mesh):
    placed = (
        P("section", "dp", None),
        P("dp", None),
        P("section", None),
        P("section", "dp", None),
        P("section", "dp", None),
        P("section", None),
        P("section", None, None),
        P("section", "dp", None),
        P("section", "dp", None),
        P("section", "dp", None),
        P("section", "dp", None),
        P("section", "dp", None),
        P("section", "dp", None),
        P("section", "dp", None),
    )
    fits = mesh.shape["dp"] == 8 and mesh.shape["section"] >= 4
    return jax.shard_map(
        columns_plan if fits else plain_plan,
        mesh=mesh,
        in_specs=placed,
        out_specs=(
            P("section", "dp", None),
            P("section", "dp", None),
            P("section", "dp", None),
            P("section", "dp", None),
            P("section", "dp", None),
            P("section", "dp", None),
            P("section", "dp", None),
            P("section", None),
            P("section", "dp", None),
        ),
        check_vma=False,
    )
```

```python
import functools

import jax
import jax.numpy as jnp
from jax import lax
from jax.experimental import pallas as pl
from jax.experimental.pallas import tpu as pltpu
from jax.sharding import PartitionSpec as P

beta_one = 0.9
beta_two = 0.95
learn_rate = 0.002
decay_rate = 0.1
adam_steps = 100.0
norm_eps = 1e-06
adam_eps = 1e-08
scale_eps = 1e-06
mib = 1024 * 1024
bf16 = jnp.bfloat16
f32 = jnp.float32


def normalize(inputs, norm_gain):
    widened = inputs.astype(jnp.float32)
    inverse = lax.rsqrt(jnp.mean(widened * widened, axis=-1, keepdims=True) + norm_eps)
    return (widened, inverse, (widened * inverse * norm_gain).astype(jnp.bfloat16))


def matmul(first_op, second_op):
    return jnp.dot(first_op, second_op, preferred_element_type=jnp.float32)


def transposed(first_op, second_op):
    return lax.dot_general(
        first_op, second_op, (((1,), (1,)), ((), ())), preferred_element_type=jnp.float32
    )


def adam_update(master, moment_old, second_old, gradient):
    moment_one = beta_one * moment_old + (1.0 - beta_one) * gradient
    moment_two = beta_two * second_old + (1.0 - beta_two) * gradient * gradient
    unbiased_one = moment_one / (1.0 - beta_one**adam_steps)
    unbiased_two = moment_two / (1.0 - beta_two**adam_steps)
    updated = master - learn_rate * (
        unbiased_one / (jnp.sqrt(unbiased_two) + adam_eps) + decay_rate * master
    )
    return (updated, moment_one, moment_two)


def factors(gate_pre, up_pre):
    sigmoid = jax.nn.sigmoid(gate_pre)
    return (up_pre * (sigmoid * (1.0 + gate_pre * (1.0 - sigmoid))), gate_pre * sigmoid)


def swap(value, distance):
    pairs = [(source, source ^ distance) for source in range(lax.axis_size("dp"))]
    return lax.ppermute(value, "dp", pairs)


def swap_some(value, distance, core):
    pairs = [(k, k ^ distance) for k in range(lax.axis_size("dp")) if k % 2 == core]
    return lax.ppermute(value, "dp", pairs)


def spread_weights(gate, up):
    near = [swap(part, distance) for distance in (2, 4, 1) for part in (gate, up)]
    gate_x, up_x, gate_y, up_y, gate_c, up_c = near
    gate_d, up_d = swap(gate_y, 2), swap(up_x, 4)
    return [
        (gate, up),
        (gate_c, up_c),
        (gate_x, up_x),
        (swap(gate_x, 1), swap(up_x, 1)),
        (gate_y, up_y),
        (swap(gate_y, 1), swap(up_y, 1)),
        (gate_d, up_d),
        (swap(gate_d, 1), swap(up_d, 1)),
    ]


def spread_near(value):
    return (swap(value, 1), swap(value, 2), swap(value, 4))


def spread_far(value, near):
    across_c, across_x, across_y = near
    across_d = swap_some(across_y, 2, 0) + swap_some(across_x, 4, 1)
    return [
        value,
        across_c,
        across_x,
        swap(across_x, 1),
        across_y,
        swap(across_y, 1),
        across_d,
        swap(across_d, 1),
    ]


def ring_max(value, axis):
    count = lax.axis_size(axis)
    span = 1
    while span < count:
        pairs = [(source, (source + span) % count) for source in range(count)]
        value = jnp.maximum(value, lax.ppermute(value, axis, pairs))
        span *= 2
    return value


def column_chunks(total, width=512):
    return [(start, min(width, total - start)) for start in range(0, total, width)]


def finish_stage(upstream, normed_grad, widened, gain_row):
    inverse = lax.rsqrt(jnp.mean(widened * widened, axis=1, keepdims=True) + norm_eps)
    gained = gain_row * normed_grad
    mean_term = jnp.mean(widened * gained, axis=1, keepdims=True)
    cubed = inverse * inverse * inverse
    return (upstream.astype(f32) + inverse * gained - widened * cubed * mean_term).astype(bf16)


def prep_kernel(inputs_ref, next_ref, cot_ref, gain_ref, *refs, partners, sections):
    sources = refs[:6]
    normed_ref, turned_ref, cot_out = refs[6:9]
    targets = refs[9 : 9 + partners]
    held, blocks, sems = refs[9 + partners :]
    copies = [pltpu.make_async_copy(sources[k], held.at[k], sems.at[k]) for k in range(6)]
    for copy in copies:
        copy.start()
    features = inputs_ref.shape[1]
    gain_row = gain_ref[...]
    normed = normalize(inputs_ref[...], gain_row)[2]
    normed_ref[...] = normed
    turned_ref[:features] = normed.T
    turned_ref[features:] = normalize(next_ref[...], gain_row)[2].T
    last = lax.axis_index("section") == sections - 1
    cot_out[...] = cot_ref[...] * jnp.where(last, 1.0, 0.0).astype(bf16)
    columns = blocks.shape[3] // 2
    for place in range(6):
        copies[place].wait()
        kind, side = place // 2, place % 2
        narrow = held[place].astype(bf16)
        for k in range(partners):
            blocks[k, kind, :, side * columns : (side + 1) * columns] = narrow[
                :, k * columns : (k + 1) * columns
            ]
    own = lax.axis_index("dp")
    for distance in range(partners):
        targets[distance][...] = blocks[own ^ distance]


def first_kernel(
    scale_ref, upstream_ref, inputs_ref, normed_ref, gain_ref, down, *refs, partners
):
    pieces = refs[: 2 * partners]
    result_ref, gate_factor_ref, up_factor_ref, gate_full, up_full = refs[2 * partners :]
    rows = pieces[0].shape[0]
    own = lax.axis_index("dp")
    for index in range(2 * partners):
        place = pl.ds(pl.multiple_of((own ^ (index // 2)) * rows, 16), rows)
        full = gate_full if index % 2 == 0 else up_full
        full[place, :] = pieces[index][...]
    upstream = upstream_ref[...]
    normed = normed_ref[...]
    normed_grad = jnp.zeros(upstream.shape, f32)
    for start, width in column_chunks(gate_full.shape[1]):
        part = slice(start, start + width)
        gate_part, up_part = gate_full[:, part], up_full[:, part]
        gate_factor, up_factor = factors(
            matmul(normed, gate_part) * scale_ref[0], matmul(normed, up_part) * scale_ref[1]
        )
        gate_factor = (gate_factor * scale_ref[0]).astype(bf16)
        up_factor = (up_factor * scale_ref[1]).astype(bf16)
        gate_factor_ref[:, part] = gate_factor
        up_factor_ref[:, part] = up_factor
        hidden_grad = transposed(upstream, down[part, :])
        normed_grad += transposed((hidden_grad * gate_factor).astype(bf16), gate_part)
        normed_grad += transposed((hidden_grad * up_factor).astype(bf16), up_part)
    result_ref[...] = finish_stage(
        upstream, normed_grad, inputs_ref[...].astype(f32), gain_ref[...]
    )


def stage_kernel(
    upstream_ref, inputs_ref, gain_ref, down, gate_full, up_full, gate_factor, up_factor, *rest
):
    result_ref = rest[-1]
    upstream = upstream_ref[...]
    normed_grad = jnp.zeros(upstream.shape, f32)
    for start, width in column_chunks(gate_full.shape[1]):
        part = slice(start, start + width)
        hidden_grad = transposed(upstream, down[part, :])
        gate_grad = (hidden_grad * gate_factor[:, part]).astype(bf16)
        up_grad = (hidden_grad * up_factor[:, part]).astype(bf16)
        normed_grad += transposed(gate_grad, gate_full[:, part])
        normed_grad += transposed(up_grad, up_full[:, part])
    result_ref[...] = finish_stage(
        upstream, normed_grad, inputs_ref[...].astype(f32), gain_ref[...]
    )


def factors_kernel(scale_ref, gate_full, up_full, *refs, partners):
    pieces = refs[:partners]
    out_gate, out_up, gate, up, normed = refs[-5:]
    features, columns = gate.shape
    tokens = pieces[0].shape[1]
    group = normed.shape[0] // tokens
    own = lax.axis_index("dp")
    for k in range(partners):
        part = slice(k * columns, (k + 1) * columns)

        @pl.when(own == k)
        def pick():
            gate[...] = gate_full[:, part]
            up[...] = up_full[:, part]

    for first in range(0, partners, group):
        for k in range(group):
            normed[k * tokens : (k + 1) * tokens, :] = pieces[first + k][:features].T
        rows = slice(first * tokens, (first + group) * tokens)
        gate_factor, up_factor = factors(
            matmul(normed[...], gate[...]) * scale_ref[0],
            matmul(normed[...], up[...]) * scale_ref[1],
        )
        out_gate[rows, :] = gate_factor.astype(bf16)
        out_up[rows, :] = up_factor.astype(bf16)


def weight_kernel(down_ref, gate_factor, up_factor, *refs, distances, first):
    count = len(distances)
    pieces, turned = refs[:count], refs[count : 2 * count]
    if first:
        out_ref = refs[2 * count]
    else:
        start_ref = refs[2 * count]
        outs = refs[2 * count + 1 : -3]
    upstream, normed, total = refs[-3:]
    own = lax.axis_index("dp")
    tokens, features = pieces[0].shape
    columns = gate_factor.shape[1]
    factor_rows = []
    for place, distance in enumerate(distances):
        block = slice(place * tokens, (place + 1) * tokens)
        upstream[block, :] = pieces[place][...]
        normed[:, block] = turned[place][:features]
        factor_rows.append(slice(distance * tokens, (distance + 1) * tokens))
    down_cols = down_ref[pl.ds(pl.multiple_of(own * columns, 16), columns), :]
    hidden_grad = transposed(upstream[...], down_cols)
    gate_grad = hidden_grad * jnp.concatenate([gate_factor[rows, :] for rows in factor_rows], axis=0)
    up_grad = hidden_grad * jnp.concatenate([up_factor[rows, :] for rows in factor_rows], axis=0)
    grads = jnp.concatenate([gate_grad, up_grad], axis=1).astype(bf16)
    product = matmul(normed[...], grads)
    if first:
        out_ref[...] = product
        return
    total[...] = (start_ref[...] + product).astype(bf16)
    outs[0][...] = total[...]
    rows = outs[1].shape[0]
    for distance in range(len(outs) - 1):
        place = pl.ds(pl.multiple_of((own ^ distance) * rows, 16), rows)
        outs[1 + distance][...] = total[place, :]


def next_kernel(gradient_ref, *refs, partners):
    state, turned_parts = refs[:partners], refs[partners : 2 * partners]
    outs = refs[2 * partners : 3 * partners]
    peak_ref, updated_all, turned, joined = refs[3 * partners :]
    features = updated_all.shape[0]
    tokens = turned_parts[0].shape[1]
    columns = turned.shape[0] // 2
    group = joined.shape[1] // tokens
    own = lax.axis_index("dp")
    peaks = jnp.zeros((1, 2 * columns), f32)
    rows = state[0].shape[1]
    for distance in range(partners):
        place = pl.ds(pl.multiple_of((own ^ distance) * rows, 16), rows)
        updated, unused_one, unused_two = adam_update(
            state[distance][0].astype(f32),
            state[distance][1].astype(f32),
            state[distance][2].astype(f32),
            gradient_ref[place, :].astype(f32),
        )
        peaks = jnp.maximum(peaks, jnp.max(jnp.abs(updated), axis=0, keepdims=True))
        updated_all[place, :] = updated.astype(bf16)
    for start in range(0, features, 128):
        turned[:, start : start + 128] = updated_all[start : start + 128, :].T
    is_gate = lax.broadcasted_iota(jnp.int32, peaks.shape, 1) < columns
    peak_ref[0:1, :] = jnp.full((1, 128), jnp.max(jnp.where(is_gate, peaks, 0.0)), f32)
    peak_ref[1:8, :] = jnp.full((7, 128), jnp.max(jnp.where(is_gate, 0.0, peaks)), f32)
    for first in range(0, partners, group):
        for k in range(group):
            joined[:, k * tokens : (k + 1) * tokens] = turned_parts[first + k][features:]
        both = matmul(turned[...], joined[...])
        gate, up = both[:columns], both[columns:]
        hidden = (gate * jax.nn.sigmoid(gate) * up).astype(bf16)
        for k in range(group):
            outs[first + k][...] = hidden[:, k * tokens : (k + 1) * tokens]


def join_kernel(*refs, partners):
    pieces = refs[:partners]
    out_ref, held = refs[partners:]
    own = lax.axis_index("dp")
    columns = held.shape[1]
    for distance in range(partners):
        held[own ^ distance] = pieces[distance][...]
    for k in range(partners):
        out_ref[:, k * columns : (k + 1) * columns] = held[k].T


def rows_kernel(*refs, partners, side):
    pieces = refs[:partners]
    sources, targets = refs[partners : partners + 3], refs[partners + 3 : partners + 6]
    blocks, gradient = refs[partners + 6 :]
    own = lax.axis_index("dp")
    columns = pieces[0].shape[1] // 2
    for distance in range(partners):
        blocks[own ^ distance] = pieces[distance][...].astype(f32)
    for k in range(partners):
        gradient[:, k * columns : (k + 1) * columns] = blocks[
            k, :, side * columns : (side + 1) * columns
        ]
    results = adam_update(sources[0][...], sources[1][...], sources[2][...], gradient[...])
    for kind in range(3):
        targets[kind][...] = results[kind]


def cost(flops, accessed):
    return pl.CostEstimate(flops=flops, bytes_accessed=accessed, transcendentals=0)


def smem_space():
    return pl.BlockSpec(memory_space=pltpu.SMEM)


def params(limit):
    return pltpu.CompilerParams(vmem_limit_bytes=limit * mib)


def in_vmem(count):
    return [pl.BlockSpec(memory_space=pltpu.VMEM)] * count


def run_prep(inputs, next_part, cotangent, gain_row, sources, partners, sections):
    tokens, features = inputs.shape
    rows, hidden = sources[0].shape
    both = 2 * (hidden // partners)
    tall = jax.ShapeDtypeStruct((tokens, features), bf16)
    block = jax.ShapeDtypeStruct((3, rows, both), bf16)
    return pl.pallas_call(
        functools.partial(prep_kernel, partners=partners, sections=sections),
        out_shape=(tall, jax.ShapeDtypeStruct((2 * features, tokens), bf16), tall)
        + (block,) * partners,
        in_specs=in_vmem(4) + [pl.BlockSpec(memory_space=pl.ANY)] * 6,
        out_specs=tuple(in_vmem(3 + partners)),
        scratch_shapes=[
            pltpu.VMEM((6, rows, hidden), f32),
            pltpu.VMEM((partners, 3, rows, both), bf16),
            pltpu.SemaphoreType.DMA((6,)),
        ],
        compiler_params=params(20),
        name="prep",
    )(inputs, next_part, cotangent, gain_row, *sources)


def run_first(scale_pair, upstream, inputs, normed, gain, down, pieces):
    tokens, features = upstream.shape
    hidden = down.shape[0]
    partners = len(pieces)
    flat = [part for pair in pieces for part in pair]
    return pl.pallas_call(
        functools.partial(first_kernel, partners=partners),
        out_shape=(
            jax.ShapeDtypeStruct((tokens, features), bf16),
            jax.ShapeDtypeStruct((tokens, hidden), bf16),
            jax.ShapeDtypeStruct((tokens, hidden), bf16),
            jax.ShapeDtypeStruct((features, hidden), bf16),
            jax.ShapeDtypeStruct((features, hidden), bf16),
        ),
        in_specs=[smem_space()] + in_vmem(5 + len(flat)),
        out_specs=tuple(in_vmem(5)),
        compiler_params=params(14),
        cost_estimate=cost(10 * tokens * features * hidden, 26 * features * hidden),
        name="first_stage",
    )(scale_pair, upstream, inputs, normed, gain, down, *flat)


def run_stage(
    upstream, inputs, gain, down, gate_full, up_full, gate_factor, up_factor, arrived
):
    tokens, features = upstream.shape
    hidden = down.shape[0]
    return pl.pallas_call(
        stage_kernel,
        out_shape=jax.ShapeDtypeStruct((tokens, features), bf16),
        in_specs=in_vmem(8) + [pl.BlockSpec(memory_space=pl.ANY)] * len(arrived),
        out_specs=in_vmem(1)[0],
        compiler_params=params(10),
        cost_estimate=cost(6 * tokens * features * hidden, 8 * features * hidden),
        name="stage",
    )(upstream, inputs, gain, down, gate_full, up_full, gate_factor, up_factor, *arrived)


def run_factors(scale_pair, gate_full, up_full, pieces):
    partners = len(pieces)
    features, hidden = gate_full.shape
    tokens = pieces[0].shape[1]
    columns = hidden // partners
    shape = jax.ShapeDtypeStruct((partners * tokens, columns), bf16)
    return pl.pallas_call(
        functools.partial(factors_kernel, partners=partners),
        out_shape=(shape, shape),
        in_specs=[smem_space()] + in_vmem(2 + partners),
        out_specs=tuple(in_vmem(2)),
        scratch_shapes=[
            pltpu.VMEM((features, columns), bf16),
            pltpu.VMEM((features, columns), bf16),
            pltpu.VMEM((partners * tokens // 2, features), bf16),
        ],
        compiler_params=params(14),
        cost_estimate=cost(4 * partners * tokens * features * columns, 8 * features * columns),
        name="column_factors",
    )(scale_pair, gate_full, up_full, *pieces)


def run_weights(down, factor_cols, pieces, turned, distances, partners, start=None):
    tokens, features = pieces[0].shape
    columns = factor_cols[0].shape[1]
    count = len(distances)
    first = start is None
    if first:
        shapes = jax.ShapeDtypeStruct((features, 2 * columns), f32)
        starts = []
    else:
        block = jax.ShapeDtypeStruct((features // partners, 2 * columns), bf16)
        shapes = (jax.ShapeDtypeStruct((features, 2 * columns), bf16),) + (block,) * partners
        starts = [start]
    return pl.pallas_call(
        functools.partial(weight_kernel, distances=distances, first=first),
        out_shape=shapes,
        in_specs=in_vmem(3 + 2 * count + len(starts)),
        out_specs=in_vmem(1)[0] if first else tuple(in_vmem(1 + partners)),
        scratch_shapes=[
            pltpu.VMEM((count * tokens, features), bf16),
            pltpu.VMEM((features, count * tokens), bf16),
            pltpu.VMEM((features, 2 * columns), bf16),
        ],
        compiler_params=params(18),
        cost_estimate=cost(6 * count * tokens * features * columns, 12 * features * columns),
        name="column_gradients",
    )(down, *factor_cols, *pieces, *turned, *starts)


def run_next(gradient, state, turned):
    partners = len(state)
    features, both = gradient.shape
    tokens = turned[0].shape[1]
    block = jax.ShapeDtypeStruct((both // 2, tokens), bf16)
    return pl.pallas_call(
        functools.partial(next_kernel, partners=partners),
        out_shape=(block,) * partners + (jax.ShapeDtypeStruct((8, 128), f32),),
        in_specs=in_vmem(1 + 2 * partners),
        out_specs=tuple(in_vmem(1 + partners)),
        scratch_shapes=[
            pltpu.VMEM((features, both), bf16),
            pltpu.VMEM((both, features), bf16),
            pltpu.VMEM((features, partners * tokens // 2), bf16),
        ],
        compiler_params=params(18),
        cost_estimate=cost(2 * partners * tokens * features * both, 16 * features * both),
        name="next_columns",
    )(gradient, *state, *turned)


def run_join(pieces):
    partners = len(pieces)
    columns, tokens = pieces[0].shape
    return pl.pallas_call(
        functools.partial(join_kernel, partners=partners),
        out_shape=jax.ShapeDtypeStruct((tokens, partners * columns), bf16),
        in_specs=in_vmem(partners),
        out_specs=in_vmem(1)[0],
        scratch_shapes=[pltpu.VMEM((partners, columns, tokens), bf16)],
        compiler_params=params(8),
        name="next_join",
    )(*pieces)


def run_rows(pieces, sources, side):
    partners = len(pieces)
    rows, hidden = sources[0].shape
    both = pieces[0].shape[1]
    step = 16
    row_spec = pl.BlockSpec((step, hidden), lambda i: (i, 0))
    return pl.pallas_call(
        functools.partial(rows_kernel, partners=partners, side=side),
        grid=(rows // step,),
        out_shape=tuple(jax.ShapeDtypeStruct((rows, hidden), f32) for _ in range(3)),
        in_specs=[pl.BlockSpec((step, both), lambda i: (i, 0))] * partners
        + [row_spec] * 3,
        out_specs=(row_spec,) * 3,
        scratch_shapes=[
            pltpu.VMEM((partners, step, both), f32),
            pltpu.VMEM((step, hidden), f32),
        ],
        compiler_params=params(8),
        cost_estimate=cost(20 * rows * hidden, 96 * rows * hidden),
        name="row_update",
    )(*pieces, *sources)


def down_shift(value, sections):
    return lax.ppermute(value, "section", [(source, source - 1) for source in range(1, sections)])


def columns_plan(
    section_inputs,
    cotangent,
    norm_gain,
    quant_gate,
    quant_up,
    scales,
    down_proj,
    master_gate,
    master_up,
    moment_gate,
    moment_up,
    second_gate,
    second_up,
    next_inputs,
):
    gain_row = norm_gain[0]
    scale_pair = scales[0]
    down_local = down_proj[0]
    inputs = section_inputs[0]
    partners = lax.axis_size("dp")
    sections = lax.axis_size("section")
    gain = gain_row[None]
    gate_sources = (master_gate[0], moment_gate[0], second_gate[0])
    up_sources = (master_up[0], moment_up[0], second_up[0])

    weight_pieces = spread_weights(quant_gate[0], quant_up[0])
    normed, turned, cotangent_here, *state_blocks = run_prep(
        inputs,
        next_inputs[0],
        cotangent,
        gain,
        [part for pair in zip(gate_sources, up_sources) for part in pair],
        partners,
        sections,
    )
    result, gate_factor, up_factor, gate_full, up_full = run_first(
        scale_pair, cotangent, inputs, normed, gain, down_local, weight_pieces
    )

    def next_stage(upstream, arrived):
        return run_stage(
            upstream,
            inputs,
            gain,
            down_local,
            gate_full,
            up_full,
            gate_factor,
            up_factor,
            arrived,
        )

    turned_near = spread_near(turned)
    turned_all = spread_far(turned, turned_near)
    state = state_blocks[:1] + [swap(state_blocks[k], k) for k in range(1, partners)]
    held = [list(turned_near), turned_all[3:] + [state[2], state[4]]]
    for turn in range(sections - 1):
        upstream = cotangent_here + down_shift(result, sections)
        if turn < sections - 2:
            result = next_stage(upstream, held[turn] if turn < 2 else [])
    factor_cols = run_factors(scale_pair, gate_full, up_full, turned_all)
    near = spread_near(upstream)
    far = spread_far(upstream, near)
    result = next_stage(upstream, [state[k] for k in (1, 3, 5, 6, 7)])
    order = (0, 1, 2, 4)
    gradient = run_weights(
        down_local,
        factor_cols,
        [far[k] for k in order],
        [turned_all[k] for k in order],
        order,
        partners,
    )
    order = (3, 5, 6, 7)
    gradient, *row_blocks = run_weights(
        down_local,
        factor_cols,
        [far[k] for k in order],
        [turned_all[k] for k in order],
        order,
        partners,
        gradient,
    )
    row_pieces = row_blocks[:1] + [swap(row_blocks[k], k) for k in range(1, partners)]
    *token_blocks, peaks = run_next(gradient, state, turned_all)
    token_pieces = token_blocks[:1] + [swap(token_blocks[k], k) for k in range(1, partners)]
    for distance in (1, 2, 4):
        peaks = jnp.maximum(peaks, swap(peaks, distance))
    new_gate, mom_gate, sec_gate = run_rows(row_pieces, gate_sources, 0)
    new_up, mom_up, sec_up = run_rows(row_pieces, up_sources, 1)
    next_hidden = run_join(token_pieces)
    new_scales = peaks[:2, 0] + scale_eps
    updated = (new_gate, new_up, mom_gate, mom_up, sec_gate, sec_up)
    return (
        result[None],
        *(part[None] for part in updated),
        new_scales[None, :],
        next_hidden[None],
    )


def plain_plan(
    section_inputs,
    cotangent,
    norm_gain,
    quant_gate,
    quant_up,
    scales,
    down_proj,
    master_gate,
    master_up,
    moment_gate,
    moment_up,
    second_gate,
    second_up,
    next_inputs,
):
    gain_row = norm_gain[0]
    scale_pair = scales[0]
    down_local = down_proj[0]
    hidden_count = quant_gate.shape[2]
    sections = lax.axis_size("section")
    position = lax.axis_index("section")
    is_last = position == sections - 1
    both_full = lax.all_gather(
        jnp.concatenate([quant_gate[0], quant_up[0]], axis=1), "dp", axis=0, tiled=True
    )
    widened, inverse, normed = normalize(section_inputs[0], gain_row)
    both_pre = jnp.dot(normed, both_full, preferred_element_type=jnp.float32)
    gate_pre = both_pre[:, :hidden_count] * scale_pair[0]
    up_pre = both_pre[:, hidden_count:] * scale_pair[1]
    sigmoid = jax.nn.sigmoid(gate_pre)
    up_factor = gate_pre * sigmoid
    gate_factor = up_pre * (sigmoid * (1.0 + gate_pre * (1.0 - sigmoid)))
    cubed = inverse * inverse * inverse

    def stage(upstream):
        hidden_grad = transposed(upstream, down_local)
        gate_grad = (hidden_grad * gate_factor).astype(jnp.bfloat16)
        up_grad = (hidden_grad * up_factor).astype(jnp.bfloat16)
        normed_grad = (
            transposed(gate_grad, both_full[:, :hidden_count]) * scale_pair[0]
            + transposed(up_grad, both_full[:, hidden_count:]) * scale_pair[1]
        )
        gained = gain_row * normed_grad
        mean_term = jnp.mean(widened * gained, axis=-1, keepdims=True)
        result = upstream.astype(jnp.float32) + inverse * gained - widened * cubed * mean_term
        return (result.astype(jnp.bfloat16), gate_grad, up_grad)

    upstream = cotangent
    for turn in range(sections):
        result, gate_grad, up_grad = stage(upstream)
        if turn < sections - 1:
            incoming = lax.ppermute(
                result, "section", [(source, source - 1) for source in range(1, sections)]
            )
            upstream = jnp.where(is_last, cotangent, incoming)

    grads_all = jnp.concatenate([gate_grad, up_grad], axis=1)
    summed = lax.psum_scatter(
        lax.dot_general(
            normed, grads_all, (((0,), (0,)), ((), ())), preferred_element_type=jnp.float32
        ).astype(jnp.bfloat16),
        "dp",
        scatter_dimension=0,
        tiled=True,
    ).astype(jnp.float32)
    new_gate, mom_gate, sec_gate = adam_update(
        master_gate[0], moment_gate[0], second_gate[0], summed[:, :hidden_count]
    )
    new_up, mom_up, sec_up = adam_update(
        master_up[0], moment_up[0], second_up[0], summed[:, hidden_count:]
    )
    peaks = jnp.stack([jnp.max(jnp.abs(new_gate)), jnp.max(jnp.abs(new_up))])
    new_scales = ring_max(peaks, "dp") + scale_eps
    unused_one, unused_two, next_normed = normalize(next_inputs[0], gain_row)
    stacked = jnp.concatenate([new_gate, new_up], axis=1).astype(jnp.bfloat16)
    both_next = jnp.dot(
        next_normed,
        lax.all_gather(stacked, "dp", axis=0, tiled=True),
        preferred_element_type=jnp.float32,
    )
    next_hidden = (
        jax.nn.silu(both_next[:, :hidden_count]) * both_next[:, hidden_count:]
    ).astype(jnp.bfloat16)
    return (
        result[None],
        new_gate[None],
        new_up[None],
        mom_gate[None],
        mom_up[None],
        sec_gate[None],
        sec_up[None],
        new_scales[None, :],
        next_hidden[None],
    )


def solution(mesh):
    placed = (
        P("section", "dp", None),
        P("dp", None),
        P("section", None),
        P("section", "dp", None),
        P("section", "dp", None),
        P("section", None),
        P("section", None, None),
        P("section", "dp", None),
        P("section", "dp", None),
        P("section", "dp", None),
        P("section", "dp", None),
        P("section", "dp", None),
        P("section", "dp", None),
        P("section", "dp", None),
    )
    fits = mesh.shape["dp"] == 8 and mesh.shape["section"] >= 4
    return jax.shard_map(
        columns_plan if fits else plain_plan,
        mesh=mesh,
        in_specs=placed,
        out_specs=(
            P("section", "dp", None),
            P("section", "dp", None),
            P("section", "dp", None),
            P("section", "dp", None),
            P("section", "dp", None),
            P("section", "dp", None),
            P("section", "dp", None),
            P("section", None),
            P("section", "dp", None),
        ),
        check_vma=False,
    )
```

```python
import functools

import jax
import jax.numpy as jnp
from jax import lax
from jax.experimental import pallas as pl
from jax.experimental.pallas import tpu as pltpu
from jax.sharding import PartitionSpec as P

beta_one = 0.9
beta_two = 0.95
learn_rate = 0.002
decay_rate = 0.1
adam_steps = 100.0
norm_eps = 1e-06
adam_eps = 1e-08
scale_eps = 1e-06
mib = 1024 * 1024
bf16 = jnp.bfloat16
f32 = jnp.float32


def normalize(inputs, norm_gain):
    widened = inputs.astype(jnp.float32)
    inverse = lax.rsqrt(jnp.mean(widened * widened, axis=-1, keepdims=True) + norm_eps)
    return (widened, inverse, (widened * inverse * norm_gain).astype(jnp.bfloat16))


def matmul(first_op, second_op):
    return jnp.dot(first_op, second_op, preferred_element_type=jnp.float32)


def transposed(first_op, second_op):
    return lax.dot_general(
        first_op, second_op, (((1,), (1,)), ((), ())), preferred_element_type=jnp.float32
    )


def adam_update(master, moment_old, second_old, gradient):
    moment_one = beta_one * moment_old + (1.0 - beta_one) * gradient
    moment_two = beta_two * second_old + (1.0 - beta_two) * gradient * gradient
    unbiased_one = moment_one / (1.0 - beta_one**adam_steps)
    unbiased_two = moment_two / (1.0 - beta_two**adam_steps)
    updated = master - learn_rate * (
        unbiased_one / (jnp.sqrt(unbiased_two) + adam_eps) + decay_rate * master
    )
    return (updated, moment_one, moment_two)


def factors(gate_pre, up_pre):
    sigmoid = jax.nn.sigmoid(gate_pre)
    return (up_pre * (sigmoid * (1.0 + gate_pre * (1.0 - sigmoid))), gate_pre * sigmoid)


def exchange(blocks):
    return lax.all_to_all(blocks, "dp", split_axis=0, concat_axis=0, tiled=True)


def swap(value, distance):
    pairs = [(source, source ^ distance) for source in range(lax.axis_size("dp"))]
    return lax.ppermute(value, "dp", pairs)


def swap_some(value, distance, core):
    pairs = [(k, k ^ distance) for k in range(lax.axis_size("dp")) if k % 2 == core]
    return lax.ppermute(value, "dp", pairs)


def spread_weights(gate, up):
    near = [swap(part, distance) for distance in (2, 4, 1) for part in (gate, up)]
    gate_x, up_x, gate_y, up_y, gate_c, up_c = near
    gate_d, up_d = swap(gate_y, 2), swap(up_x, 4)
    return [
        (gate, up),
        (gate_c, up_c),
        (gate_x, up_x),
        (swap(gate_x, 1), swap(up_x, 1)),
        (gate_y, up_y),
        (swap(gate_y, 1), swap(up_y, 1)),
        (gate_d, up_d),
        (swap(gate_d, 1), swap(up_d, 1)),
    ]


def spread_near(value):
    return (swap(value, 1), swap(value, 2), swap(value, 4))


def spread_far(value, near):
    across_c, across_x, across_y = near
    across_d = swap_some(across_y, 2, 0) + swap_some(across_x, 4, 1)
    return [
        value,
        across_c,
        across_x,
        swap(across_x, 1),
        across_y,
        swap(across_y, 1),
        across_d,
        swap(across_d, 1),
    ]


def ring_max(value, axis):
    count = lax.axis_size(axis)
    span = 1
    while span < count:
        pairs = [(source, (source + span) % count) for source in range(count)]
        value = jnp.maximum(value, lax.ppermute(value, axis, pairs))
        span *= 2
    return value


def column_chunks(total, width=512):
    return [(start, min(width, total - start)) for start in range(0, total, width)]


def finish_stage(upstream, normed_grad, widened, gain_row):
    inverse = lax.rsqrt(jnp.mean(widened * widened, axis=1, keepdims=True) + norm_eps)
    gained = gain_row * normed_grad
    mean_term = jnp.mean(widened * gained, axis=1, keepdims=True)
    cubed = inverse * inverse * inverse
    return (upstream.astype(f32) + inverse * gained - widened * cubed * mean_term).astype(bf16)


def turn_kernel(inputs_ref, next_ref, gain_ref, *rest):
    turned_ref = rest[-1]
    features = inputs_ref.shape[1]
    turned_ref[:features] = normalize(inputs_ref[...], gain_ref[...])[2].T
    turned_ref[features:] = normalize(next_ref[...], gain_ref[...])[2].T


def state_kernel(*refs, partners):
    sources, targets = refs[:6], refs[6 : 6 + partners]
    held, blocks, sems = refs[6 + partners :]
    copies = [pltpu.make_async_copy(sources[k], held.at[k], sems.at[k]) for k in range(6)]
    for copy in copies:
        copy.start()
    columns = blocks.shape[3] // 2
    for place in range(6):
        copies[place].wait()
        kind, side = place // 2, place % 2
        narrow = held[place].astype(bf16)
        for k in range(partners):
            blocks[k, kind, :, side * columns : (side + 1) * columns] = narrow[
                :, k * columns : (k + 1) * columns
            ]
    own = lax.axis_index("dp")
    for distance in range(partners):
        targets[distance][...] = blocks[own ^ distance]


def first_kernel(
    scale_ref, upstream_ref, inputs_ref, gain_ref, down, *refs, partners, sections
):
    pieces = refs[: 2 * partners]
    result_ref, cot_ref, gate_factor_ref, up_factor_ref, gate_full, up_full = refs[-6:]
    rows = pieces[0].shape[0]
    own = lax.axis_index("dp")
    for index in range(2 * partners):
        place = pl.ds(pl.multiple_of((own ^ (index // 2)) * rows, 16), rows)
        full = gate_full if index % 2 == 0 else up_full
        full[place, :] = pieces[index][...]
    upstream = upstream_ref[...]
    last = lax.axis_index("section") == sections - 1
    cot_ref[...] = upstream * jnp.where(last, 1.0, 0.0).astype(bf16)
    normed = normalize(inputs_ref[...], gain_ref[...])[2]
    normed_grad = jnp.zeros(upstream.shape, f32)
    for start, width in column_chunks(gate_full.shape[1]):
        part = slice(start, start + width)
        gate_part, up_part = gate_full[:, part], up_full[:, part]
        gate_factor, up_factor = factors(
            matmul(normed, gate_part) * scale_ref[0], matmul(normed, up_part) * scale_ref[1]
        )
        gate_factor = (gate_factor * scale_ref[0]).astype(bf16)
        up_factor = (up_factor * scale_ref[1]).astype(bf16)
        gate_factor_ref[:, part] = gate_factor
        up_factor_ref[:, part] = up_factor
        hidden_grad = transposed(upstream, down[part, :])
        normed_grad += transposed((hidden_grad * gate_factor).astype(bf16), gate_part)
        normed_grad += transposed((hidden_grad * up_factor).astype(bf16), up_part)
    result_ref[...] = finish_stage(
        upstream, normed_grad, inputs_ref[...].astype(f32), gain_ref[...]
    )


def stage_kernel(
    upstream_ref, inputs_ref, gain_ref, down, gate_full, up_full, gate_factor, up_factor, *rest
):
    result_ref = rest[-1]
    upstream = upstream_ref[...]
    normed_grad = jnp.zeros(upstream.shape, f32)
    for start, width in column_chunks(gate_full.shape[1]):
        part = slice(start, start + width)
        hidden_grad = transposed(upstream, down[part, :])
        gate_grad = (hidden_grad * gate_factor[:, part]).astype(bf16)
        up_grad = (hidden_grad * up_factor[:, part]).astype(bf16)
        normed_grad += transposed(gate_grad, gate_full[:, part])
        normed_grad += transposed(up_grad, up_full[:, part])
    result_ref[...] = finish_stage(
        upstream, normed_grad, inputs_ref[...].astype(f32), gain_ref[...]
    )


def factors_kernel(scale_ref, gate_full, up_full, *refs, partners):
    pieces = refs[:partners]
    out_gate, out_up, gate, up, normed, stack = refs[-6:]
    features, columns = gate.shape
    tokens = pieces[0].shape[1]
    group = normed.shape[0] // tokens
    own = lax.axis_index("dp")
    for k in range(partners):
        part = slice(k * columns, (k + 1) * columns)

        @pl.when(own == k)
        def pick():
            gate[...] = gate_full[:, part]
            up[...] = up_full[:, part]

    for k in range(partners):
        stack[k] = pieces[k][:features]

    def one_group(index, carry):
        for k in range(group):
            normed[k * tokens : (k + 1) * tokens, :] = stack[index * group + k].T
        rows = pl.ds(pl.multiple_of(index * (group * tokens), 16), group * tokens)
        gate_factor, up_factor = factors(
            matmul(normed[...], gate[...]) * scale_ref[0],
            matmul(normed[...], up[...]) * scale_ref[1],
        )
        out_gate[rows, :] = gate_factor.astype(bf16)
        out_up[rows, :] = up_factor.astype(bf16)
        return carry

    lax.fori_loop(0, partners // group, one_group, 0)


def weight_kernel(down_ref, gate_factor, up_factor, *refs, distances, first):
    count = len(distances)
    pieces, turned = refs[:count], refs[count : 2 * count]
    if first:
        out_ref = refs[-4]
    else:
        start_ref = refs[2 * count]
        outs = refs[2 * count + 1 : -3]
    upstream, normed, total = refs[-3:]
    own = lax.axis_index("dp")
    tokens, features = pieces[0].shape
    columns = gate_factor.shape[1]
    factor_rows = []
    for place, distance in enumerate(distances):
        block = slice(place * tokens, (place + 1) * tokens)
        upstream[block, :] = pieces[place][...]
        normed[:, block] = turned[place][:features]
        factor_rows.append(slice(distance * tokens, (distance + 1) * tokens))
    down_cols = down_ref[pl.ds(pl.multiple_of(own * columns, 16), columns), :]
    hidden_grad = transposed(upstream[...], down_cols)
    gate_grad = hidden_grad * jnp.concatenate([gate_factor[rows, :] for rows in factor_rows], axis=0)
    up_grad = hidden_grad * jnp.concatenate([up_factor[rows, :] for rows in factor_rows], axis=0)
    grads = jnp.concatenate([gate_grad, up_grad], axis=1).astype(bf16)
    product = matmul(normed[...], grads)
    if first:
        out_ref[...] = product
        return
    total[...] = (start_ref[...] + product).astype(bf16)
    outs[0][...] = total[...]
    rows = outs[1].shape[0]
    for distance in range(len(outs) - 1):
        place = pl.ds(pl.multiple_of((own ^ distance) * rows, 16), rows)
        outs[1 + distance][...] = total[place, :]


def next_kernel(gradient_ref, *refs, partners):
    state, turned_parts = refs[:partners], refs[partners : 2 * partners]
    out_ref, peak_ref, updated_all, turned, joined = refs[2 * partners :]
    features = updated_all.shape[0]
    tokens = turned_parts[0].shape[1]
    columns = turned.shape[0] // 2
    group = joined.shape[1] // tokens
    own = lax.axis_index("dp")
    peaks = jnp.zeros((1, 2 * columns), f32)
    rows = state[0].shape[1]
    for distance in range(partners):
        place = pl.ds(pl.multiple_of((own ^ distance) * rows, 16), rows)
        updated, unused_one, unused_two = adam_update(
            state[distance][0].astype(f32),
            state[distance][1].astype(f32),
            state[distance][2].astype(f32),
            gradient_ref[place, :].astype(f32),
        )
        peaks = jnp.maximum(peaks, jnp.max(jnp.abs(updated), axis=0, keepdims=True))
        updated_all[place, :] = updated.astype(bf16)
    for start in range(0, features, 128):
        turned[:, start : start + 128] = updated_all[start : start + 128, :].T
    is_gate = lax.broadcasted_iota(jnp.int32, peaks.shape, 1) < columns
    peak_ref[0:1, :] = jnp.full((1, 128), jnp.max(jnp.where(is_gate, peaks, 0.0)), f32)
    peak_ref[1:8, :] = jnp.full((7, 128), jnp.max(jnp.where(is_gate, 0.0, peaks)), f32)
    for first in range(0, partners, group):
        for k in range(group):
            joined[:, k * tokens : (k + 1) * tokens] = turned_parts[first + k][features:]
        both = matmul(turned[...], joined[...])
        gate, up = both[:columns], both[columns:]
        hidden = (gate * jax.nn.sigmoid(gate) * up).astype(bf16)
        for k in range(group):
            out_ref[own ^ (first + k)] = hidden[:, k * tokens : (k + 1) * tokens]


def rows_kernel(*refs, partners, side):
    pieces = refs[:partners]
    sources, peak_ref = refs[partners : partners + 3], refs[partners + 3]
    targets, peak_out = refs[partners + 4 : partners + 7], refs[partners + 7]
    blocks, gradient = refs[partners + 8 :]
    peak_out[...] = peak_ref[...]
    own = lax.axis_index("dp")
    columns = pieces[0].shape[1] // 2
    for distance in range(partners):
        blocks[own ^ distance] = pieces[distance][...].astype(f32)
    for k in range(partners):
        gradient[:, k * columns : (k + 1) * columns] = blocks[
            k, :, side * columns : (side + 1) * columns
        ]
    results = adam_update(sources[0][...], sources[1][...], sources[2][...], gradient[...])
    for kind in range(3):
        targets[kind][...] = results[kind]


def cost(flops, accessed):
    return pl.CostEstimate(flops=flops, bytes_accessed=accessed, transcendentals=0)


def smem_space():
    return pl.BlockSpec(memory_space=pltpu.SMEM)


def params(limit):
    return pltpu.CompilerParams(vmem_limit_bytes=limit * mib)


def whole(shape):
    return pl.BlockSpec(shape, lambda *unused: (0,) * len(shape))


def in_any(count):
    return [pl.BlockSpec(memory_space=pl.ANY)] * count


def in_vmem(count):
    return [pl.BlockSpec(memory_space=pltpu.VMEM)] * count


def run_turn(inputs, next_part, gain_row, arrived):
    tokens, features = inputs.shape
    return pl.pallas_call(
        turn_kernel,
        out_shape=jax.ShapeDtypeStruct((2 * features, tokens), bf16),
        in_specs=in_vmem(3) + in_any(len(arrived)),
        out_specs=in_vmem(1)[0],
        compiler_params=params(6),
        name="turn",
    )(inputs, next_part, gain_row, *arrived)


def run_state(sources, partners):
    rows, hidden = sources[0].shape
    both = 2 * (hidden // partners)
    return pl.pallas_call(
        functools.partial(state_kernel, partners=partners),
        out_shape=(jax.ShapeDtypeStruct((3, rows, both), bf16),) * partners,
        in_specs=in_any(6),
        out_specs=tuple(in_vmem(partners)),
        scratch_shapes=[
            pltpu.VMEM((6, rows, hidden), f32),
            pltpu.VMEM((partners, 3, rows, both), bf16),
            pltpu.SemaphoreType.DMA((6,)),
        ],
        compiler_params=params(20),
        name="state_blocks",
    )(*sources)


def run_first(scale_pair, upstream, inputs, gain, down, pieces, arrived, sections):
    tokens, features = upstream.shape
    hidden = down.shape[0]
    partners = len(pieces)
    flat = [part for pair in pieces for part in pair]
    return pl.pallas_call(
        functools.partial(first_kernel, partners=partners, sections=sections),
        out_shape=(
            jax.ShapeDtypeStruct((tokens, features), bf16),
            jax.ShapeDtypeStruct((tokens, features), bf16),
            jax.ShapeDtypeStruct((tokens, hidden), bf16),
            jax.ShapeDtypeStruct((tokens, hidden), bf16),
            jax.ShapeDtypeStruct((features, hidden), bf16),
            jax.ShapeDtypeStruct((features, hidden), bf16),
        ),
        in_specs=[smem_space()] + in_vmem(4 + len(flat)) + in_any(len(arrived)),
        out_specs=tuple(in_vmem(6)),
        compiler_params=params(14),
        cost_estimate=cost(10 * tokens * features * hidden, 26 * features * hidden),
        name="first_stage",
    )(scale_pair, upstream, inputs, gain, down, *flat, *arrived)


def run_stage(
    upstream, inputs, gain, down, gate_full, up_full, gate_factor, up_factor, arrived
):
    tokens, features = upstream.shape
    hidden = down.shape[0]
    return pl.pallas_call(
        stage_kernel,
        out_shape=jax.ShapeDtypeStruct((tokens, features), bf16),
        in_specs=in_vmem(8) + in_any(len(arrived)),
        out_specs=in_vmem(1)[0],
        compiler_params=params(10),
        cost_estimate=cost(6 * tokens * features * hidden, 8 * features * hidden),
        name="stage",
    )(upstream, inputs, gain, down, gate_full, up_full, gate_factor, up_factor, *arrived)


def run_factors(scale_pair, gate_full, up_full, pieces, arrived):
    partners = len(pieces)
    features, hidden = gate_full.shape
    tokens = pieces[0].shape[1]
    columns = hidden // partners
    shape = jax.ShapeDtypeStruct((partners * tokens, columns), bf16)
    return pl.pallas_call(
        functools.partial(factors_kernel, partners=partners),
        out_shape=(shape, shape),
        in_specs=[smem_space()] + in_vmem(2 + partners) + in_any(len(arrived)),
        out_specs=tuple(in_vmem(2)),
        scratch_shapes=[
            pltpu.VMEM((features, columns), bf16),
            pltpu.VMEM((features, columns), bf16),
            pltpu.VMEM((partners * tokens // 2, features), bf16),
            pltpu.VMEM((partners, features, tokens), bf16),
        ],
        compiler_params=params(18),
        cost_estimate=cost(4 * partners * tokens * features * columns, 8 * features * columns),
        name="column_factors",
    )(scale_pair, gate_full, up_full, *pieces, *arrived)


def run_weights(down, factor_cols, pieces, turned, distances, partners, start=None, arrived=()):
    tokens, features = pieces[0].shape
    columns = factor_cols[0].shape[1]
    count = len(distances)
    first = start is None
    if first:
        shapes = jax.ShapeDtypeStruct((features, 2 * columns), f32)
        starts = []
    else:
        block = jax.ShapeDtypeStruct((features // partners, 2 * columns), bf16)
        shapes = (jax.ShapeDtypeStruct((features, 2 * columns), bf16),) + (block,) * partners
        starts = [start]
    return pl.pallas_call(
        functools.partial(weight_kernel, distances=distances, first=first),
        out_shape=shapes,
        in_specs=in_vmem(3 + 2 * count + len(starts)) + in_any(len(arrived)),
        out_specs=in_vmem(1)[0] if first else tuple(in_vmem(1 + partners)),
        scratch_shapes=[
            pltpu.VMEM((count * tokens, features), bf16),
            pltpu.VMEM((features, count * tokens), bf16),
            pltpu.VMEM((features, 2 * columns), bf16),
        ],
        compiler_params=params(18),
        cost_estimate=cost(6 * count * tokens * features * columns, 12 * features * columns),
        name="column_gradients",
    )(down, *factor_cols, *pieces, *turned, *starts, *arrived)


def run_next(gradient, state, turned):
    partners = len(state)
    features, both = gradient.shape
    tokens = turned[0].shape[1]
    return pl.pallas_call(
        functools.partial(next_kernel, partners=partners),
        out_shape=(
            jax.ShapeDtypeStruct((partners, both // 2, tokens), bf16),
            jax.ShapeDtypeStruct((8, 128), f32),
        ),
        in_specs=in_vmem(1 + 2 * partners),
        out_specs=tuple(in_vmem(2)),
        scratch_shapes=[
            pltpu.VMEM((features, both), bf16),
            pltpu.VMEM((both, features), bf16),
            pltpu.VMEM((features, partners * tokens // 2), bf16),
        ],
        compiler_params=params(18),
        cost_estimate=cost(2 * partners * tokens * features * both, 16 * features * both),
        name="next_columns",
    )(gradient, *state, *turned)


def run_rows(pieces, sources, peaks, side):
    partners = len(pieces)
    rows, hidden = sources[0].shape
    both = pieces[0].shape[1]
    step = 16
    row_spec = pl.BlockSpec((step, hidden), lambda i: (i, 0))
    return pl.pallas_call(
        functools.partial(rows_kernel, partners=partners, side=side),
        grid=(rows // step,),
        out_shape=(jax.ShapeDtypeStruct((rows, hidden), f32),) * 3
        + (jax.ShapeDtypeStruct(peaks.shape, f32),),
        in_specs=[pl.BlockSpec((step, both), lambda i: (i, 0))] * partners
        + [row_spec] * 3
        + [whole(peaks.shape)],
        out_specs=(row_spec,) * 3 + (whole(peaks.shape),),
        scratch_shapes=[
            pltpu.VMEM((partners, step, both), f32),
            pltpu.VMEM((step, hidden), f32),
        ],
        compiler_params=params(8),
        cost_estimate=cost(20 * rows * hidden, 96 * rows * hidden),
        name="row_update",
    )(*pieces, *sources, peaks)


def down_shift(value, sections):
    return lax.ppermute(value, "section", [(source, source - 1) for source in range(1, sections)])


def columns_plan(
    section_inputs,
    cotangent,
    norm_gain,
    quant_gate,
    quant_up,
    scales,
    down_proj,
    master_gate,
    master_up,
    moment_gate,
    moment_up,
    second_gate,
    second_up,
    next_inputs,
):
    gain_row = norm_gain[0]
    scale_pair = scales[0]
    down_local = down_proj[0]
    inputs = section_inputs[0]
    partners = lax.axis_size("dp")
    sections = lax.axis_size("section")
    gain = gain_row[None]
    gate_sources = (master_gate[0], moment_gate[0], second_gate[0])
    up_sources = (master_up[0], moment_up[0], second_up[0])

    weight_pieces = spread_weights(quant_gate[0], quant_up[0])
    state_blocks = run_state(
        [part for pair in zip(gate_sources, up_sources) for part in pair], partners
    )
    turned = run_turn(inputs, next_inputs[0], gain, weight_pieces[6])
    result, cotangent_here, gate_factor, up_factor, gate_full, up_full = run_first(
        scale_pair, cotangent, inputs, gain, down_local, weight_pieces, [turned], sections
    )

    def next_stage(upstream, arrived):
        return run_stage(
            upstream,
            inputs,
            gain,
            down_local,
            gate_full,
            up_full,
            gate_factor,
            up_factor,
            arrived,
        )

    turned_near = spread_near(turned)
    turned_all = spread_far(turned, turned_near)
    state = list(state_blocks[:1]) + [swap(state_blocks[k], k) for k in range(1, partners)]
    held = [list(turned_near) + [state_blocks[0]], [turned_all[k] for k in (3, 5, 6, 7)] + [state[2], state[4]]]
    for turn in range(sections - 1):
        upstream = cotangent_here + down_shift(result, sections)
        if turn < sections - 2:
            result = next_stage(upstream, held[turn] if turn < 2 else [])
    factor_cols = run_factors(scale_pair, gate_full, up_full, turned_all, [state[3], state[5]])
    near = spread_near(upstream)
    far = spread_far(upstream, near)
    result = next_stage(upstream, [factor_cols[0], state[1], state[6], state[7]])
    order = (0, 1, 2, 4)
    gradient = run_weights(
        down_local,
        factor_cols,
        [far[k] for k in order],
        [turned_all[k] for k in order],
        order,
        partners,
        arrived=[result],
    )
    order = (3, 5, 6, 7)
    gradient, *row_blocks = run_weights(
        down_local,
        factor_cols,
        [far[k] for k in order],
        [turned_all[k] for k in order],
        order,
        partners,
        gradient,
    )
    row_pieces = row_blocks[:1] + [swap(row_blocks[k], k) for k in range(1, partners)]
    token_blocks, peaks = run_next(gradient, state, turned_all)
    next_hidden = exchange(token_blocks).reshape(-1, token_blocks.shape[2]).T
    new_gate, mom_gate, sec_gate, peaks = run_rows(row_pieces, gate_sources, peaks, 0)
    peaks = jnp.maximum(peaks, swap(peaks, 1))
    new_up, mom_up, sec_up, peaks = run_rows(row_pieces, up_sources, peaks, 1)
    for distance in (2, 4):
        peaks = jnp.maximum(peaks, swap(peaks, distance))
    new_scales = peaks[:2, 0] + scale_eps
    updated = (new_gate, new_up, mom_gate, mom_up, sec_gate, sec_up)
    return (
        result[None],
        *(part[None] for part in updated),
        new_scales[None, :],
        next_hidden[None],
    )


def plain_plan(
    section_inputs,
    cotangent,
    norm_gain,
    quant_gate,
    quant_up,
    scales,
    down_proj,
    master_gate,
    master_up,
    moment_gate,
    moment_up,
    second_gate,
    second_up,
    next_inputs,
):
    gain_row = norm_gain[0]
    scale_pair = scales[0]
    down_local = down_proj[0]
    hidden_count = quant_gate.shape[2]
    sections = lax.axis_size("section")
    position = lax.axis_index("section")
    is_last = position == sections - 1
    both_full = lax.all_gather(
        jnp.concatenate([quant_gate[0], quant_up[0]], axis=1), "dp", axis=0, tiled=True
    )
    widened, inverse, normed = normalize(section_inputs[0], gain_row)
    both_pre = jnp.dot(normed, both_full, preferred_element_type=jnp.float32)
    gate_pre = both_pre[:, :hidden_count] * scale_pair[0]
    up_pre = both_pre[:, hidden_count:] * scale_pair[1]
    sigmoid = jax.nn.sigmoid(gate_pre)
    up_factor = gate_pre * sigmoid
    gate_factor = up_pre * (sigmoid * (1.0 + gate_pre * (1.0 - sigmoid)))
    cubed = inverse * inverse * inverse

    def stage(upstream):
        hidden_grad = transposed(upstream, down_local)
        gate_grad = (hidden_grad * gate_factor).astype(jnp.bfloat16)
        up_grad = (hidden_grad * up_factor).astype(jnp.bfloat16)
        normed_grad = (
            transposed(gate_grad, both_full[:, :hidden_count]) * scale_pair[0]
            + transposed(up_grad, both_full[:, hidden_count:]) * scale_pair[1]
        )
        gained = gain_row * normed_grad
        mean_term = jnp.mean(widened * gained, axis=-1, keepdims=True)
        result = upstream.astype(jnp.float32) + inverse * gained - widened * cubed * mean_term
        return (result.astype(jnp.bfloat16), gate_grad, up_grad)

    upstream = cotangent
    for turn in range(sections):
        result, gate_grad, up_grad = stage(upstream)
        if turn < sections - 1:
            incoming = lax.ppermute(
                result, "section", [(source, source - 1) for source in range(1, sections)]
            )
            upstream = jnp.where(is_last, cotangent, incoming)

    grads_all = jnp.concatenate([gate_grad, up_grad], axis=1)
    summed = lax.psum_scatter(
        lax.dot_general(
            normed, grads_all, (((0,), (0,)), ((), ())), preferred_element_type=jnp.float32
        ).astype(jnp.bfloat16),
        "dp",
        scatter_dimension=0,
        tiled=True,
    ).astype(jnp.float32)
    new_gate, mom_gate, sec_gate = adam_update(
        master_gate[0], moment_gate[0], second_gate[0], summed[:, :hidden_count]
    )
    new_up, mom_up, sec_up = adam_update(
        master_up[0], moment_up[0], second_up[0], summed[:, hidden_count:]
    )
    peaks = jnp.stack([jnp.max(jnp.abs(new_gate)), jnp.max(jnp.abs(new_up))])
    new_scales = ring_max(peaks, "dp") + scale_eps
    unused_one, unused_two, next_normed = normalize(next_inputs[0], gain_row)
    stacked = jnp.concatenate([new_gate, new_up], axis=1).astype(jnp.bfloat16)
    both_next = jnp.dot(
        next_normed,
        lax.all_gather(stacked, "dp", axis=0, tiled=True),
        preferred_element_type=jnp.float32,
    )
    next_hidden = (
        jax.nn.silu(both_next[:, :hidden_count]) * both_next[:, hidden_count:]
    ).astype(jnp.bfloat16)
    return (
        result[None],
        new_gate[None],
        new_up[None],
        mom_gate[None],
        mom_up[None],
        sec_gate[None],
        sec_up[None],
        new_scales[None, :],
        next_hidden[None],
    )


def solution(mesh):
    placed = (
        P("section", "dp", None),
        P("dp", None),
        P("section", None),
        P("section", "dp", None),
        P("section", "dp", None),
        P("section", None),
        P("section", None, None),
        P("section", "dp", None),
        P("section", "dp", None),
        P("section", "dp", None),
        P("section", "dp", None),
        P("section", "dp", None),
        P("section", "dp", None),
        P("section", "dp", None),
    )
    fits = mesh.shape["dp"] == 8 and mesh.shape["section"] >= 4
    return jax.shard_map(
        columns_plan if fits else plain_plan,
        mesh=mesh,
        in_specs=placed,
        out_specs=(
            P("section", "dp", None),
            P("section", "dp", None),
            P("section", "dp", None),
            P("section", "dp", None),
            P("section", "dp", None),
            P("section", "dp", None),
            P("section", "dp", None),
            P("section", None),
            P("section", "dp", None),
        ),
        check_vma=False,
    )
```

```python
import functools

import jax
import jax.numpy as jnp
from jax import lax
from jax.experimental import pallas as pl
from jax.experimental.pallas import tpu as pltpu
from jax.sharding import PartitionSpec as P

beta_one = 0.9
beta_two = 0.95
learn_rate = 0.002
decay_rate = 0.1
adam_steps = 100.0
norm_eps = 1e-06
adam_eps = 1e-08
scale_eps = 1e-06
mib = 1024 * 1024
bf16 = jnp.bfloat16
f32 = jnp.float32


def normalize(inputs, norm_gain):
    widened = inputs.astype(jnp.float32)
    inverse = lax.rsqrt(jnp.mean(widened * widened, axis=-1, keepdims=True) + norm_eps)
    return (widened, inverse, (widened * inverse * norm_gain).astype(jnp.bfloat16))


def matmul(first_op, second_op):
    return jnp.dot(first_op, second_op, preferred_element_type=jnp.float32)


def transposed(first_op, second_op):
    return lax.dot_general(
        first_op, second_op, (((1,), (1,)), ((), ())), preferred_element_type=jnp.float32
    )


def adam_update(master, moment_old, second_old, gradient):
    moment_one = beta_one * moment_old + (1.0 - beta_one) * gradient
    moment_two = beta_two * second_old + (1.0 - beta_two) * gradient * gradient
    unbiased_one = moment_one / (1.0 - beta_one**adam_steps)
    unbiased_two = moment_two / (1.0 - beta_two**adam_steps)
    updated = master - learn_rate * (
        unbiased_one / (jnp.sqrt(unbiased_two) + adam_eps) + decay_rate * master
    )
    return (updated, moment_one, moment_two)


def factors(gate_pre, up_pre):
    sigmoid = jax.nn.sigmoid(gate_pre)
    return (up_pre * (sigmoid * (1.0 + gate_pre * (1.0 - sigmoid))), gate_pre * sigmoid)


def exchange(blocks):
    return lax.all_to_all(blocks, "dp", split_axis=0, concat_axis=0, tiled=True)


def swap(value, distance):
    pairs = [(source, source ^ distance) for source in range(lax.axis_size("dp"))]
    return lax.ppermute(value, "dp", pairs)


def swap_some(value, distance, core):
    pairs = [(k, k ^ distance) for k in range(lax.axis_size("dp")) if k % 2 == core]
    return lax.ppermute(value, "dp", pairs)


def spread_weights(gate, up):
    near = [swap(part, distance) for distance in (2, 4, 1) for part in (gate, up)]
    gate_x, up_x, gate_y, up_y, gate_c, up_c = near
    gate_d, up_d = swap(gate_y, 2), swap(up_x, 4)
    return [
        (gate, up),
        (gate_c, up_c),
        (gate_x, up_x),
        (swap(gate_x, 1), swap(up_x, 1)),
        (gate_y, up_y),
        (swap(gate_y, 1), swap(up_y, 1)),
        (gate_d, up_d),
        (swap(gate_d, 1), swap(up_d, 1)),
    ]


def spread_near(value):
    return (swap(value, 1), swap(value, 2), swap(value, 4))


def spread_far(value, near):
    across_c, across_x, across_y = near
    across_d = swap_some(across_y, 2, 0) + swap_some(across_x, 4, 1)
    return [
        value,
        across_c,
        across_x,
        swap(across_x, 1),
        across_y,
        swap(across_y, 1),
        across_d,
        swap(across_d, 1),
    ]


def ring_max(value, axis):
    count = lax.axis_size(axis)
    span = 1
    while span < count:
        pairs = [(source, (source + span) % count) for source in range(count)]
        value = jnp.maximum(value, lax.ppermute(value, axis, pairs))
        span *= 2
    return value


def column_chunks(total, width=512):
    return [(start, min(width, total - start)) for start in range(0, total, width)]


def finish_stage(upstream, normed_grad, widened, gain_row):
    inverse = lax.rsqrt(jnp.mean(widened * widened, axis=1, keepdims=True) + norm_eps)
    gained = gain_row * normed_grad
    mean_term = jnp.mean(widened * gained, axis=1, keepdims=True)
    cubed = inverse * inverse * inverse
    return (upstream.astype(f32) + inverse * gained - widened * cubed * mean_term).astype(bf16)


def turn_kernel(inputs_ref, next_ref, gain_ref, *rest):
    turned_ref = rest[-1]
    features = inputs_ref.shape[1]
    turned_ref[:features] = normalize(inputs_ref[...], gain_ref[...])[2].T
    turned_ref[features:] = normalize(next_ref[...], gain_ref[...])[2].T


def state_kernel(*refs):
    sources = refs[:6]
    blocks, held, sems = refs[-3:]
    copies = [pltpu.make_async_copy(sources[k], held.at[k], sems.at[k]) for k in range(6)]
    for copy in copies:
        copy.start()
    partners, columns = blocks.shape[0], blocks.shape[3] // 2
    for place in range(6):
        copies[place].wait()
        kind, side = place // 2, place % 2
        narrow = held[place].astype(bf16)
        for k in range(partners):
            blocks[k, kind, :, side * columns : (side + 1) * columns] = narrow[
                :, k * columns : (k + 1) * columns
            ]


def relay_kernel(first_ref, second_ref, *rest):
    rest[-2][...] = first_ref[...]
    rest[-1][...] = second_ref[...]


def first_kernel(
    scale_ref, upstream_ref, inputs_ref, gain_ref, down, *refs, partners, sections
):
    pieces = refs[: 2 * partners]
    result_ref, cot_ref, gate_factor_ref, up_factor_ref, gate_hbm, up_hbm = refs[-9:-3]
    gate_full, up_full, sems = refs[-3:]
    rows = pieces[0].shape[0]
    own = lax.axis_index("dp")
    for index in range(2 * partners):
        place = pl.ds(pl.multiple_of((own ^ (index // 2)) * rows, 16), rows)
        full = gate_full if index % 2 == 0 else up_full
        full[place, :] = pieces[index][...]
    stores = [
        pltpu.make_async_copy(gate_full, gate_hbm, sems.at[0]),
        pltpu.make_async_copy(up_full, up_hbm, sems.at[1]),
    ]
    for copy in stores:
        copy.start()
    upstream = upstream_ref[...]
    last = lax.axis_index("section") == sections - 1
    cot_ref[...] = upstream * jnp.where(last, 1.0, 0.0).astype(bf16)
    normed = normalize(inputs_ref[...], gain_ref[...])[2]
    normed_grad = jnp.zeros(upstream.shape, f32)
    for start, width in column_chunks(gate_full.shape[1]):
        part = slice(start, start + width)
        gate_part, up_part = gate_full[:, part], up_full[:, part]
        gate_factor, up_factor = factors(
            matmul(normed, gate_part) * scale_ref[0], matmul(normed, up_part) * scale_ref[1]
        )
        gate_factor = (gate_factor * scale_ref[0]).astype(bf16)
        up_factor = (up_factor * scale_ref[1]).astype(bf16)
        gate_factor_ref[:, part] = gate_factor
        up_factor_ref[:, part] = up_factor
        hidden_grad = transposed(upstream, down[part, :])
        normed_grad += transposed((hidden_grad * gate_factor).astype(bf16), gate_part)
        normed_grad += transposed((hidden_grad * up_factor).astype(bf16), up_part)
    result_ref[...] = finish_stage(
        upstream, normed_grad, inputs_ref[...].astype(f32), gain_ref[...]
    )
    for copy in stores:
        copy.wait()


def stage_kernel(
    upstream_ref, inputs_ref, gain_ref, down, gate_full, up_full, gate_factor, up_factor, *rest
):
    result_ref = rest[-1]
    upstream = upstream_ref[...]
    normed_grad = jnp.zeros(upstream.shape, f32)
    for start, width in column_chunks(gate_full.shape[1]):
        part = slice(start, start + width)
        hidden_grad = transposed(upstream, down[part, :])
        gate_grad = (hidden_grad * gate_factor[:, part]).astype(bf16)
        up_grad = (hidden_grad * up_factor[:, part]).astype(bf16)
        normed_grad += transposed(gate_grad, gate_full[:, part])
        normed_grad += transposed(up_grad, up_full[:, part])
    result_ref[...] = finish_stage(
        upstream, normed_grad, inputs_ref[...].astype(f32), gain_ref[...]
    )


def factors_kernel(scale_ref, gate_full, up_full, cot_ref, *refs, partners):
    pieces = refs[:partners]
    out_gate, out_up, cot_out, gate, up, normed, stack = refs[-7:]
    cot_out[...] = cot_ref[...]
    features, columns = gate.shape
    tokens = pieces[0].shape[1]
    group = normed.shape[0] // tokens
    own = lax.axis_index("dp")
    for k in range(partners):
        part = slice(k * columns, (k + 1) * columns)

        @pl.when(own == k)
        def pick():
            gate[...] = gate_full[:, part]
            up[...] = up_full[:, part]

    for k in range(partners):
        stack[k] = pieces[k][:features]

    def one_group(index, carry):
        for k in range(group):
            normed[k * tokens : (k + 1) * tokens, :] = stack[index * group + k].T
        rows = pl.ds(pl.multiple_of(index * (group * tokens), 16), group * tokens)
        gate_factor, up_factor = factors(
            matmul(normed[...], gate[...]) * scale_ref[0],
            matmul(normed[...], up[...]) * scale_ref[1],
        )
        out_gate[rows, :] = gate_factor.astype(bf16)
        out_up[rows, :] = up_factor.astype(bf16)
        return carry

    lax.fori_loop(0, partners // group, one_group, 0)


def weight_kernel(down_ref, gate_factor, up_factor, *refs, distances, first):
    count = len(distances)
    pieces, turned = refs[:count], refs[count : 2 * count]
    if first:
        out_ref = refs[-4]
    else:
        start_ref = refs[2 * count]
        outs = refs[2 * count + 1 : -3]
    upstream, normed, total = refs[-3:]
    own = lax.axis_index("dp")
    tokens, features = pieces[0].shape
    columns = gate_factor.shape[1]
    factor_rows = []
    for place, distance in enumerate(distances):
        block = slice(place * tokens, (place + 1) * tokens)
        upstream[block, :] = pieces[place][...]
        normed[:, block] = turned[place][:features]
        factor_rows.append(slice(distance * tokens, (distance + 1) * tokens))
    down_cols = down_ref[pl.ds(pl.multiple_of(own * columns, 16), columns), :]
    hidden_grad = transposed(upstream[...], down_cols)
    gate_grad = hidden_grad * jnp.concatenate([gate_factor[rows, :] for rows in factor_rows], axis=0)
    up_grad = hidden_grad * jnp.concatenate([up_factor[rows, :] for rows in factor_rows], axis=0)
    grads = jnp.concatenate([gate_grad, up_grad], axis=1).astype(bf16)
    product = matmul(normed[...], grads)
    if first:
        out_ref[...] = product
        return
    total[...] = (start_ref[...] + product).astype(bf16)
    outs[0][...] = total[...]
    rows = outs[1].shape[0]
    for distance in range(len(outs) - 1):
        place = pl.ds(pl.multiple_of((own ^ distance) * rows, 16), rows)
        outs[1 + distance][...] = total[place, :]


def next_kernel(gradient_ref, *refs, partners):
    state, turned_parts = refs[0], refs[1 : 1 + partners]
    out_ref, peak_ref, updated_all, turned, joined = refs[1 + partners :]
    features = updated_all.shape[0]
    tokens = turned_parts[0].shape[1]
    columns = turned.shape[0] // 2
    group = joined.shape[1] // tokens
    own = lax.axis_index("dp")
    peaks = jnp.zeros((1, 2 * columns), f32)
    rows = state.shape[2]
    for k in range(partners):
        place = slice(k * rows, (k + 1) * rows)
        updated, unused_one, unused_two = adam_update(
            state[k, 0].astype(f32),
            state[k, 1].astype(f32),
            state[k, 2].astype(f32),
            gradient_ref[place, :].astype(f32),
        )
        peaks = jnp.maximum(peaks, jnp.max(jnp.abs(updated), axis=0, keepdims=True))
        updated_all[place, :] = updated.astype(bf16)
    for start in range(0, features, 128):
        turned[:, start : start + 128] = updated_all[start : start + 128, :].T
    is_gate = lax.broadcasted_iota(jnp.int32, peaks.shape, 1) < columns
    peak_ref[0:1, :] = jnp.full((1, 128), jnp.max(jnp.where(is_gate, peaks, 0.0)), f32)
    peak_ref[1:8, :] = jnp.full((7, 128), jnp.max(jnp.where(is_gate, 0.0, peaks)), f32)
    for first in range(0, partners, group):
        for k in range(group):
            joined[:, k * tokens : (k + 1) * tokens] = turned_parts[first + k][features:]
        both = matmul(turned[...], joined[...])
        gate, up = both[:columns], both[columns:]
        hidden = (gate * jax.nn.sigmoid(gate) * up).astype(bf16)
        for k in range(group):
            out_ref[own ^ (first + k)] = hidden[:, k * tokens : (k + 1) * tokens]


def rows_kernel(*refs, partners, side):
    pieces = refs[:partners]
    sources, peak_ref = refs[partners : partners + 3], refs[partners + 3]
    targets, peak_out = refs[partners + 4 : partners + 7], refs[partners + 7]
    blocks, gradient = refs[partners + 8 :]
    peak_out[...] = peak_ref[...]
    own = lax.axis_index("dp")
    columns = pieces[0].shape[1] // 2
    for distance in range(partners):
        blocks[own ^ distance] = pieces[distance][...].astype(f32)
    for k in range(partners):
        gradient[:, k * columns : (k + 1) * columns] = blocks[
            k, :, side * columns : (side + 1) * columns
        ]
    results = adam_update(sources[0][...], sources[1][...], sources[2][...], gradient[...])
    for kind in range(3):
        targets[kind][...] = results[kind]


def cost(flops, accessed):
    return pl.CostEstimate(flops=flops, bytes_accessed=accessed, transcendentals=0)


def smem_space():
    return pl.BlockSpec(memory_space=pltpu.SMEM)


def params(limit):
    return pltpu.CompilerParams(vmem_limit_bytes=limit * mib)


def whole(shape):
    return pl.BlockSpec(shape, lambda *unused: (0,) * len(shape))


def in_any(count):
    return [pl.BlockSpec(memory_space=pl.ANY)] * count


def in_vmem(count):
    return [pl.BlockSpec(memory_space=pltpu.VMEM)] * count


def run_turn(inputs, next_part, gain_row, arrived):
    tokens, features = inputs.shape
    return pl.pallas_call(
        turn_kernel,
        out_shape=jax.ShapeDtypeStruct((2 * features, tokens), bf16),
        in_specs=in_vmem(3) + in_any(len(arrived)),
        out_specs=in_vmem(1)[0],
        compiler_params=params(6),
        name="turn",
    )(inputs, next_part, gain_row, *arrived)


def run_state(sources, partners, arrived):
    rows, hidden = sources[0].shape
    both = 2 * (hidden // partners)
    return pl.pallas_call(
        state_kernel,
        out_shape=jax.ShapeDtypeStruct((partners, 3, rows, both), bf16),
        in_specs=in_any(6 + len(arrived)),
        out_specs=in_vmem(1)[0],
        scratch_shapes=[
            pltpu.VMEM((6, rows, hidden), f32),
            pltpu.SemaphoreType.DMA((6,)),
        ],
        compiler_params=params(20),
        name="state_blocks",
    )(*sources, *arrived)


def run_relay(first, second, arrived):
    return pl.pallas_call(
        relay_kernel,
        out_shape=(jax.ShapeDtypeStruct(first.shape, bf16),) * 2,
        in_specs=in_vmem(2) + in_any(len(arrived)),
        out_specs=tuple(in_vmem(2)),
        compiler_params=params(4),
        name="relay",
    )(first, second, *arrived)


def run_first(scale_pair, upstream, inputs, gain, down, pieces, arrived, sections):
    tokens, features = upstream.shape
    hidden = down.shape[0]
    partners = len(pieces)
    flat = [part for pair in pieces for part in pair]
    return pl.pallas_call(
        functools.partial(first_kernel, partners=partners, sections=sections),
        out_shape=(
            jax.ShapeDtypeStruct((tokens, features), bf16),
            jax.ShapeDtypeStruct((tokens, features), bf16),
            jax.ShapeDtypeStruct((tokens, hidden), bf16),
            jax.ShapeDtypeStruct((tokens, hidden), bf16),
            jax.ShapeDtypeStruct((features, hidden), bf16),
            jax.ShapeDtypeStruct((features, hidden), bf16),
        ),
        in_specs=[smem_space()] + in_vmem(4 + len(flat)) + in_any(len(arrived)),
        out_specs=tuple(in_vmem(4) + in_any(2)),
        scratch_shapes=[
            pltpu.VMEM((features, hidden), bf16),
            pltpu.VMEM((features, hidden), bf16),
            pltpu.SemaphoreType.DMA((2,)),
        ],
        compiler_params=params(24),
        cost_estimate=cost(10 * tokens * features * hidden, 26 * features * hidden),
        name="first_stage",
    )(scale_pair, upstream, inputs, gain, down, *flat, *arrived)


def run_stage(
    upstream, inputs, gain, down, gate_full, up_full, gate_factor, up_factor, arrived
):
    tokens, features = upstream.shape
    hidden = down.shape[0]
    return pl.pallas_call(
        stage_kernel,
        out_shape=jax.ShapeDtypeStruct((tokens, features), bf16),
        in_specs=in_vmem(8) + in_any(len(arrived)),
        out_specs=in_vmem(1)[0],
        compiler_params=params(10),
        cost_estimate=cost(6 * tokens * features * hidden, 8 * features * hidden),
        name="stage",
    )(upstream, inputs, gain, down, gate_full, up_full, gate_factor, up_factor, *arrived)


def run_factors(scale_pair, gate_full, up_full, cotangent, pieces):
    partners = len(pieces)
    features, hidden = gate_full.shape
    tokens = pieces[0].shape[1]
    columns = hidden // partners
    shape = jax.ShapeDtypeStruct((partners * tokens, columns), bf16)
    return pl.pallas_call(
        functools.partial(factors_kernel, partners=partners),
        out_shape=(shape, shape, jax.ShapeDtypeStruct(cotangent.shape, bf16)),
        in_specs=[smem_space()] + in_vmem(3 + partners),
        out_specs=tuple(in_vmem(3)),
        scratch_shapes=[
            pltpu.VMEM((features, columns), bf16),
            pltpu.VMEM((features, columns), bf16),
            pltpu.VMEM((partners * tokens // 2, features), bf16),
            pltpu.VMEM((partners, features, tokens), bf16),
        ],
        compiler_params=params(18),
        cost_estimate=cost(4 * partners * tokens * features * columns, 8 * features * columns),
        name="column_factors",
    )(scale_pair, gate_full, up_full, cotangent, *pieces)


def run_weights(down, factor_cols, pieces, turned, distances, partners, start=None, arrived=()):
    tokens, features = pieces[0].shape
    columns = factor_cols[0].shape[1]
    count = len(distances)
    first = start is None
    if first:
        shapes = jax.ShapeDtypeStruct((features, 2 * columns), f32)
        starts = []
    else:
        block = jax.ShapeDtypeStruct((features // partners, 2 * columns), bf16)
        shapes = (jax.ShapeDtypeStruct((features, 2 * columns), bf16),) + (block,) * partners
        starts = [start]
    return pl.pallas_call(
        functools.partial(weight_kernel, distances=distances, first=first),
        out_shape=shapes,
        in_specs=in_vmem(3 + 2 * count + len(starts)) + in_any(len(arrived)),
        out_specs=in_vmem(1)[0] if first else tuple(in_vmem(1 + partners)),
        scratch_shapes=[
            pltpu.VMEM((count * tokens, features), bf16),
            pltpu.VMEM((features, count * tokens), bf16),
            pltpu.VMEM((features, 2 * columns), bf16),
        ],
        compiler_params=params(18),
        cost_estimate=cost(6 * count * tokens * features * columns, 12 * features * columns),
        name="column_gradients",
    )(down, *factor_cols, *pieces, *turned, *starts, *arrived)


def run_next(gradient, state, turned):
    partners = len(turned)
    features, both = gradient.shape
    tokens = turned[0].shape[1]
    return pl.pallas_call(
        functools.partial(next_kernel, partners=partners),
        out_shape=(
            jax.ShapeDtypeStruct((partners, both // 2, tokens), bf16),
            jax.ShapeDtypeStruct((8, 128), f32),
        ),
        in_specs=in_vmem(2 + partners),
        out_specs=tuple(in_vmem(2)),
        scratch_shapes=[
            pltpu.VMEM((features, both), bf16),
            pltpu.VMEM((both, features), bf16),
            pltpu.VMEM((features, partners * tokens // 2), bf16),
        ],
        compiler_params=params(18),
        cost_estimate=cost(2 * partners * tokens * features * both, 16 * features * both),
        name="next_columns",
    )(gradient, state, *turned)


def run_rows(pieces, sources, peaks, side):
    partners = len(pieces)
    rows, hidden = sources[0].shape
    both = pieces[0].shape[1]
    step = 16
    row_spec = pl.BlockSpec((step, hidden), lambda i: (i, 0))
    return pl.pallas_call(
        functools.partial(rows_kernel, partners=partners, side=side),
        grid=(rows // step,),
        out_shape=(jax.ShapeDtypeStruct((rows, hidden), f32),) * 3
        + (jax.ShapeDtypeStruct(peaks.shape, f32),),
        in_specs=[pl.BlockSpec((step, both), lambda i: (i, 0))] * partners
        + [row_spec] * 3
        + [whole(peaks.shape)],
        out_specs=(row_spec,) * 3 + (whole(peaks.shape),),
        scratch_shapes=[
            pltpu.VMEM((partners, step, both), f32),
            pltpu.VMEM((step, hidden), f32),
        ],
        compiler_params=params(8),
        cost_estimate=cost(20 * rows * hidden, 2000 * rows * hidden),
        name="row_update",
    )(*pieces, *sources, peaks)


def down_shift(value, sections):
    return lax.ppermute(value, "section", [(source, source - 1) for source in range(1, sections)])


def columns_plan(
    section_inputs,
    cotangent,
    norm_gain,
    quant_gate,
    quant_up,
    scales,
    down_proj,
    master_gate,
    master_up,
    moment_gate,
    moment_up,
    second_gate,
    second_up,
    next_inputs,
):
    gain_row = norm_gain[0]
    scale_pair = scales[0]
    down_local = down_proj[0]
    inputs = section_inputs[0]
    partners = lax.axis_size("dp")
    sections = lax.axis_size("section")
    gain = gain_row[None]
    gate_sources = (master_gate[0], moment_gate[0], second_gate[0])
    up_sources = (master_up[0], moment_up[0], second_up[0])

    weight_pieces = spread_weights(quant_gate[0], quant_up[0])
    turned = run_turn(inputs, next_inputs[0], gain, weight_pieces[6])
    result, cotangent_here, gate_factor, up_factor, gate_full, up_full = run_first(
        scale_pair, cotangent, inputs, gain, down_local, weight_pieces, [turned], sections
    )

    def next_stage(upstream, arrived):
        return run_stage(
            upstream,
            inputs,
            gain,
            down_local,
            gate_full,
            up_full,
            gate_factor,
            up_factor,
            arrived,
        )

    across_c, across_x, across_y = spread_near(turned)
    state_blocks = run_state(
        [part for pair in zip(gate_sources, up_sources) for part in pair], partners, [result]
    )
    state = exchange(state_blocks)
    for turn in range(sections - 1):
        incoming = down_shift(result, sections)
        if turn == sections - 2:
            *factor_cols, cotangent_here = run_factors(
                scale_pair, gate_full, up_full, cotangent_here, turned_all
            )
        upstream = cotangent_here + incoming
        if turn < sections - 2:
            result = next_stage(upstream, [])
        if turn == 0:
            across_x, across_y = run_relay(across_x, across_y, [result])
            turned_all = spread_far(turned, (across_c, across_x, across_y))
    near = spread_near(upstream)
    far = spread_far(upstream, near)
    result = next_stage(upstream, [])
    order = (0, 1, 2, 4)
    gradient = run_weights(
        down_local,
        factor_cols,
        [far[k] for k in order],
        [turned_all[k] for k in order],
        order,
        partners,
        arrived=[result],
    )
    order = (3, 5, 6, 7)
    gradient, *row_blocks = run_weights(
        down_local,
        factor_cols,
        [far[k] for k in order],
        [turned_all[k] for k in order],
        order,
        partners,
        gradient,
    )
    row_pieces = row_blocks[:1] + [swap(row_blocks[k], k) for k in range(1, partners)]
    token_blocks, peaks = run_next(gradient, state, turned_all)
    next_hidden = exchange(token_blocks).reshape(-1, token_blocks.shape[2]).T
    new_gate, mom_gate, sec_gate, peaks = run_rows(row_pieces, gate_sources, peaks, 0)
    peaks = jnp.maximum(peaks, swap(peaks, 1))
    new_up, mom_up, sec_up, peaks = run_rows(row_pieces, up_sources, peaks, 1)
    for distance in (2, 4):
        peaks = jnp.maximum(peaks, swap(peaks, distance))
    new_scales = peaks[:2, 0] + scale_eps
    updated = (new_gate, new_up, mom_gate, mom_up, sec_gate, sec_up)
    return (
        result[None],
        *(part[None] for part in updated),
        new_scales[None, :],
        next_hidden[None],
    )


def plain_plan(
    section_inputs,
    cotangent,
    norm_gain,
    quant_gate,
    quant_up,
    scales,
    down_proj,
    master_gate,
    master_up,
    moment_gate,
    moment_up,
    second_gate,
    second_up,
    next_inputs,
):
    gain_row = norm_gain[0]
    scale_pair = scales[0]
    down_local = down_proj[0]
    hidden_count = quant_gate.shape[2]
    sections = lax.axis_size("section")
    position = lax.axis_index("section")
    is_last = position == sections - 1
    both_full = lax.all_gather(
        jnp.concatenate([quant_gate[0], quant_up[0]], axis=1), "dp", axis=0, tiled=True
    )
    widened, inverse, normed = normalize(section_inputs[0], gain_row)
    both_pre = jnp.dot(normed, both_full, preferred_element_type=jnp.float32)
    gate_pre = both_pre[:, :hidden_count] * scale_pair[0]
    up_pre = both_pre[:, hidden_count:] * scale_pair[1]
    sigmoid = jax.nn.sigmoid(gate_pre)
    up_factor = gate_pre * sigmoid
    gate_factor = up_pre * (sigmoid * (1.0 + gate_pre * (1.0 - sigmoid)))
    cubed = inverse * inverse * inverse

    def stage(upstream):
        hidden_grad = transposed(upstream, down_local)
        gate_grad = (hidden_grad * gate_factor).astype(jnp.bfloat16)
        up_grad = (hidden_grad * up_factor).astype(jnp.bfloat16)
        normed_grad = (
            transposed(gate_grad, both_full[:, :hidden_count]) * scale_pair[0]
            + transposed(up_grad, both_full[:, hidden_count:]) * scale_pair[1]
        )
        gained = gain_row * normed_grad
        mean_term = jnp.mean(widened * gained, axis=-1, keepdims=True)
        result = upstream.astype(jnp.float32) + inverse * gained - widened * cubed * mean_term
        return (result.astype(jnp.bfloat16), gate_grad, up_grad)

    upstream = cotangent
    for turn in range(sections):
        result, gate_grad, up_grad = stage(upstream)
        if turn < sections - 1:
            incoming = lax.ppermute(
                result, "section", [(source, source - 1) for source in range(1, sections)]
            )
            upstream = jnp.where(is_last, cotangent, incoming)

    grads_all = jnp.concatenate([gate_grad, up_grad], axis=1)
    summed = lax.psum_scatter(
        lax.dot_general(
            normed, grads_all, (((0,), (0,)), ((), ())), preferred_element_type=jnp.float32
        ).astype(jnp.bfloat16),
        "dp",
        scatter_dimension=0,
        tiled=True,
    ).astype(jnp.float32)
    new_gate, mom_gate, sec_gate = adam_update(
        master_gate[0], moment_gate[0], second_gate[0], summed[:, :hidden_count]
    )
    new_up, mom_up, sec_up = adam_update(
        master_up[0], moment_up[0], second_up[0], summed[:, hidden_count:]
    )
    peaks = jnp.stack([jnp.max(jnp.abs(new_gate)), jnp.max(jnp.abs(new_up))])
    new_scales = ring_max(peaks, "dp") + scale_eps
    unused_one, unused_two, next_normed = normalize(next_inputs[0], gain_row)
    stacked = jnp.concatenate([new_gate, new_up], axis=1).astype(jnp.bfloat16)
    both_next = jnp.dot(
        next_normed,
        lax.all_gather(stacked, "dp", axis=0, tiled=True),
        preferred_element_type=jnp.float32,
    )
    next_hidden = (
        jax.nn.silu(both_next[:, :hidden_count]) * both_next[:, hidden_count:]
    ).astype(jnp.bfloat16)
    return (
        result[None],
        new_gate[None],
        new_up[None],
        mom_gate[None],
        mom_up[None],
        sec_gate[None],
        sec_up[None],
        new_scales[None, :],
        next_hidden[None],
    )


def solution(mesh):
    placed = (
        P("section", "dp", None),
        P("dp", None),
        P("section", None),
        P("section", "dp", None),
        P("section", "dp", None),
        P("section", None),
        P("section", None, None),
        P("section", "dp", None),
        P("section", "dp", None),
        P("section", "dp", None),
        P("section", "dp", None),
        P("section", "dp", None),
        P("section", "dp", None),
        P("section", "dp", None),
    )
    fits = mesh.shape["dp"] == 8 and mesh.shape["section"] >= 4
    return jax.shard_map(
        columns_plan if fits else plain_plan,
        mesh=mesh,
        in_specs=placed,
        out_specs=(
            P("section", "dp", None),
            P("section", "dp", None),
            P("section", "dp", None),
            P("section", "dp", None),
            P("section", "dp", None),
            P("section", "dp", None),
            P("section", "dp", None),
            P("section", None),
            P("section", "dp", None),
        ),
        check_vma=False,
    )
```

```python
import functools

import jax
import jax.numpy as jnp
from jax import lax
from jax.experimental import pallas as pl
from jax.experimental.pallas import tpu as pltpu
from jax.sharding import PartitionSpec as P

beta_one = 0.9
beta_two = 0.95
learn_rate = 0.002
decay_rate = 0.1
adam_steps = 100.0
norm_eps = 1e-06
adam_eps = 1e-08
scale_eps = 1e-06
mib = 1024 * 1024
bf16 = jnp.bfloat16
f32 = jnp.float32


def normalize(inputs, norm_gain):
    widened = inputs.astype(jnp.float32)
    inverse = lax.rsqrt(jnp.mean(widened * widened, axis=-1, keepdims=True) + norm_eps)
    return (widened, inverse, (widened * inverse * norm_gain).astype(jnp.bfloat16))


def matmul(first_op, second_op):
    return jnp.dot(first_op, second_op, preferred_element_type=jnp.float32)


def transposed(first_op, second_op):
    return lax.dot_general(
        first_op, second_op, (((1,), (1,)), ((), ())), preferred_element_type=jnp.float32
    )


def adam_update(master, moment_old, second_old, gradient):
    moment_one = beta_one * moment_old + (1.0 - beta_one) * gradient
    moment_two = beta_two * second_old + (1.0 - beta_two) * gradient * gradient
    unbiased_one = moment_one / (1.0 - beta_one**adam_steps)
    unbiased_two = moment_two / (1.0 - beta_two**adam_steps)
    updated = master - learn_rate * (
        unbiased_one / (jnp.sqrt(unbiased_two) + adam_eps) + decay_rate * master
    )
    return (updated, moment_one, moment_two)


def factors(gate_pre, up_pre):
    sigmoid = jax.nn.sigmoid(gate_pre)
    return (up_pre * (sigmoid * (1.0 + gate_pre * (1.0 - sigmoid))), gate_pre * sigmoid)


def exchange(blocks):
    return [blocks[0]] + [swap(blocks[k], k) for k in range(1, len(blocks))]


def swap(value, distance):
    pairs = [(source, source ^ distance) for source in range(lax.axis_size("dp"))]
    return lax.ppermute(value, "dp", pairs)


def swap_some(value, distance, core):
    pairs = [(k, k ^ distance) for k in range(lax.axis_size("dp")) if k % 2 == core]
    return lax.ppermute(value, "dp", pairs)


def spread_weights(gate, up):
    near = [swap(part, distance) for distance in (2, 4, 1) for part in (gate, up)]
    gate_x, up_x, gate_y, up_y, gate_c, up_c = near
    gate_d, up_d = swap(gate_y, 2), swap(up_x, 4)
    return [
        (gate, up),
        (gate_c, up_c),
        (gate_x, up_x),
        (swap(gate_x, 1), swap(up_x, 1)),
        (gate_y, up_y),
        (swap(gate_y, 1), swap(up_y, 1)),
        (gate_d, up_d),
        (swap(gate_d, 1), swap(up_d, 1)),
    ]


def spread_near(value):
    return (swap(value, 1), swap(value, 2), swap(value, 4))


def spread_far(value, near, zero=None):
    across_c, across_x, across_y = near
    across_d = swap_some(across_y, 2, 0) + swap_some(across_x, 4, 1)
    if zero is not None:
        across_d = across_d + zero
    return [
        value,
        across_c,
        across_x,
        swap(across_x, 1),
        across_y,
        swap(across_y, 1),
        across_d,
        swap(across_d, 1),
    ]


def ring_max(value, axis):
    count = lax.axis_size(axis)
    span = 1
    while span < count:
        pairs = [(source, (source + span) % count) for source in range(count)]
        value = jnp.maximum(value, lax.ppermute(value, axis, pairs))
        span *= 2
    return value


def column_chunks(total, width=512):
    return [(start, min(width, total - start)) for start in range(0, total, width)]


def finish_stage(upstream, normed_grad, widened, gain_row):
    inverse = lax.rsqrt(jnp.mean(widened * widened, axis=1, keepdims=True) + norm_eps)
    gained = gain_row * normed_grad
    mean_term = jnp.mean(widened * gained, axis=1, keepdims=True)
    cubed = inverse * inverse * inverse
    return (upstream.astype(f32) + inverse * gained - widened * cubed * mean_term).astype(bf16)


def turn_kernel(inputs_ref, next_ref, gain_ref, *rest):
    turned_ref = rest[-1]
    features = inputs_ref.shape[1]
    turned_ref[:features] = normalize(inputs_ref[...], gain_ref[...])[2].T
    turned_ref[features:] = normalize(next_ref[...], gain_ref[...])[2].T


def first_kernel(
    scale_ref, upstream_ref, inputs_ref, gain_ref, down, *refs, partners, sections
):
    pieces = refs[: 2 * partners]
    result_ref, cot_ref, gate_factor_ref, up_factor_ref, gate_hbm, up_hbm = refs[-9:-3]
    gate_full, up_full, sems = refs[-3:]
    rows = pieces[0].shape[0]
    own = lax.axis_index("dp")
    for index in range(2 * partners):
        place = pl.ds(pl.multiple_of((own ^ (index // 2)) * rows, 16), rows)
        full = gate_full if index % 2 == 0 else up_full
        full[place, :] = pieces[index][...]
    stores = [
        pltpu.make_async_copy(gate_full, gate_hbm, sems.at[0]),
        pltpu.make_async_copy(up_full, up_hbm, sems.at[1]),
    ]
    for copy in stores:
        copy.start()
    upstream = upstream_ref[...]
    last = lax.axis_index("section") == sections - 1
    cot_ref[...] = upstream * jnp.where(last, 1.0, 0.0).astype(bf16)
    normed = normalize(inputs_ref[...], gain_ref[...])[2]
    normed_grad = jnp.zeros(upstream.shape, f32)
    for start, width in column_chunks(gate_full.shape[1]):
        part = slice(start, start + width)
        gate_part, up_part = gate_full[:, part], up_full[:, part]
        gate_factor, up_factor = factors(
            matmul(normed, gate_part) * scale_ref[0], matmul(normed, up_part) * scale_ref[1]
        )
        gate_factor = (gate_factor * scale_ref[0]).astype(bf16)
        up_factor = (up_factor * scale_ref[1]).astype(bf16)
        gate_factor_ref[:, part] = gate_factor
        up_factor_ref[:, part] = up_factor
        hidden_grad = transposed(upstream, down[part, :])
        normed_grad += transposed((hidden_grad * gate_factor).astype(bf16), gate_part)
        normed_grad += transposed((hidden_grad * up_factor).astype(bf16), up_part)
    result_ref[...] = finish_stage(
        upstream, normed_grad, inputs_ref[...].astype(f32), gain_ref[...]
    )
    for copy in stores:
        copy.wait()


def stage_kernel(
    upstream_ref, inputs_ref, gain_ref, down, gate_full, up_full, gate_factor, up_factor, *rest
):
    passed = len(rest) // 2
    result_ref = rest[passed]
    for place in range(passed):
        rest[passed + 1 + place][...] = rest[place][...]
    upstream = upstream_ref[...]
    normed_grad = jnp.zeros(upstream.shape, f32)
    for start, width in column_chunks(gate_full.shape[1]):
        part = slice(start, start + width)
        hidden_grad = transposed(upstream, down[part, :])
        gate_grad = (hidden_grad * gate_factor[:, part]).astype(bf16)
        up_grad = (hidden_grad * up_factor[:, part]).astype(bf16)
        normed_grad += transposed(gate_grad, gate_full[:, part])
        normed_grad += transposed(up_grad, up_full[:, part])
    result_ref[...] = finish_stage(
        upstream, normed_grad, inputs_ref[...].astype(f32), gain_ref[...]
    )


def factors_kernel(scale_ref, gate_full, up_full, cot_ref, *refs, partners):
    pieces = refs[:partners]
    out_gate, out_up, cot_out, gate, up, normed, stack = refs[-7:]
    cot_out[...] = cot_ref[...]
    features, columns = gate.shape
    tokens = pieces[0].shape[1]
    group = normed.shape[0] // tokens
    own = lax.axis_index("dp")
    for k in range(partners):
        part = slice(k * columns, (k + 1) * columns)

        @pl.when(own == k)
        def pick():
            gate[...] = gate_full[:, part]
            up[...] = up_full[:, part]

    for k in range(partners):
        stack[k] = pieces[k][:features]

    def one_group(index, carry):
        for k in range(group):
            normed[k * tokens : (k + 1) * tokens, :] = stack[index * group + k].T
        rows = pl.ds(pl.multiple_of(index * (group * tokens), 16), group * tokens)
        gate_factor, up_factor = factors(
            matmul(normed[...], gate[...]) * scale_ref[0],
            matmul(normed[...], up[...]) * scale_ref[1],
        )
        out_gate[rows, :] = gate_factor.astype(bf16)
        out_up[rows, :] = up_factor.astype(bf16)
        return carry

    lax.fori_loop(0, partners // group, one_group, 0)


def weight_kernel(down_ref, gate_factor, up_factor, *refs, distances, first):
    count = len(distances)
    pieces, turned = refs[:count], refs[count : 2 * count]
    if first:
        out_ref, zero_ref = refs[-5:-3]
        zero_ref[...] = jnp.zeros(zero_ref.shape, bf16)
    else:
        start_ref = refs[2 * count]
        outs = refs[2 * count + 1 : -3]
    upstream, normed, total = refs[-3:]
    own = lax.axis_index("dp")
    tokens, features = pieces[0].shape
    columns = gate_factor.shape[1]
    factor_rows = []
    for place, distance in enumerate(distances):
        block = slice(place * tokens, (place + 1) * tokens)
        upstream[block, :] = pieces[place][...]
        normed[:, block] = turned[place][:features]
        factor_rows.append(slice(distance * tokens, (distance + 1) * tokens))
    down_cols = down_ref[pl.ds(pl.multiple_of(own * columns, 16), columns), :]
    hidden_grad = transposed(upstream[...], down_cols)
    gate_grad = hidden_grad * jnp.concatenate([gate_factor[rows, :] for rows in factor_rows], axis=0)
    up_grad = hidden_grad * jnp.concatenate([up_factor[rows, :] for rows in factor_rows], axis=0)
    grads = jnp.concatenate([gate_grad, up_grad], axis=1).astype(bf16)
    product = matmul(normed[...], grads)
    if first:
        out_ref[...] = product
        return
    total[...] = (start_ref[...] + product).astype(bf16)
    rows = outs[0].shape[0]
    for distance in range(len(outs)):
        place = pl.ds(pl.multiple_of((own ^ distance) * rows, 16), rows)
        outs[distance][...] = total[place, :]


def next_kernel(*refs, partners):
    rows_in, turned_parts = refs[:partners], refs[partners : 2 * partners]
    outs = refs[-3 - partners : -3]
    weights, turned, joined = refs[-3:]
    features = weights.shape[0]
    tokens = turned_parts[0].shape[1]
    columns = turned.shape[0] // 2
    group = joined.shape[1] // tokens
    own = lax.axis_index("dp")
    rows = rows_in[0].shape[0]
    for distance in range(partners):
        place = pl.ds(pl.multiple_of((own ^ distance) * rows, 16), rows)
        weights[place, :] = rows_in[distance][...]
    for start in range(0, features, 128):
        turned[:, start : start + 128] = weights[start : start + 128, :].T
    for first in range(0, partners, group):
        for k in range(group):
            joined[:, k * tokens : (k + 1) * tokens] = turned_parts[first + k][features:]
        both = matmul(turned[...], joined[...])
        gate, up = both[:columns], both[columns:]
        hidden = (gate * jax.nn.sigmoid(gate) * up).astype(bf16)
        for k in range(group):
            outs[first + k][...] = hidden[:, k * tokens : (k + 1) * tokens]


def join_kernel(*refs, partners):
    pieces = refs[:partners]
    out_ref, held = refs[partners:]
    own = lax.axis_index("dp")
    columns = held.shape[1]
    for distance in range(partners):
        held[own ^ distance] = pieces[distance][...]
    for k in range(partners):
        out_ref[:, k * columns : (k + 1) * columns] = held[k].T


def rows_kernel(*refs, partners, unused_count):
    pieces, sources = refs[:partners], refs[partners : partners + 6]
    outs = refs[partners + 6 + unused_count :]
    targets, news, peak_ref = outs[:6], outs[6 : 6 + partners], outs[6 + partners]
    blocks, gradient = outs[7 + partners :]
    own = lax.axis_index("dp")
    columns = pieces[0].shape[1] // 2
    peaks = []
    for distance in range(partners):
        blocks[own ^ distance] = pieces[distance][...].astype(f32)
    for side in range(2):
        part = slice(side * columns, (side + 1) * columns)
        for k in range(partners):
            gradient[:, k * columns : (k + 1) * columns] = blocks[k, :, part]
        results = adam_update(
            sources[side][...], sources[2 + side][...], sources[4 + side][...], gradient[...]
        )
        for kind in range(3):
            targets[2 * kind + side][...] = results[kind]
        peaks.append(jnp.max(jnp.abs(results[0])))
        gradient[...] = results[0]
        for k in range(partners):
            blocks[k, :, part] = gradient[:, k * columns : (k + 1) * columns]
    for distance in range(partners):
        news[distance][...] = blocks[own ^ distance].astype(bf16)
    shape = (4, peak_ref.shape[1])
    both = jnp.concatenate([jnp.full(shape, peaks[0], f32), jnp.full(shape, peaks[1], f32)], axis=0)

    @pl.when(pl.program_id(0) == 0)
    def begin():
        peak_ref[...] = both

    @pl.when(pl.program_id(0) > 0)
    def further():
        peak_ref[...] = jnp.maximum(peak_ref[...], both)


def cost(flops, accessed):
    return pl.CostEstimate(flops=flops, bytes_accessed=accessed, transcendentals=0)


def smem_space():
    return pl.BlockSpec(memory_space=pltpu.SMEM)


def params(limit):
    return pltpu.CompilerParams(vmem_limit_bytes=limit * mib)


def whole(shape):
    return pl.BlockSpec(shape, lambda *unused: (0,) * len(shape))


def in_any(count):
    return [pl.BlockSpec(memory_space=pl.ANY)] * count


def in_vmem(count):
    return [pl.BlockSpec(memory_space=pltpu.VMEM)] * count


def run_turn(inputs, next_part, gain_row, arrived):
    tokens, features = inputs.shape
    return pl.pallas_call(
        turn_kernel,
        out_shape=jax.ShapeDtypeStruct((2 * features, tokens), bf16),
        in_specs=in_vmem(3) + in_any(len(arrived)),
        out_specs=in_vmem(1)[0],
        compiler_params=params(6),
        name="turn",
    )(inputs, next_part, gain_row, *arrived)


def run_first(scale_pair, upstream, inputs, gain, down, pieces, arrived, sections):
    tokens, features = upstream.shape
    hidden = down.shape[0]
    partners = len(pieces)
    flat = [part for pair in pieces for part in pair]
    return pl.pallas_call(
        functools.partial(first_kernel, partners=partners, sections=sections),
        out_shape=(
            jax.ShapeDtypeStruct((tokens, features), bf16),
            jax.ShapeDtypeStruct((tokens, features), bf16),
            jax.ShapeDtypeStruct((tokens, hidden), bf16),
            jax.ShapeDtypeStruct((tokens, hidden), bf16),
            jax.ShapeDtypeStruct((features, hidden), bf16),
            jax.ShapeDtypeStruct((features, hidden), bf16),
        ),
        in_specs=[smem_space()] + in_vmem(4 + len(flat)) + in_any(len(arrived)),
        out_specs=tuple(in_vmem(4) + in_any(2)),
        scratch_shapes=[
            pltpu.VMEM((features, hidden), bf16),
            pltpu.VMEM((features, hidden), bf16),
            pltpu.SemaphoreType.DMA((2,)),
        ],
        compiler_params=params(24),
        cost_estimate=cost(10 * tokens * features * hidden, 26 * features * hidden),
        name="first_stage",
    )(scale_pair, upstream, inputs, gain, down, *flat, *arrived)


def run_stage(
    upstream, inputs, gain, down, gate_full, up_full, gate_factor, up_factor, passed
):
    tokens, features = upstream.shape
    hidden = down.shape[0]
    return pl.pallas_call(
        stage_kernel,
        out_shape=(jax.ShapeDtypeStruct((tokens, features), bf16),)
        + tuple(jax.ShapeDtypeStruct(part.shape, bf16) for part in passed),
        in_specs=in_vmem(8 + len(passed)),
        out_specs=tuple(in_vmem(1 + len(passed))),
        compiler_params=params(10),
        cost_estimate=cost(6 * tokens * features * hidden, 8 * features * hidden),
        name="stage",
    )(upstream, inputs, gain, down, gate_full, up_full, gate_factor, up_factor, *passed)


def run_factors(scale_pair, gate_full, up_full, cotangent, pieces):
    partners = len(pieces)
    features, hidden = gate_full.shape
    tokens = pieces[0].shape[1]
    columns = hidden // partners
    shape = jax.ShapeDtypeStruct((partners * tokens, columns), bf16)
    return pl.pallas_call(
        functools.partial(factors_kernel, partners=partners),
        out_shape=(shape, shape, jax.ShapeDtypeStruct(cotangent.shape, bf16)),
        in_specs=[smem_space()] + in_vmem(3 + partners),
        out_specs=tuple(in_vmem(3)),
        scratch_shapes=[
            pltpu.VMEM((features, columns), bf16),
            pltpu.VMEM((features, columns), bf16),
            pltpu.VMEM((partners * tokens // 2, features), bf16),
            pltpu.VMEM((partners, features, tokens), bf16),
        ],
        compiler_params=params(18),
        cost_estimate=cost(4 * partners * tokens * features * columns, 8 * features * columns),
        name="column_factors",
    )(scale_pair, gate_full, up_full, cotangent, *pieces)


def run_weights(down, factor_cols, pieces, turned, distances, partners, start=None):
    tokens, features = pieces[0].shape
    columns = factor_cols[0].shape[1]
    count = len(distances)
    first = start is None
    if first:
        shapes = (
            jax.ShapeDtypeStruct((features, 2 * columns), f32),
            jax.ShapeDtypeStruct((tokens, features), bf16),
        )
        starts = []
    else:
        block = jax.ShapeDtypeStruct((features // partners, 2 * columns), bf16)
        shapes = (block,) * partners
        starts = [start]
    return pl.pallas_call(
        functools.partial(weight_kernel, distances=distances, first=first),
        out_shape=shapes,
        in_specs=in_vmem(3 + 2 * count + len(starts)),
        out_specs=tuple(in_vmem(len(shapes))),
        scratch_shapes=[
            pltpu.VMEM((count * tokens, features), bf16),
            pltpu.VMEM((features, count * tokens), bf16),
            pltpu.VMEM((features, 2 * columns), bf16),
        ],
        compiler_params=params(18),
        cost_estimate=cost(6 * count * tokens * features * columns, 12 * features * columns),
        name="column_gradients",
    )(down, *factor_cols, *pieces, *turned, *starts)


def run_next(rows_in, turned, arrived):
    partners = len(turned)
    rows, both = rows_in[0].shape
    tokens = turned[0].shape[1]
    features = partners * rows
    return pl.pallas_call(
        functools.partial(next_kernel, partners=partners),
        out_shape=(jax.ShapeDtypeStruct((both // 2, tokens), bf16),) * partners,
        in_specs=in_vmem(2 * partners) + in_any(len(arrived)),
        out_specs=tuple(in_vmem(partners)),
        scratch_shapes=[
            pltpu.VMEM((features, both), bf16),
            pltpu.VMEM((both, features), bf16),
            pltpu.VMEM((features, partners * tokens // 2), bf16),
        ],
        compiler_params=params(18),
        cost_estimate=cost(2 * partners * tokens * features * both, 16 * features * both),
        name="next_columns",
    )(*rows_in, *turned, *arrived)


def run_join(pieces):
    partners = len(pieces)
    columns, tokens = pieces[0].shape
    return pl.pallas_call(
        functools.partial(join_kernel, partners=partners),
        out_shape=jax.ShapeDtypeStruct((tokens, partners * columns), bf16),
        in_specs=in_vmem(partners),
        out_specs=in_vmem(1)[0],
        scratch_shapes=[pltpu.VMEM((partners, columns, tokens), bf16)],
        compiler_params=params(8),
        name="next_join",
    )(*pieces)


def run_rows(pieces, sources, arrived):
    partners = len(pieces)
    rows, hidden = sources[0].shape
    both = pieces[0].shape[1]
    step = 16
    row_spec = pl.BlockSpec((step, hidden), lambda i: (i, 0))
    block_spec = pl.BlockSpec((step, both), lambda i: (i, 0))
    return pl.pallas_call(
        functools.partial(rows_kernel, partners=partners, unused_count=len(arrived)),
        grid=(rows // step,),
        out_shape=(jax.ShapeDtypeStruct((rows, hidden), f32),) * 6
        + (jax.ShapeDtypeStruct((rows, both), bf16),) * partners
        + (jax.ShapeDtypeStruct((8, 128), f32),),
        in_specs=[block_spec] * partners + [row_spec] * 6 + in_any(len(arrived)),
        out_specs=(row_spec,) * 6 + (block_spec,) * partners + (whole((8, 128)),),
        scratch_shapes=[
            pltpu.VMEM((partners, step, both), f32),
            pltpu.VMEM((step, hidden), f32),
        ],
        compiler_params=params(10),
        cost_estimate=cost(40 * rows * hidden, 48 * rows * hidden),
        name="row_update",
    )(*pieces, *sources, *arrived)


def down_shift(value, sections):
    return lax.ppermute(value, "section", [(source, source - 1) for source in range(1, sections)])


def columns_plan(
    section_inputs,
    cotangent,
    norm_gain,
    quant_gate,
    quant_up,
    scales,
    down_proj,
    master_gate,
    master_up,
    moment_gate,
    moment_up,
    second_gate,
    second_up,
    next_inputs,
):
    gain_row = norm_gain[0]
    scale_pair = scales[0]
    down_local = down_proj[0]
    inputs = section_inputs[0]
    partners = lax.axis_size("dp")
    sections = lax.axis_size("section")
    gain = gain_row[None]
    sources = [
        part[0]
        for part in (master_gate, master_up, moment_gate, moment_up, second_gate, second_up)
    ]

    weight_pieces = spread_weights(quant_gate[0], quant_up[0])
    turned = run_turn(inputs, next_inputs[0], gain, weight_pieces[6])
    across_c, across_x, across_y = spread_near(turned)
    result, cotangent_here, gate_factor, up_factor, gate_full, up_full = run_first(
        scale_pair, cotangent, inputs, gain, down_local, weight_pieces, [turned], sections
    )

    def next_stage(upstream, passed):
        return run_stage(
            upstream, inputs, gain, down_local, gate_full, up_full, gate_factor, up_factor, passed
        )

    for turn in range(sections - 1):
        incoming = down_shift(result, sections)
        if turn == sections - 2:
            *factor_cols, cotangent_here = run_factors(
                scale_pair, gate_full, up_full, cotangent_here, turned_all
            )
        upstream = cotangent_here + incoming
        if turn == 0:
            result, across_x, across_y = next_stage(upstream, [across_x, across_y])
            turned_all = spread_far(turned, (across_c, across_x, across_y))
        elif turn < sections - 2:
            (result,) = next_stage(upstream, [])
    (result,) = next_stage(upstream, [])
    near = spread_near(upstream)
    order = (0, 1, 2, 4)
    gradient, zero = run_weights(
        down_local,
        factor_cols,
        [upstream, *near],
        [turned_all[k] for k in order],
        order,
        partners,
    )
    far = spread_far(upstream, near, zero)
    order = (3, 5, 6, 7)
    row_blocks = run_weights(
        down_local,
        factor_cols,
        [far[k] for k in order],
        [turned_all[k] for k in order],
        order,
        partners,
        gradient,
    )
    *updated, peaks = run_rows(exchange(row_blocks), sources, [result])
    updated, new_blocks = updated[:6], updated[6:]
    for distance in (1, 2, 4):
        peaks = jnp.maximum(peaks, swap(peaks, distance))
    new_scales = peaks[::4, 0] + scale_eps
    token_blocks = run_next(exchange(new_blocks), turned_all, [peaks])
    next_hidden = run_join(exchange(token_blocks))
    return (
        result[None],
        *(part[None] for part in updated),
        new_scales[None, :],
        next_hidden[None],
    )


def plain_plan(
    section_inputs,
    cotangent,
    norm_gain,
    quant_gate,
    quant_up,
    scales,
    down_proj,
    master_gate,
    master_up,
    moment_gate,
    moment_up,
    second_gate,
    second_up,
    next_inputs,
):
    gain_row = norm_gain[0]
    scale_pair = scales[0]
    down_local = down_proj[0]
    hidden_count = quant_gate.shape[2]
    sections = lax.axis_size("section")
    position = lax.axis_index("section")
    is_last = position == sections - 1
    both_full = lax.all_gather(
        jnp.concatenate([quant_gate[0], quant_up[0]], axis=1), "dp", axis=0, tiled=True
    )
    widened, inverse, normed = normalize(section_inputs[0], gain_row)
    both_pre = jnp.dot(normed, both_full, preferred_element_type=jnp.float32)
    gate_pre = both_pre[:, :hidden_count] * scale_pair[0]
    up_pre = both_pre[:, hidden_count:] * scale_pair[1]
    sigmoid = jax.nn.sigmoid(gate_pre)
    up_factor = gate_pre * sigmoid
    gate_factor = up_pre * (sigmoid * (1.0 + gate_pre * (1.0 - sigmoid)))
    cubed = inverse * inverse * inverse

    def stage(upstream):
        hidden_grad = transposed(upstream, down_local)
        gate_grad = (hidden_grad * gate_factor).astype(jnp.bfloat16)
        up_grad = (hidden_grad * up_factor).astype(jnp.bfloat16)
        normed_grad = (
            transposed(gate_grad, both_full[:, :hidden_count]) * scale_pair[0]
            + transposed(up_grad, both_full[:, hidden_count:]) * scale_pair[1]
        )
        gained = gain_row * normed_grad
        mean_term = jnp.mean(widened * gained, axis=-1, keepdims=True)
        result = upstream.astype(jnp.float32) + inverse * gained - widened * cubed * mean_term
        return (result.astype(jnp.bfloat16), gate_grad, up_grad)

    upstream = cotangent
    for turn in range(sections):
        result, gate_grad, up_grad = stage(upstream)
        if turn < sections - 1:
            incoming = lax.ppermute(
                result, "section", [(source, source - 1) for source in range(1, sections)]
            )
            upstream = jnp.where(is_last, cotangent, incoming)

    grads_all = jnp.concatenate([gate_grad, up_grad], axis=1)
    summed = lax.psum_scatter(
        lax.dot_general(
            normed, grads_all, (((0,), (0,)), ((), ())), preferred_element_type=jnp.float32
        ).astype(jnp.bfloat16),
        "dp",
        scatter_dimension=0,
        tiled=True,
    ).astype(jnp.float32)
    new_gate, mom_gate, sec_gate = adam_update(
        master_gate[0], moment_gate[0], second_gate[0], summed[:, :hidden_count]
    )
    new_up, mom_up, sec_up = adam_update(
        master_up[0], moment_up[0], second_up[0], summed[:, hidden_count:]
    )
    peaks = jnp.stack([jnp.max(jnp.abs(new_gate)), jnp.max(jnp.abs(new_up))])
    new_scales = ring_max(peaks, "dp") + scale_eps
    unused_one, unused_two, next_normed = normalize(next_inputs[0], gain_row)
    stacked = jnp.concatenate([new_gate, new_up], axis=1).astype(jnp.bfloat16)
    both_next = jnp.dot(
        next_normed,
        lax.all_gather(stacked, "dp", axis=0, tiled=True),
        preferred_element_type=jnp.float32,
    )
    next_hidden = (
        jax.nn.silu(both_next[:, :hidden_count]) * both_next[:, hidden_count:]
    ).astype(jnp.bfloat16)
    return (
        result[None],
        new_gate[None],
        new_up[None],
        mom_gate[None],
        mom_up[None],
        sec_gate[None],
        sec_up[None],
        new_scales[None, :],
        next_hidden[None],
    )


def solution(mesh):
    placed = (
        P("section", "dp", None),
        P("dp", None),
        P("section", None),
        P("section", "dp", None),
        P("section", "dp", None),
        P("section", None),
        P("section", None, None),
        P("section", "dp", None),
        P("section", "dp", None),
        P("section", "dp", None),
        P("section", "dp", None),
        P("section", "dp", None),
        P("section", "dp", None),
        P("section", "dp", None),
    )
    fits = mesh.shape["dp"] == 8 and mesh.shape["section"] >= 4
    return jax.shard_map(
        columns_plan if fits else plain_plan,
        mesh=mesh,
        in_specs=placed,
        out_specs=(
            P("section", "dp", None),
            P("section", "dp", None),
            P("section", "dp", None),
            P("section", "dp", None),
            P("section", "dp", None),
            P("section", "dp", None),
            P("section", "dp", None),
            P("section", None),
            P("section", "dp", None),
        ),
        check_vma=False,
    )
```

```python
import functools

import jax
import jax.numpy as jnp
from jax import lax
from jax.experimental import pallas as pl
from jax.experimental.pallas import tpu as pltpu
from jax.sharding import PartitionSpec as P

beta_one = 0.9
beta_two = 0.95
learn_rate = 0.002
decay_rate = 0.1
adam_steps = 100.0
norm_eps = 1e-06
adam_eps = 1e-08
scale_eps = 1e-06
mib = 1024 * 1024
bf16 = jnp.bfloat16
f32 = jnp.float32


def normalize(inputs, norm_gain):
    widened = inputs.astype(jnp.float32)
    inverse = lax.rsqrt(jnp.mean(widened * widened, axis=-1, keepdims=True) + norm_eps)
    return (widened, inverse, (widened * inverse * norm_gain).astype(jnp.bfloat16))


def matmul(first_op, second_op):
    return jnp.dot(first_op, second_op, preferred_element_type=jnp.float32)


def transposed(first_op, second_op):
    return lax.dot_general(
        first_op, second_op, (((1,), (1,)), ((), ())), preferred_element_type=jnp.float32
    )


def adam_update(master, moment_old, second_old, gradient):
    moment_one = beta_one * moment_old + (1.0 - beta_one) * gradient
    moment_two = beta_two * second_old + (1.0 - beta_two) * gradient * gradient
    unbiased_one = moment_one / (1.0 - beta_one**adam_steps)
    unbiased_two = moment_two / (1.0 - beta_two**adam_steps)
    updated = master - learn_rate * (
        unbiased_one / (jnp.sqrt(unbiased_two) + adam_eps) + decay_rate * master
    )
    return (updated, moment_one, moment_two)


def factors(gate_pre, up_pre):
    sigmoid = jax.nn.sigmoid(gate_pre)
    return (up_pre * (sigmoid * (1.0 + gate_pre * (1.0 - sigmoid))), gate_pre * sigmoid)


def exchange(blocks):
    got = {k: swap(blocks[k], k) for k in (6, 7, 2, 4, 3, 5, 1)}
    return [blocks[0]] + [got[k] for k in range(1, len(blocks))]


def swap(value, distance):
    pairs = [(source, source ^ distance) for source in range(lax.axis_size("dp"))]
    return lax.ppermute(value, "dp", pairs)


def swap_some(value, distance, core):
    pairs = [(k, k ^ distance) for k in range(lax.axis_size("dp")) if k % 2 == core]
    return lax.ppermute(value, "dp", pairs)


def spread_weights(gate, up):
    near = [swap(part, distance) for distance in (2, 4, 1) for part in (gate, up)]
    gate_x, up_x, gate_y, up_y, gate_c, up_c = near
    gate_d, up_d = swap(gate_y, 2), swap(up_x, 4)
    return [
        (gate, up),
        (gate_c, up_c),
        (gate_x, up_x),
        (swap(gate_x, 1), swap(up_x, 1)),
        (gate_y, up_y),
        (swap(gate_y, 1), swap(up_y, 1)),
        (gate_d, up_d),
        (swap(gate_d, 1), swap(up_d, 1)),
    ]


def spread_near(value):
    return (swap(value, 1), swap(value, 2), swap(value, 4))


def spread_far(value, near, zero=None):
    across_c, across_x, across_y = near
    across_d = swap_some(across_y, 2, 0) + swap_some(across_x, 4, 1)
    if zero is not None:
        across_d = across_d + zero
    return [
        value,
        across_c,
        across_x,
        swap(across_x, 1),
        across_y,
        swap(across_y, 1),
        across_d,
        swap(across_d, 1),
    ]


def ring_max(value, axis):
    count = lax.axis_size(axis)
    span = 1
    while span < count:
        pairs = [(source, (source + span) % count) for source in range(count)]
        value = jnp.maximum(value, lax.ppermute(value, axis, pairs))
        span *= 2
    return value


def column_chunks(total, width=512):
    return [(start, min(width, total - start)) for start in range(0, total, width)]


def finish_stage(upstream, normed_grad, widened, gain_row):
    inverse = lax.rsqrt(jnp.mean(widened * widened, axis=1, keepdims=True) + norm_eps)
    gained = gain_row * normed_grad
    mean_term = jnp.mean(widened * gained, axis=1, keepdims=True)
    cubed = inverse * inverse * inverse
    return (upstream.astype(f32) + inverse * gained - widened * cubed * mean_term).astype(bf16)


def turn_kernel(inputs_ref, next_ref, gain_ref, *rest):
    turned_ref = rest[-1]
    features = inputs_ref.shape[1]
    turned_ref[:features] = normalize(inputs_ref[...], gain_ref[...])[2].T
    turned_ref[features:] = normalize(next_ref[...], gain_ref[...])[2].T


def first_kernel(
    scale_ref, upstream_ref, inputs_ref, gain_ref, down_hbm, *refs, partners, sections
):
    pieces = refs[: 2 * partners]
    result_ref, cot_ref, gate_factor_ref, up_factor_ref, gate_full, up_full, down, sem = refs[-8:]
    fetch = pltpu.make_async_copy(down_hbm, down, sem)
    fetch.start()
    rows = pieces[0].shape[0]
    own = lax.axis_index("dp")
    for index in range(2 * partners):
        place = pl.ds(pl.multiple_of((own ^ (index // 2)) * rows, 16), rows)
        full = gate_full if index % 2 == 0 else up_full
        full[place, :] = pieces[index][...]
    upstream = upstream_ref[...]
    last = lax.axis_index("section") == sections - 1
    cot_ref[...] = upstream * jnp.where(last, 1.0, 0.0).astype(bf16)
    normed = normalize(inputs_ref[...], gain_ref[...])[2]
    normed_grad = jnp.zeros(upstream.shape, f32)
    for start, width in column_chunks(gate_full.shape[1]):
        part = slice(start, start + width)
        gate_part, up_part = gate_full[:, part], up_full[:, part]
        gate_factor, up_factor = factors(
            matmul(normed, gate_part) * scale_ref[0], matmul(normed, up_part) * scale_ref[1]
        )
        gate_factor = (gate_factor * scale_ref[0]).astype(bf16)
        up_factor = (up_factor * scale_ref[1]).astype(bf16)
        gate_factor_ref[:, part] = gate_factor
        up_factor_ref[:, part] = up_factor
        if start == 0:
            fetch.wait()
        hidden_grad = transposed(upstream, down[part, :])
        normed_grad += transposed((hidden_grad * gate_factor).astype(bf16), gate_part)
        normed_grad += transposed((hidden_grad * up_factor).astype(bf16), up_part)
    result_ref[...] = finish_stage(
        upstream, normed_grad, inputs_ref[...].astype(f32), gain_ref[...]
    )


def stage_kernel(
    upstream_ref, inputs_ref, gain_ref, down, gate_full, up_full, gate_factor, up_factor, *rest
):
    passed = len(rest) // 2
    result_ref = rest[passed]
    for place in range(passed):
        rest[passed + 1 + place][...] = rest[place][...]
    upstream = upstream_ref[...]
    normed_grad = jnp.zeros(upstream.shape, f32)
    for start, width in column_chunks(gate_full.shape[1]):
        part = slice(start, start + width)
        hidden_grad = transposed(upstream, down[part, :])
        gate_grad = (hidden_grad * gate_factor[:, part]).astype(bf16)
        up_grad = (hidden_grad * up_factor[:, part]).astype(bf16)
        normed_grad += transposed(gate_grad, gate_full[:, part])
        normed_grad += transposed(up_grad, up_full[:, part])
    result_ref[...] = finish_stage(
        upstream, normed_grad, inputs_ref[...].astype(f32), gain_ref[...]
    )


def factors_kernel(scale_ref, gate_full, up_full, cot_ref, *refs, partners):
    pieces = refs[:partners]
    out_gate, out_up, cot_out, gate, up, normed, stack = refs[-7:]
    cot_out[...] = cot_ref[...]
    features, columns = gate.shape
    tokens = pieces[0].shape[1]
    group = normed.shape[0] // tokens
    own = lax.axis_index("dp")
    for k in range(partners):
        part = slice(k * columns, (k + 1) * columns)

        @pl.when(own == k)
        def pick():
            gate[...] = gate_full[:, part]
            up[...] = up_full[:, part]

    for k in range(partners):
        stack[k] = pieces[k][:features]

    def one_group(index, carry):
        for k in range(group):
            normed[k * tokens : (k + 1) * tokens, :] = stack[index * group + k].T
        rows = pl.ds(pl.multiple_of(index * (group * tokens), 16), group * tokens)
        gate_factor, up_factor = factors(
            matmul(normed[...], gate[...]) * scale_ref[0],
            matmul(normed[...], up[...]) * scale_ref[1],
        )
        out_gate[rows, :] = gate_factor.astype(bf16)
        out_up[rows, :] = up_factor.astype(bf16)
        return carry

    lax.fori_loop(0, partners // group, one_group, 0)


def weight_kernel(down_ref, gate_factor, up_factor, *refs, distances, first):
    count = len(distances)
    pieces, turned = refs[:count], refs[count : 2 * count]
    if first:
        out_ref, zero_ref = refs[-5:-3]
        zero_ref[...] = jnp.zeros(zero_ref.shape, bf16)
    else:
        start_ref = refs[2 * count]
        outs = refs[2 * count + 1 : -3]
    upstream, normed, total = refs[-3:]
    own = lax.axis_index("dp")
    tokens, features = pieces[0].shape
    columns = gate_factor.shape[1]
    factor_rows = []
    for place, distance in enumerate(distances):
        block = slice(place * tokens, (place + 1) * tokens)
        upstream[block, :] = pieces[place][...]
        normed[:, block] = turned[place][:features]
        factor_rows.append(slice(distance * tokens, (distance + 1) * tokens))
    down_cols = down_ref[pl.ds(pl.multiple_of(own * columns, 16), columns), :]
    hidden_grad = transposed(upstream[...], down_cols)
    gate_grad = hidden_grad * jnp.concatenate([gate_factor[rows, :] for rows in factor_rows], axis=0)
    up_grad = hidden_grad * jnp.concatenate([up_factor[rows, :] for rows in factor_rows], axis=0)
    grads = jnp.concatenate([gate_grad, up_grad], axis=1).astype(bf16)
    product = matmul(normed[...], grads)
    if first:
        out_ref[...] = product
        return
    total[...] = (start_ref[...] + product).astype(bf16)
    rows = outs[0].shape[0]
    for distance in range(len(outs)):
        place = pl.ds(pl.multiple_of((own ^ distance) * rows, 16), rows)
        outs[distance][...] = total[place, :]


def next_kernel(peak_ref, *refs, partners):
    rows_in, turned_parts = refs[:partners], refs[partners : 2 * partners]
    outs = refs[-3 - partners : -3]
    weights, turned, joined = refs[-3:]
    features = weights.shape[0]
    tokens = turned_parts[0].shape[1]
    columns = turned.shape[0] // 2
    group = joined.shape[1] // tokens
    own = lax.axis_index("dp")
    rows = rows_in[0].shape[0]
    for distance in range(partners):
        place = pl.ds(pl.multiple_of((own ^ distance) * rows, 16), rows)
        weights[place, :] = rows_in[distance][...]
    for start in range(0, features, 128):
        turned[:, start : start + 128] = weights[start : start + 128, :].T
    for first in range(0, partners, group):
        for k in range(group):
            joined[:, k * tokens : (k + 1) * tokens] = turned_parts[first + k][features:]
        both = matmul(turned[...], joined[...])
        gate, up = both[:columns], both[columns:]
        hidden = (gate * jax.nn.sigmoid(gate) * up).astype(bf16)
        for k in range(group):
            outs[first + k][:columns] = hidden[:, k * tokens : (k + 1) * tokens]
    rest = jnp.concatenate([peak_ref[...]] * (tokens // peak_ref.shape[1]), axis=1)
    parts = []
    for unused in range(2):
        parts.append(rest.astype(bf16))
        rest = rest - parts[-1].astype(f32)
    high, middle, low = parts[0], parts[1], rest.astype(bf16)
    for k in range(partners):
        outs[k][columns:] = jnp.concatenate([high, middle, low, low], axis=0)


def join_kernel(*refs, partners):
    pieces = refs[:partners]
    out_ref, peak_ref, held = refs[partners:]
    own = lax.axis_index("dp")
    columns = held.shape[1]
    peaks = None
    for distance in range(partners):
        held[own ^ distance] = pieces[distance][:columns]
        parts = pieces[distance][columns:].astype(f32)
        value = parts[:8] + parts[8:16] + parts[16:24]
        peaks = value if peaks is None else jnp.maximum(peaks, value)
    peak_ref[...] = peaks
    for k in range(partners):
        out_ref[:, k * columns : (k + 1) * columns] = held[k].T


def rows_kernel(*refs, partners, unused_count):
    pieces, sources = refs[:partners], refs[partners : partners + 6]
    outs = refs[partners + 6 + unused_count :]
    targets, news, peak_ref = outs[:6], outs[6 : 6 + partners], outs[6 + partners]
    blocks, gradient = outs[7 + partners :]
    own = lax.axis_index("dp")
    columns = pieces[0].shape[1] // 2
    peaks = []
    for distance in range(partners):
        blocks[own ^ distance] = pieces[distance][...].astype(f32)
    for side in range(2):
        part = slice(side * columns, (side + 1) * columns)
        for k in range(partners):
            gradient[:, k * columns : (k + 1) * columns] = blocks[k, :, part]
        results = adam_update(
            sources[side][...], sources[2 + side][...], sources[4 + side][...], gradient[...]
        )
        for kind in range(3):
            targets[2 * kind + side][...] = results[kind]
        peaks.append(jnp.max(jnp.abs(results[0])))
        gradient[...] = results[0]
        for k in range(partners):
            blocks[k, :, part] = gradient[:, k * columns : (k + 1) * columns]
    for distance in range(partners):
        news[distance][...] = blocks[own ^ distance].astype(bf16)
    shape = (4, peak_ref.shape[1])
    both = jnp.concatenate([jnp.full(shape, peaks[0], f32), jnp.full(shape, peaks[1], f32)], axis=0)

    @pl.when(pl.program_id(0) == 0)
    def begin():
        peak_ref[...] = both

    @pl.when(pl.program_id(0) > 0)
    def further():
        peak_ref[...] = jnp.maximum(peak_ref[...], both)


def cost(flops, accessed):
    return pl.CostEstimate(flops=flops, bytes_accessed=accessed, transcendentals=0)


def smem_space():
    return pl.BlockSpec(memory_space=pltpu.SMEM)


def params(limit):
    return pltpu.CompilerParams(vmem_limit_bytes=limit * mib)


def whole(shape):
    return pl.BlockSpec(shape, lambda *unused: (0,) * len(shape))


def in_any(count):
    return [pl.BlockSpec(memory_space=pl.ANY)] * count


def in_vmem(count):
    return [pl.BlockSpec(memory_space=pltpu.VMEM)] * count


def run_turn(inputs, next_part, gain_row, arrived):
    tokens, features = inputs.shape
    return pl.pallas_call(
        turn_kernel,
        out_shape=jax.ShapeDtypeStruct((2 * features, tokens), bf16),
        in_specs=in_vmem(3) + in_any(len(arrived)),
        out_specs=in_vmem(1)[0],
        compiler_params=params(6),
        name="turn",
    )(inputs, next_part, gain_row, *arrived)


def run_first(scale_pair, upstream, inputs, gain, down, pieces, arrived, sections):
    tokens, features = upstream.shape
    hidden = down.shape[0]
    partners = len(pieces)
    flat = [part for pair in pieces for part in pair]
    return pl.pallas_call(
        functools.partial(first_kernel, partners=partners, sections=sections),
        out_shape=(
            jax.ShapeDtypeStruct((tokens, features), bf16),
            jax.ShapeDtypeStruct((tokens, features), bf16),
            jax.ShapeDtypeStruct((tokens, hidden), bf16),
            jax.ShapeDtypeStruct((tokens, hidden), bf16),
            jax.ShapeDtypeStruct((features, hidden), bf16),
            jax.ShapeDtypeStruct((features, hidden), bf16),
            jax.ShapeDtypeStruct((hidden, features), bf16),
        ),
        in_specs=[smem_space()]
        + in_vmem(3)
        + in_any(1)
        + in_vmem(len(flat))
        + in_any(len(arrived)),
        out_specs=tuple(in_vmem(7)),
        scratch_shapes=[pltpu.SemaphoreType.DMA],
        compiler_params=params(14),
        cost_estimate=cost(10 * tokens * features * hidden, 26 * features * hidden),
        name="first_stage",
    )(scale_pair, upstream, inputs, gain, down, *flat, *arrived)


def run_stage(
    upstream, inputs, gain, down, gate_full, up_full, gate_factor, up_factor, passed
):
    tokens, features = upstream.shape
    hidden = down.shape[0]
    return pl.pallas_call(
        stage_kernel,
        out_shape=(jax.ShapeDtypeStruct((tokens, features), bf16),)
        + tuple(jax.ShapeDtypeStruct(part.shape, bf16) for part in passed),
        in_specs=in_vmem(8 + len(passed)),
        out_specs=tuple(in_vmem(1 + len(passed))),
        compiler_params=params(10),
        cost_estimate=cost(6 * tokens * features * hidden, 8 * features * hidden),
        name="stage",
    )(upstream, inputs, gain, down, gate_full, up_full, gate_factor, up_factor, *passed)


def run_factors(scale_pair, gate_full, up_full, cotangent, pieces):
    partners = len(pieces)
    features, hidden = gate_full.shape
    tokens = pieces[0].shape[1]
    columns = hidden // partners
    shape = jax.ShapeDtypeStruct((partners * tokens, columns), bf16)
    return pl.pallas_call(
        functools.partial(factors_kernel, partners=partners),
        out_shape=(shape, shape, jax.ShapeDtypeStruct(cotangent.shape, bf16)),
        in_specs=[smem_space()] + in_vmem(3 + partners),
        out_specs=tuple(in_vmem(3)),
        scratch_shapes=[
            pltpu.VMEM((features, columns), bf16),
            pltpu.VMEM((features, columns), bf16),
            pltpu.VMEM((partners * tokens // 2, features), bf16),
            pltpu.VMEM((partners, features, tokens), bf16),
        ],
        compiler_params=params(18),
        cost_estimate=cost(4 * partners * tokens * features * columns, 8 * features * columns),
        name="column_factors",
    )(scale_pair, gate_full, up_full, cotangent, *pieces)


def run_weights(down, factor_cols, pieces, turned, distances, partners, start=None):
    tokens, features = pieces[0].shape
    columns = factor_cols[0].shape[1]
    count = len(distances)
    first = start is None
    if first:
        shapes = (
            jax.ShapeDtypeStruct((features, 2 * columns), f32),
            jax.ShapeDtypeStruct((tokens, features), bf16),
        )
        starts = []
    else:
        block = jax.ShapeDtypeStruct((features // partners, 2 * columns), bf16)
        shapes = (block,) * partners
        starts = [start]
    return pl.pallas_call(
        functools.partial(weight_kernel, distances=distances, first=first),
        out_shape=shapes,
        in_specs=in_vmem(3 + 2 * count + len(starts)),
        out_specs=tuple(in_vmem(len(shapes))),
        scratch_shapes=[
            pltpu.VMEM((count * tokens, features), bf16),
            pltpu.VMEM((features, count * tokens), bf16),
            pltpu.VMEM((features, 2 * columns), bf16),
        ],
        compiler_params=params(18),
        cost_estimate=cost(6 * count * tokens * features * columns, 12 * features * columns),
        name="column_gradients",
    )(down, *factor_cols, *pieces, *turned, *starts)


def run_next(peaks, rows_in, turned):
    partners = len(turned)
    rows, both = rows_in[0].shape
    tokens = turned[0].shape[1]
    features = partners * rows
    return pl.pallas_call(
        functools.partial(next_kernel, partners=partners),
        out_shape=(jax.ShapeDtypeStruct((both // 2 + 32, tokens), bf16),) * partners,
        in_specs=in_vmem(1 + 2 * partners),
        out_specs=tuple(in_vmem(partners)),
        scratch_shapes=[
            pltpu.VMEM((features, both), bf16),
            pltpu.VMEM((both, features), bf16),
            pltpu.VMEM((features, partners * tokens // 2), bf16),
        ],
        compiler_params=params(18),
        cost_estimate=cost(2 * partners * tokens * features * both, 16 * features * both),
        name="next_columns",
    )(peaks, *rows_in, *turned)


def run_join(pieces):
    partners = len(pieces)
    columns, tokens = pieces[0].shape[0] - 32, pieces[0].shape[1]
    return pl.pallas_call(
        functools.partial(join_kernel, partners=partners),
        out_shape=(
            jax.ShapeDtypeStruct((tokens, partners * columns), bf16),
            jax.ShapeDtypeStruct((8, tokens), f32),
        ),
        in_specs=in_vmem(partners),
        out_specs=tuple(in_vmem(2)),
        scratch_shapes=[pltpu.VMEM((partners, columns, tokens), bf16)],
        compiler_params=params(8),
        name="next_join",
    )(*pieces)


def run_rows(pieces, sources, arrived):
    partners = len(pieces)
    rows, hidden = sources[0].shape
    both = pieces[0].shape[1]
    step = 16
    row_spec = pl.BlockSpec((step, hidden), lambda i: (i, 0))
    block_spec = pl.BlockSpec((step, both), lambda i: (i, 0))
    return pl.pallas_call(
        functools.partial(rows_kernel, partners=partners, unused_count=len(arrived)),
        grid=(rows // step,),
        out_shape=(jax.ShapeDtypeStruct((rows, hidden), f32),) * 6
        + (jax.ShapeDtypeStruct((rows, both), bf16),) * partners
        + (jax.ShapeDtypeStruct((8, 128), f32),),
        in_specs=[block_spec] * partners + [row_spec] * 6 + in_any(len(arrived)),
        out_specs=(row_spec,) * 6 + (block_spec,) * partners + (whole((8, 128)),),
        scratch_shapes=[
            pltpu.VMEM((partners, step, both), f32),
            pltpu.VMEM((step, hidden), f32),
        ],
        compiler_params=params(10),
        cost_estimate=cost(40 * rows * hidden, 48 * rows * hidden),
        name="row_update",
    )(*pieces, *sources, *arrived)


def down_shift(value, sections):
    return lax.ppermute(value, "section", [(source, source - 1) for source in range(1, sections)])


def columns_plan(
    section_inputs,
    cotangent,
    norm_gain,
    quant_gate,
    quant_up,
    scales,
    down_proj,
    master_gate,
    master_up,
    moment_gate,
    moment_up,
    second_gate,
    second_up,
    next_inputs,
):
    gain_row = norm_gain[0]
    scale_pair = scales[0]
    down_local = down_proj[0]
    inputs = section_inputs[0]
    partners = lax.axis_size("dp")
    sections = lax.axis_size("section")
    gain = gain_row[None]
    sources = [
        part[0]
        for part in (master_gate, master_up, moment_gate, moment_up, second_gate, second_up)
    ]

    weight_pieces = spread_weights(quant_gate[0], quant_up[0])
    turned = run_turn(inputs, next_inputs[0], gain, weight_pieces[6])
    across_c, across_x, across_y = spread_near(turned)
    result, cotangent_here, gate_factor, up_factor, gate_full, up_full, down_here = run_first(
        scale_pair, cotangent, inputs, gain, down_local, weight_pieces, [turned], sections
    )

    def next_stage(upstream, passed):
        return run_stage(
            upstream, inputs, gain, down_here, gate_full, up_full, gate_factor, up_factor, passed
        )

    for turn in range(sections - 1):
        incoming = down_shift(result, sections)
        if turn == sections - 2:
            *factor_cols, cotangent_here = run_factors(
                scale_pair, gate_full, up_full, cotangent_here, turned_all
            )
        upstream = cotangent_here + incoming
        if turn == 0:
            result, across_x, across_y = next_stage(upstream, [across_x, across_y])
            turned_all = spread_far(turned, (across_c, across_x, across_y))
        elif turn < sections - 2:
            (result,) = next_stage(upstream, [])
    (result,) = next_stage(upstream, [])
    near = spread_near(upstream)
    order = (0, 1, 2, 4)
    gradient, zero = run_weights(
        down_here,
        factor_cols,
        [upstream, *near],
        [turned_all[k] for k in order],
        order,
        partners,
    )
    far = spread_far(upstream, near, zero)
    order = (3, 5, 6, 7)
    row_blocks = run_weights(
        down_here,
        factor_cols,
        [far[k] for k in order],
        [turned_all[k] for k in order],
        order,
        partners,
        gradient,
    )
    *updated, peaks = run_rows(exchange(row_blocks), sources, [result])
    updated, new_blocks = updated[:6], updated[6:]
    token_blocks = run_next(peaks, exchange(new_blocks), turned_all)
    next_hidden, peaks = run_join(exchange(token_blocks))
    new_scales = peaks[::4, 0] + scale_eps
    return (
        result[None],
        *(part[None] for part in updated),
        new_scales[None, :],
        next_hidden[None],
    )


def plain_plan(
    section_inputs,
    cotangent,
    norm_gain,
    quant_gate,
    quant_up,
    scales,
    down_proj,
    master_gate,
    master_up,
    moment_gate,
    moment_up,
    second_gate,
    second_up,
    next_inputs,
):
    gain_row = norm_gain[0]
    scale_pair = scales[0]
    down_local = down_proj[0]
    hidden_count = quant_gate.shape[2]
    sections = lax.axis_size("section")
    position = lax.axis_index("section")
    is_last = position == sections - 1
    both_full = lax.all_gather(
        jnp.concatenate([quant_gate[0], quant_up[0]], axis=1), "dp", axis=0, tiled=True
    )
    widened, inverse, normed = normalize(section_inputs[0], gain_row)
    both_pre = jnp.dot(normed, both_full, preferred_element_type=jnp.float32)
    gate_pre = both_pre[:, :hidden_count] * scale_pair[0]
    up_pre = both_pre[:, hidden_count:] * scale_pair[1]
    sigmoid = jax.nn.sigmoid(gate_pre)
    up_factor = gate_pre * sigmoid
    gate_factor = up_pre * (sigmoid * (1.0 + gate_pre * (1.0 - sigmoid)))
    cubed = inverse * inverse * inverse

    def stage(upstream):
        hidden_grad = transposed(upstream, down_local)
        gate_grad = (hidden_grad * gate_factor).astype(jnp.bfloat16)
        up_grad = (hidden_grad * up_factor).astype(jnp.bfloat16)
        normed_grad = (
            transposed(gate_grad, both_full[:, :hidden_count]) * scale_pair[0]
            + transposed(up_grad, both_full[:, hidden_count:]) * scale_pair[1]
        )
        gained = gain_row * normed_grad
        mean_term = jnp.mean(widened * gained, axis=-1, keepdims=True)
        result = upstream.astype(jnp.float32) + inverse * gained - widened * cubed * mean_term
        return (result.astype(jnp.bfloat16), gate_grad, up_grad)

    upstream = cotangent
    for turn in range(sections):
        result, gate_grad, up_grad = stage(upstream)
        if turn < sections - 1:
            incoming = lax.ppermute(
                result, "section", [(source, source - 1) for source in range(1, sections)]
            )
            upstream = jnp.where(is_last, cotangent, incoming)

    grads_all = jnp.concatenate([gate_grad, up_grad], axis=1)
    summed = lax.psum_scatter(
        lax.dot_general(
            normed, grads_all, (((0,), (0,)), ((), ())), preferred_element_type=jnp.float32
        ).astype(jnp.bfloat16),
        "dp",
        scatter_dimension=0,
        tiled=True,
    ).astype(jnp.float32)
    new_gate, mom_gate, sec_gate = adam_update(
        master_gate[0], moment_gate[0], second_gate[0], summed[:, :hidden_count]
    )
    new_up, mom_up, sec_up = adam_update(
        master_up[0], moment_up[0], second_up[0], summed[:, hidden_count:]
    )
    peaks = jnp.stack([jnp.max(jnp.abs(new_gate)), jnp.max(jnp.abs(new_up))])
    new_scales = ring_max(peaks, "dp") + scale_eps
    unused_one, unused_two, next_normed = normalize(next_inputs[0], gain_row)
    stacked = jnp.concatenate([new_gate, new_up], axis=1).astype(jnp.bfloat16)
    both_next = jnp.dot(
        next_normed,
        lax.all_gather(stacked, "dp", axis=0, tiled=True),
        preferred_element_type=jnp.float32,
    )
    next_hidden = (
        jax.nn.silu(both_next[:, :hidden_count]) * both_next[:, hidden_count:]
    ).astype(jnp.bfloat16)
    return (
        result[None],
        new_gate[None],
        new_up[None],
        mom_gate[None],
        mom_up[None],
        sec_gate[None],
        sec_up[None],
        new_scales[None, :],
        next_hidden[None],
    )


def solution(mesh):
    placed = (
        P("section", "dp", None),
        P("dp", None),
        P("section", None),
        P("section", "dp", None),
        P("section", "dp", None),
        P("section", None),
        P("section", None, None),
        P("section", "dp", None),
        P("section", "dp", None),
        P("section", "dp", None),
        P("section", "dp", None),
        P("section", "dp", None),
        P("section", "dp", None),
        P("section", "dp", None),
    )
    fits = mesh.shape["dp"] == 8 and mesh.shape["section"] >= 4
    return jax.shard_map(
        columns_plan if fits else plain_plan,
        mesh=mesh,
        in_specs=placed,
        out_specs=(
            P("section", "dp", None),
            P("section", "dp", None),
            P("section", "dp", None),
            P("section", "dp", None),
            P("section", "dp", None),
            P("section", "dp", None),
            P("section", "dp", None),
            P("section", None),
            P("section", "dp", None),
        ),
        check_vma=False,
    )
```

```python
import functools

import jax
import jax.numpy as jnp
from jax import lax
from jax.experimental import pallas as pl
from jax.experimental.pallas import tpu as pltpu
from jax.sharding import PartitionSpec as P

beta_one = 0.9
beta_two = 0.95
learn_rate = 0.002
decay_rate = 0.1
adam_steps = 100.0
norm_eps = 1e-06
adam_eps = 1e-08
scale_eps = 1e-06
mib = 1024 * 1024
bf16 = jnp.bfloat16
f32 = jnp.float32


def normalize(inputs, norm_gain):
    widened = inputs.astype(jnp.float32)
    inverse = lax.rsqrt(jnp.mean(widened * widened, axis=-1, keepdims=True) + norm_eps)
    return (widened, inverse, (widened * inverse * norm_gain).astype(jnp.bfloat16))


def matmul(first_op, second_op):
    return jnp.dot(first_op, second_op, preferred_element_type=jnp.float32)


def transposed(first_op, second_op):
    return lax.dot_general(
        first_op, second_op, (((1,), (1,)), ((), ())), preferred_element_type=jnp.float32
    )


def adam_update(master, moment_old, second_old, gradient):
    moment_one = beta_one * moment_old + (1.0 - beta_one) * gradient
    moment_two = beta_two * second_old + (1.0 - beta_two) * gradient * gradient
    unbiased_one = moment_one / (1.0 - beta_one**adam_steps)
    unbiased_two = moment_two / (1.0 - beta_two**adam_steps)
    updated = master - learn_rate * (
        unbiased_one / (jnp.sqrt(unbiased_two) + adam_eps) + decay_rate * master
    )
    return (updated, moment_one, moment_two)


def factors(gate_pre, up_pre):
    sigmoid = jax.nn.sigmoid(gate_pre)
    return (up_pre * (sigmoid * (1.0 + gate_pre * (1.0 - sigmoid))), gate_pre * sigmoid)


def exchange(blocks):
    got = {k: swap(blocks[k], k) for k in (6, 7, 2, 4, 3, 5, 1)}
    return [blocks[0]] + [got[k] for k in range(1, len(blocks))]


def swap(value, distance):
    pairs = [(source, source ^ distance) for source in range(lax.axis_size("dp"))]
    return lax.ppermute(value, "dp", pairs)


def swap_some(value, distance, core):
    pairs = [(k, k ^ distance) for k in range(lax.axis_size("dp")) if k % 2 == core]
    return lax.ppermute(value, "dp", pairs)


def spread_weights(gate, up):
    near = [swap(part, distance) for distance in (2, 4, 1) for part in (gate, up)]
    gate_x, up_x, gate_y, up_y, gate_c, up_c = near
    gate_d, up_d = swap(gate_y, 2), swap(up_x, 4)
    return [
        (gate, up),
        (gate_c, up_c),
        (gate_x, up_x),
        (swap(gate_x, 1), swap(up_x, 1)),
        (gate_y, up_y),
        (swap(gate_y, 1), swap(up_y, 1)),
        (gate_d, up_d),
        (swap(gate_d, 1), swap(up_d, 1)),
    ]


def spread_near(value):
    return (swap(value, 1), swap(value, 2), swap(value, 4))


def spread_far(value, near, zero=None):
    across_c, across_x, across_y = near
    across_d = swap_some(across_y, 2, 0) + swap_some(across_x, 4, 1)
    if zero is not None:
        across_d = across_d + zero
    return [
        value,
        across_c,
        across_x,
        swap(across_x, 1),
        across_y,
        swap(across_y, 1),
        across_d,
        swap(across_d, 1),
    ]


def ring_max(value, axis):
    count = lax.axis_size(axis)
    span = 1
    while span < count:
        pairs = [(source, (source + span) % count) for source in range(count)]
        value = jnp.maximum(value, lax.ppermute(value, axis, pairs))
        span *= 2
    return value


def column_chunks(total, width=512):
    return [(start, min(width, total - start)) for start in range(0, total, width)]


def finish_stage(upstream, normed_grad, widened, gain_row):
    inverse = lax.rsqrt(jnp.mean(widened * widened, axis=1, keepdims=True) + norm_eps)
    gained = gain_row * normed_grad
    mean_term = jnp.mean(widened * gained, axis=1, keepdims=True)
    cubed = inverse * inverse * inverse
    return (upstream.astype(f32) + inverse * gained - widened * cubed * mean_term).astype(bf16)


def turn_kernel(inputs_hbm, next_hbm, gain_hbm, *rest):
    turned_ref, inputs, following, gain, sems = rest[-5:]
    pairs = ((inputs_hbm, inputs), (next_hbm, following), (gain_hbm, gain))
    copies = [
        pltpu.make_async_copy(source, target, sems.at[place])
        for place, (source, target) in enumerate(pairs)
    ]
    for copy in copies:
        copy.start()
    for copy in copies:
        copy.wait()
    features = inputs.shape[1]
    turned_ref[:features] = normalize(inputs[...], gain[...])[2].T
    turned_ref[features:] = normalize(following[...], gain[...])[2].T


def first_kernel(
    scale_ref, upstream_ref, inputs_ref, gain_ref, down_hbm, *refs, partners, sections
):
    pieces = refs[: 2 * partners]
    refs = refs[-8:]
    result_ref, cot_ref, gate_factor_ref, up_factor_ref, gate_full, up_full, down, sem = refs
    fetch = pltpu.make_async_copy(down_hbm, down, sem)
    fetch.start()
    rows = pieces[0].shape[0]
    own = lax.axis_index("dp")
    for index in range(2 * partners):
        place = pl.ds(pl.multiple_of((own ^ (index // 2)) * rows, 16), rows)
        full = gate_full if index % 2 == 0 else up_full
        full[place, :] = pieces[index][...]
    upstream = upstream_ref[...]
    last = lax.axis_index("section") == sections - 1
    cot_ref[...] = upstream * jnp.where(last, 1.0, 0.0).astype(bf16)
    normed = normalize(inputs_ref[...], gain_ref[...])[2]
    normed_grad = jnp.zeros(upstream.shape, f32)
    for start, width in column_chunks(gate_full.shape[1]):
        part = slice(start, start + width)
        gate_part, up_part = gate_full[:, part], up_full[:, part]
        gate_factor, up_factor = factors(
            matmul(normed, gate_part) * scale_ref[0], matmul(normed, up_part) * scale_ref[1]
        )
        gate_factor = (gate_factor * scale_ref[0]).astype(bf16)
        up_factor = (up_factor * scale_ref[1]).astype(bf16)
        gate_factor_ref[:, part] = gate_factor
        up_factor_ref[:, part] = up_factor
        if start == 0:
            fetch.wait()
        hidden_grad = transposed(upstream, down[part, :])
        normed_grad += transposed((hidden_grad * gate_factor).astype(bf16), gate_part)
        normed_grad += transposed((hidden_grad * up_factor).astype(bf16), up_part)
    result_ref[...] = finish_stage(
        upstream, normed_grad, inputs_ref[...].astype(f32), gain_ref[...]
    )


def stage_kernel(
    upstream_ref, inputs_ref, gain_ref, down, gate_full, up_full, gate_factor, up_factor, *rest, half
):
    passed = len(rest) // 2
    result_ref = rest[passed]
    for place in range(passed):
        rest[passed + 1 + place][...] = rest[place][...]
    upstream = upstream_ref[...]
    rows = slice(half * upstream.shape[0], (half + 1) * upstream.shape[0])
    normed_grad = jnp.zeros(upstream.shape, f32)
    for start, width in column_chunks(gate_full.shape[1]):
        part = slice(start, start + width)
        hidden_grad = transposed(upstream, down[part, :])
        gate_grad = (hidden_grad * gate_factor[rows, part]).astype(bf16)
        up_grad = (hidden_grad * up_factor[rows, part]).astype(bf16)
        normed_grad += transposed(gate_grad, gate_full[:, part])
        normed_grad += transposed(up_grad, up_full[:, part])
    result_ref[...] = finish_stage(
        upstream, normed_grad, inputs_ref[rows, :].astype(f32), gain_ref[...]
    )


def factors_kernel(scale_ref, gate_full, up_full, cot_ref, *refs, partners):
    pieces = refs[:partners]
    out_gate, out_up, cot_out, gate, up, normed, stack = refs[-7:]
    cot_out[...] = cot_ref[...]
    features, columns = gate.shape
    tokens = pieces[0].shape[1]
    group = normed.shape[0] // tokens
    own = lax.axis_index("dp")
    for k in range(partners):
        part = slice(k * columns, (k + 1) * columns)

        @pl.when(own == k)
        def pick():
            gate[...] = gate_full[:, part]
            up[...] = up_full[:, part]

    for k in range(partners):
        stack[k] = pieces[k][:features]

    def one_group(index, carry):
        for k in range(group):
            normed[k * tokens : (k + 1) * tokens, :] = stack[index * group + k].T
        rows = pl.ds(pl.multiple_of(index * (group * tokens), 16), group * tokens)
        gate_factor, up_factor = factors(
            matmul(normed[...], gate[...]) * scale_ref[0],
            matmul(normed[...], up[...]) * scale_ref[1],
        )
        out_gate[rows, :] = gate_factor.astype(bf16)
        out_up[rows, :] = up_factor.astype(bf16)
        return carry

    lax.fori_loop(0, partners // group, one_group, 0)


def weight_kernel(down_ref, gate_factor, up_factor, *refs, distances, first):
    count = len(distances)
    pieces, turned = refs[:count], refs[count : 2 * count]
    if first:
        out_ref, zero_ref = refs[-5:-3]
        zero_ref[...] = jnp.zeros(zero_ref.shape, bf16)
    else:
        start_ref = refs[2 * count]
        outs = refs[2 * count + 1 : -3]
    upstream, normed, total = refs[-3:]
    own = lax.axis_index("dp")
    tokens, features = pieces[0].shape
    columns = gate_factor.shape[1]
    factor_rows = []
    for place, distance in enumerate(distances):
        block = slice(place * tokens, (place + 1) * tokens)
        upstream[block, :] = pieces[place][...]
        normed[:, block] = turned[place][:features]
        factor_rows.append(slice(distance * tokens, (distance + 1) * tokens))
    down_cols = down_ref[pl.ds(pl.multiple_of(own * columns, 16), columns), :]
    hidden_grad = transposed(upstream[...], down_cols)
    gate_grad = hidden_grad * jnp.concatenate([gate_factor[rows, :] for rows in factor_rows], axis=0)
    up_grad = hidden_grad * jnp.concatenate([up_factor[rows, :] for rows in factor_rows], axis=0)
    grads = jnp.concatenate([gate_grad, up_grad], axis=1).astype(bf16)
    product = matmul(normed[...], grads)
    if first:
        out_ref[...] = product
        return
    total[...] = (start_ref[...] + product).astype(bf16)
    rows = outs[0].shape[0]
    for distance in range(len(outs)):
        place = pl.ds(pl.multiple_of((own ^ distance) * rows, 16), rows)
        outs[distance][...] = total[place, :]


def next_kernel(peak_ref, *refs, partners):
    rows_in, turned_parts = refs[:partners], refs[partners : 2 * partners]
    outs = refs[-3 - partners : -3]
    weights, turned, joined = refs[-3:]
    features = weights.shape[0]
    tokens = turned_parts[0].shape[1]
    columns = turned.shape[0] // 2
    group = joined.shape[1] // tokens
    own = lax.axis_index("dp")
    rows = rows_in[0].shape[0]
    for distance in range(partners):
        place = pl.ds(pl.multiple_of((own ^ distance) * rows, 16), rows)
        weights[place, :] = rows_in[distance][...]
    for start in range(0, features, 128):
        turned[:, start : start + 128] = weights[start : start + 128, :].T
    for first in range(0, partners, group):
        for k in range(group):
            joined[:, k * tokens : (k + 1) * tokens] = turned_parts[first + k][features:]
        both = matmul(turned[...], joined[...])
        gate, up = both[:columns], both[columns:]
        hidden = (gate * jax.nn.sigmoid(gate) * up).astype(bf16)
        for k in range(group):
            outs[first + k][:columns] = hidden[:, k * tokens : (k + 1) * tokens]
    rest = jnp.concatenate([peak_ref[...]] * (tokens // peak_ref.shape[1]), axis=1)
    parts = []
    for unused in range(2):
        parts.append(rest.astype(bf16))
        rest = rest - parts[-1].astype(f32)
    parts.append(rest.astype(bf16))
    extra = jnp.concatenate([part.astype(f32)[2:6] for part in parts + parts[-1:]], axis=0)
    for k in range(partners):
        outs[k][columns:] = extra.astype(bf16)


def join_kernel(*refs, partners):
    pieces = refs[:partners]
    out_ref, peak_ref, held = refs[partners:]
    own = lax.axis_index("dp")
    columns = held.shape[1]
    peaks = None
    for distance in range(partners):
        held[own ^ distance] = pieces[distance][:columns]
        parts = pieces[distance][columns:].astype(f32)
        value = parts[:4] + parts[4:8] + parts[8:12]
        peaks = value if peaks is None else jnp.maximum(peaks, value)
    peak_ref[...] = peaks
    for k in range(partners):
        out_ref[:, k * columns : (k + 1) * columns] = held[k].T


def rows_kernel(*refs, partners, unused_count):
    pieces, sources = refs[:partners], refs[partners : partners + 6]
    outs = refs[partners + 6 + unused_count :]
    targets, news, peak_ref = outs[:6], outs[6 : 6 + partners], outs[6 + partners]
    blocks, gradient = outs[7 + partners :]
    own = lax.axis_index("dp")
    columns = pieces[0].shape[1] // 2
    peaks = []
    for distance in range(partners):
        blocks[own ^ distance] = pieces[distance][...].astype(f32)
    for side in range(2):
        part = slice(side * columns, (side + 1) * columns)
        for k in range(partners):
            gradient[:, k * columns : (k + 1) * columns] = blocks[k, :, part]
        results = adam_update(
            sources[side][...], sources[2 + side][...], sources[4 + side][...], gradient[...]
        )
        for kind in range(3):
            targets[2 * kind + side][...] = results[kind]
        peaks.append(jnp.max(jnp.abs(results[0])))
        gradient[...] = results[0]
        for k in range(partners):
            blocks[k, :, part] = gradient[:, k * columns : (k + 1) * columns]
    for distance in range(partners):
        news[distance][...] = blocks[own ^ distance].astype(bf16)
    shape = (4, peak_ref.shape[1])
    both = jnp.concatenate([jnp.full(shape, peaks[0], f32), jnp.full(shape, peaks[1], f32)], axis=0)

    @pl.when(pl.program_id(0) == 0)
    def begin():
        peak_ref[...] = both

    @pl.when(pl.program_id(0) > 0)
    def further():
        peak_ref[...] = jnp.maximum(peak_ref[...], both)


def cost(flops, accessed):
    return pl.CostEstimate(flops=flops, bytes_accessed=accessed, transcendentals=0)


def smem_space():
    return pl.BlockSpec(memory_space=pltpu.SMEM)


def params(limit):
    return pltpu.CompilerParams(vmem_limit_bytes=limit * mib)


def whole(shape):
    return pl.BlockSpec(shape, lambda *unused: (0,) * len(shape))


def in_hbm(count):
    return [pl.BlockSpec(memory_space=pltpu.HBM)] * count


def in_any(count):
    return [pl.BlockSpec(memory_space=pl.ANY)] * count


def in_vmem(count):
    return [pl.BlockSpec(memory_space=pltpu.VMEM)] * count


def run_turn(inputs, next_part, gain_row, arrived):
    tokens, features = inputs.shape
    return pl.pallas_call(
        turn_kernel,
        out_shape=jax.ShapeDtypeStruct((2 * features, tokens), bf16),
        in_specs=in_hbm(3) + in_any(len(arrived)),
        out_specs=in_vmem(1)[0],
        scratch_shapes=[
            pltpu.VMEM((tokens, features), bf16),
            pltpu.VMEM((tokens, features), bf16),
            pltpu.VMEM((1, features), f32),
            pltpu.SemaphoreType.DMA((3,)),
        ],
        compiler_params=params(6),
        name="turn",
    )(inputs, next_part, gain_row, *arrived)


def run_first(scale_pair, upstream, inputs, gain, down, pieces, arrived, sections):
    tokens, features = upstream.shape
    hidden = down.shape[0]
    partners = len(pieces)
    flat = [part for pair in pieces for part in pair]
    return pl.pallas_call(
        functools.partial(first_kernel, partners=partners, sections=sections),
        out_shape=(
            jax.ShapeDtypeStruct((tokens, features), bf16),
            jax.ShapeDtypeStruct((tokens, features), bf16),
            jax.ShapeDtypeStruct((tokens, hidden), bf16),
            jax.ShapeDtypeStruct((tokens, hidden), bf16),
            jax.ShapeDtypeStruct((features, hidden), bf16),
            jax.ShapeDtypeStruct((features, hidden), bf16),
            jax.ShapeDtypeStruct((hidden, features), bf16),
        ),
        in_specs=[smem_space()]
        + in_vmem(3)
        + in_hbm(1)
        + in_vmem(len(flat))
        + in_any(len(arrived)),
        out_specs=tuple(in_vmem(7)),
        scratch_shapes=[pltpu.SemaphoreType.DMA],
        compiler_params=params(14),
        cost_estimate=cost(10 * tokens * features * hidden, 26 * features * hidden),
        name="first_stage",
    )(scale_pair, upstream, inputs, gain, down, *flat, *arrived)


def run_stage(
    upstream, inputs, gain, down, gate_full, up_full, gate_factor, up_factor, passed, half
):
    tokens, features = upstream.shape
    hidden = down.shape[0]
    return pl.pallas_call(
        functools.partial(stage_kernel, half=half),
        out_shape=(jax.ShapeDtypeStruct((tokens, features), bf16),)
        + tuple(jax.ShapeDtypeStruct(part.shape, bf16) for part in passed),
        in_specs=in_vmem(8 + len(passed)),
        out_specs=tuple(in_vmem(1 + len(passed))),
        compiler_params=params(10),
        cost_estimate=cost(6 * tokens * features * hidden, 8 * features * hidden),
        name="stage",
    )(upstream, inputs, gain, down, gate_full, up_full, gate_factor, up_factor, *passed)


def run_factors(scale_pair, gate_full, up_full, cotangent, pieces):
    partners = len(pieces)
    features, hidden = gate_full.shape
    tokens = pieces[0].shape[1]
    columns = hidden // partners
    shape = jax.ShapeDtypeStruct((partners * tokens, columns), bf16)
    return pl.pallas_call(
        functools.partial(factors_kernel, partners=partners),
        out_shape=(shape, shape, jax.ShapeDtypeStruct(cotangent.shape, bf16)),
        in_specs=[smem_space()] + in_vmem(3 + partners),
        out_specs=tuple(in_vmem(3)),
        scratch_shapes=[
            pltpu.VMEM((features, columns), bf16),
            pltpu.VMEM((features, columns), bf16),
            pltpu.VMEM((partners * tokens // 2, features), bf16),
            pltpu.VMEM((partners, features, tokens), bf16),
        ],
        compiler_params=params(18),
        cost_estimate=cost(4 * partners * tokens * features * columns, 8 * features * columns),
        name="column_factors",
    )(scale_pair, gate_full, up_full, cotangent, *pieces)


def run_weights(down, factor_cols, pieces, turned, distances, partners, start=None):
    tokens, features = pieces[0].shape
    columns = factor_cols[0].shape[1]
    count = len(distances)
    first = start is None
    if first:
        shapes = (
            jax.ShapeDtypeStruct((features, 2 * columns), f32),
            jax.ShapeDtypeStruct((tokens, features), bf16),
        )
        starts = []
    else:
        block = jax.ShapeDtypeStruct((features // partners, 2 * columns), bf16)
        shapes = (block,) * partners
        starts = [start]
    return pl.pallas_call(
        functools.partial(weight_kernel, distances=distances, first=first),
        out_shape=shapes,
        in_specs=in_vmem(3 + 2 * count + len(starts)),
        out_specs=tuple(in_vmem(len(shapes))),
        scratch_shapes=[
            pltpu.VMEM((count * tokens, features), bf16),
            pltpu.VMEM((features, count * tokens), bf16),
            pltpu.VMEM((features, 2 * columns), bf16),
        ],
        compiler_params=params(18),
        cost_estimate=cost(6 * count * tokens * features * columns, 12 * features * columns),
        name="column_gradients",
    )(down, *factor_cols, *pieces, *turned, *starts)


def run_next(peaks, rows_in, turned):
    partners = len(turned)
    rows, both = rows_in[0].shape
    tokens = turned[0].shape[1]
    features = partners * rows
    return pl.pallas_call(
        functools.partial(next_kernel, partners=partners),
        out_shape=(jax.ShapeDtypeStruct((both // 2 + 16, tokens), bf16),) * partners,
        in_specs=in_vmem(1 + 2 * partners),
        out_specs=tuple(in_vmem(partners)),
        scratch_shapes=[
            pltpu.VMEM((features, both), bf16),
            pltpu.VMEM((both, features), bf16),
            pltpu.VMEM((features, partners * tokens // 2), bf16),
        ],
        compiler_params=params(18),
        cost_estimate=cost(2 * partners * tokens * features * both, 16 * features * both),
        name="next_columns",
    )(peaks, *rows_in, *turned)


def run_join(pieces):
    partners = len(pieces)
    columns, tokens = pieces[0].shape[0] - 16, pieces[0].shape[1]
    return pl.pallas_call(
        functools.partial(join_kernel, partners=partners),
        out_shape=(
            jax.ShapeDtypeStruct((tokens, partners * columns), bf16),
            jax.ShapeDtypeStruct((4, tokens), f32),
        ),
        in_specs=in_vmem(partners),
        out_specs=tuple(in_vmem(2)),
        scratch_shapes=[pltpu.VMEM((partners, columns, tokens), bf16)],
        compiler_params=params(8),
        name="next_join",
    )(*pieces)


def run_rows(pieces, sources, arrived):
    partners = len(pieces)
    rows, hidden = sources[0].shape
    both = pieces[0].shape[1]
    step = 16
    row_spec = pl.BlockSpec((step, hidden), lambda i: (i, 0))
    block_spec = pl.BlockSpec((step, both), lambda i: (i, 0))
    return pl.pallas_call(
        functools.partial(rows_kernel, partners=partners, unused_count=len(arrived)),
        grid=(rows // step,),
        out_shape=(jax.ShapeDtypeStruct((rows, hidden), f32),) * 6
        + (jax.ShapeDtypeStruct((rows, both), bf16),) * partners
        + (jax.ShapeDtypeStruct((8, 128), f32),),
        in_specs=[block_spec] * partners + [row_spec] * 6 + in_any(len(arrived)),
        out_specs=(row_spec,) * 6 + (block_spec,) * partners + (whole((8, 128)),),
        scratch_shapes=[
            pltpu.VMEM((partners, step, both), f32),
            pltpu.VMEM((step, hidden), f32),
        ],
        compiler_params=params(10),
        cost_estimate=cost(40 * rows * hidden, 48 * rows * hidden),
        name="row_update",
    )(*pieces, *sources, *arrived)


def down_shift(value, sections):
    return lax.ppermute(value, "section", [(source, source - 1) for source in range(1, sections)])


def columns_plan(
    section_inputs,
    cotangent,
    norm_gain,
    quant_gate,
    quant_up,
    scales,
    down_proj,
    master_gate,
    master_up,
    moment_gate,
    moment_up,
    second_gate,
    second_up,
    next_inputs,
):
    gain_row = norm_gain[0]
    scale_pair = scales[0]
    down_local = down_proj[0]
    inputs = section_inputs[0]
    partners = lax.axis_size("dp")
    sections = lax.axis_size("section")
    gain = gain_row[None]
    sources = [
        part[0]
        for part in (master_gate, master_up, moment_gate, moment_up, second_gate, second_up)
    ]

    weight_pieces = spread_weights(quant_gate[0], quant_up[0])
    turned = run_turn(inputs, next_inputs[0], gain, weight_pieces[6])
    across_c, across_x, across_y = spread_near(turned)
    result, cotangent_here, gate_factor, up_factor, gate_full, up_full, down_here = run_first(
        scale_pair, cotangent, inputs, gain, down_local, weight_pieces, [turned], sections
    )

    def next_stage(upstream, passed, half):
        return run_stage(
            upstream,
            inputs,
            gain,
            down_here,
            gate_full,
            up_full,
            gate_factor,
            up_factor,
            passed,
            half,
        )

    results = [result]
    rows = inputs.shape[0] // 2
    for turn in range(sections - 1):
        incoming = [down_shift(part, sections) for part in results]
        if turn == sections - 2:
            *factor_cols, cotangent_here = run_factors(
                scale_pair, gate_full, up_full, cotangent_here, turned_all
            )
            upstream = cotangent_here + jnp.concatenate(incoming, axis=0)
            break
        upstream = cotangent_here + incoming[0]
        if turn == 0:
            result, across_x, across_y = next_stage(upstream, [across_x, across_y], 0)
            turned_all = spread_far(turned, (across_c, across_x, across_y))
            results = [result]
        elif turn < sections - 3:
            results = next_stage(upstream, [], 0)
        else:
            results = [
                next_stage(upstream[half * rows : (half + 1) * rows], [], half)[0]
                for half in range(2)
            ]
    (result,) = next_stage(upstream, [], 0)
    near = spread_near(upstream)
    order = (0, 1, 2, 4)
    gradient, zero = run_weights(
        down_here,
        factor_cols,
        [upstream, *near],
        [turned_all[k] for k in order],
        order,
        partners,
    )
    far = spread_far(upstream, near, zero)
    order = (3, 5, 6, 7)
    row_blocks = run_weights(
        down_here,
        factor_cols,
        [far[k] for k in order],
        [turned_all[k] for k in order],
        order,
        partners,
        gradient,
    )
    *updated, peaks = run_rows(exchange(row_blocks), sources, [result])
    updated, new_blocks = updated[:6], updated[6:]
    token_blocks = run_next(peaks, exchange(new_blocks), turned_all)
    next_hidden, peaks = run_join(exchange(token_blocks))
    new_scales = peaks[::2, 0] + scale_eps
    return (
        result[None],
        *(part[None] for part in updated),
        new_scales[None, :],
        next_hidden[None],
    )


def plain_plan(
    section_inputs,
    cotangent,
    norm_gain,
    quant_gate,
    quant_up,
    scales,
    down_proj,
    master_gate,
    master_up,
    moment_gate,
    moment_up,
    second_gate,
    second_up,
    next_inputs,
):
    gain_row = norm_gain[0]
    scale_pair = scales[0]
    down_local = down_proj[0]
    hidden_count = quant_gate.shape[2]
    sections = lax.axis_size("section")
    position = lax.axis_index("section")
    is_last = position == sections - 1
    both_full = lax.all_gather(
        jnp.concatenate([quant_gate[0], quant_up[0]], axis=1), "dp", axis=0, tiled=True
    )
    widened, inverse, normed = normalize(section_inputs[0], gain_row)
    both_pre = jnp.dot(normed, both_full, preferred_element_type=jnp.float32)
    gate_pre = both_pre[:, :hidden_count] * scale_pair[0]
    up_pre = both_pre[:, hidden_count:] * scale_pair[1]
    sigmoid = jax.nn.sigmoid(gate_pre)
    up_factor = gate_pre * sigmoid
    gate_factor = up_pre * (sigmoid * (1.0 + gate_pre * (1.0 - sigmoid)))
    cubed = inverse * inverse * inverse

    def stage(upstream):
        hidden_grad = transposed(upstream, down_local)
        gate_grad = (hidden_grad * gate_factor).astype(jnp.bfloat16)
        up_grad = (hidden_grad * up_factor).astype(jnp.bfloat16)
        normed_grad = (
            transposed(gate_grad, both_full[:, :hidden_count]) * scale_pair[0]
            + transposed(up_grad, both_full[:, hidden_count:]) * scale_pair[1]
        )
        gained = gain_row * normed_grad
        mean_term = jnp.mean(widened * gained, axis=-1, keepdims=True)
        result = upstream.astype(jnp.float32) + inverse * gained - widened * cubed * mean_term
        return (result.astype(jnp.bfloat16), gate_grad, up_grad)

    upstream = cotangent
    for turn in range(sections):
        result, gate_grad, up_grad = stage(upstream)
        if turn < sections - 1:
            incoming = lax.ppermute(
                result, "section", [(source, source - 1) for source in range(1, sections)]
            )
            upstream = jnp.where(is_last, cotangent, incoming)

    grads_all = jnp.concatenate([gate_grad, up_grad], axis=1)
    summed = lax.psum_scatter(
        lax.dot_general(
            normed, grads_all, (((0,), (0,)), ((), ())), preferred_element_type=jnp.float32
        ).astype(jnp.bfloat16),
        "dp",
        scatter_dimension=0,
        tiled=True,
    ).astype(jnp.float32)
    new_gate, mom_gate, sec_gate = adam_update(
        master_gate[0], moment_gate[0], second_gate[0], summed[:, :hidden_count]
    )
    new_up, mom_up, sec_up = adam_update(
        master_up[0], moment_up[0], second_up[0], summed[:, hidden_count:]
    )
    peaks = jnp.stack([jnp.max(jnp.abs(new_gate)), jnp.max(jnp.abs(new_up))])
    new_scales = ring_max(peaks, "dp") + scale_eps
    unused_one, unused_two, next_normed = normalize(next_inputs[0], gain_row)
    stacked = jnp.concatenate([new_gate, new_up], axis=1).astype(jnp.bfloat16)
    both_next = jnp.dot(
        next_normed,
        lax.all_gather(stacked, "dp", axis=0, tiled=True),
        preferred_element_type=jnp.float32,
    )
    next_hidden = (
        jax.nn.silu(both_next[:, :hidden_count]) * both_next[:, hidden_count:]
    ).astype(jnp.bfloat16)
    return (
        result[None],
        new_gate[None],
        new_up[None],
        mom_gate[None],
        mom_up[None],
        sec_gate[None],
        sec_up[None],
        new_scales[None, :],
        next_hidden[None],
    )


def solution(mesh):
    placed = (
        P("section", "dp", None),
        P("dp", None),
        P("section", None),
        P("section", "dp", None),
        P("section", "dp", None),
        P("section", None),
        P("section", None, None),
        P("section", "dp", None),
        P("section", "dp", None),
        P("section", "dp", None),
        P("section", "dp", None),
        P("section", "dp", None),
        P("section", "dp", None),
        P("section", "dp", None),
    )
    fits = mesh.shape["dp"] == 8 and mesh.shape["section"] >= 4
    return jax.shard_map(
        columns_plan if fits else plain_plan,
        mesh=mesh,
        in_specs=placed,
        out_specs=(
            P("section", "dp", None),
            P("section", "dp", None),
            P("section", "dp", None),
            P("section", "dp", None),
            P("section", "dp", None),
            P("section", "dp", None),
            P("section", "dp", None),
            P("section", None),
            P("section", "dp", None),
        ),
        check_vma=False,
    )
```

```python
import functools

import jax
import jax.numpy as jnp
from jax import lax
from jax.experimental import pallas as pl
from jax.experimental.pallas import tpu as pltpu
from jax.sharding import PartitionSpec as P

beta_one = 0.9
beta_two = 0.95
learn_rate = 0.002
decay_rate = 0.1
adam_steps = 100.0
norm_eps = 1e-06
adam_eps = 1e-08
scale_eps = 1e-06
mib = 1024 * 1024
bf16 = jnp.bfloat16
f32 = jnp.float32


def normalize(inputs, norm_gain):
    widened = inputs.astype(jnp.float32)
    inverse = lax.rsqrt(jnp.mean(widened * widened, axis=-1, keepdims=True) + norm_eps)
    return (widened, inverse, (widened * inverse * norm_gain).astype(jnp.bfloat16))


def matmul(first_op, second_op):
    return jnp.dot(first_op, second_op, preferred_element_type=jnp.float32)


def transposed(first_op, second_op):
    return lax.dot_general(
        first_op, second_op, (((1,), (1,)), ((), ())), preferred_element_type=jnp.float32
    )


def adam_update(master, moment_old, second_old, gradient):
    moment_one = beta_one * moment_old + (1.0 - beta_one) * gradient
    moment_two = beta_two * second_old + (1.0 - beta_two) * gradient * gradient
    unbiased_one = moment_one / (1.0 - beta_one**adam_steps)
    unbiased_two = moment_two / (1.0 - beta_two**adam_steps)
    updated = master - learn_rate * (
        unbiased_one / (jnp.sqrt(unbiased_two) + adam_eps) + decay_rate * master
    )
    return (updated, moment_one, moment_two)


def factors(gate_pre, up_pre):
    sigmoid = jax.nn.sigmoid(gate_pre)
    return (up_pre * (sigmoid * (1.0 + gate_pre * (1.0 - sigmoid))), gate_pre * sigmoid)


def exchange(blocks):
    got = {k: swap(blocks[k], k) for k in (6, 7, 2, 4, 3, 5, 1)}
    return [blocks[0]] + [got[k] for k in range(1, len(blocks))]


def swap(value, distance):
    pairs = [(source, source ^ distance) for source in range(lax.axis_size("dp"))]
    return lax.ppermute(value, "dp", pairs)


def swap_some(value, distance, core):
    pairs = [(k, k ^ distance) for k in range(lax.axis_size("dp")) if k % 2 == core]
    return lax.ppermute(value, "dp", pairs)


def spread_weights(gate, up, gate_again):
    near = [swap(part, distance) for distance in (2, 4) for part in (gate, up)]
    gate_x, up_x, gate_y, up_y = near
    gate_c, up_c = swap(gate_again, 1), swap(up, 1)
    gate_d, up_d = swap(gate_y, 2), swap(up_x, 4)
    return [
        (gate, up),
        (gate_c, up_c),
        (gate_x, up_x),
        (swap(gate_x, 1), swap(up_x, 1)),
        (gate_y, up_y),
        (swap(gate_y, 1), swap(up_y, 1)),
        (gate_d, up_d),
        (swap(gate_d, 1), swap(up_d, 1)),
    ]


def spread_near(value):
    return (swap(value, 1), swap(value, 2), swap(value, 4))


def spread_far(value, near, zero=None):
    across_c, across_x, across_y = near
    across_d = swap_some(across_y, 2, 0) + swap_some(across_x, 4, 1)
    if zero is not None:
        across_d = across_d + zero
    return [
        value,
        across_c,
        across_x,
        swap(across_x, 1),
        across_y,
        swap(across_y, 1),
        across_d,
        swap(across_d, 1),
    ]


def ring_max(value, axis):
    count = lax.axis_size(axis)
    span = 1
    while span < count:
        pairs = [(source, (source + span) % count) for source in range(count)]
        value = jnp.maximum(value, lax.ppermute(value, axis, pairs))
        span *= 2
    return value


def column_chunks(total, width=512):
    return [(start, min(width, total - start)) for start in range(0, total, width)]


def finish_stage(upstream, normed_grad, widened, gain_row):
    inverse = lax.rsqrt(jnp.mean(widened * widened, axis=1, keepdims=True) + norm_eps)
    gained = gain_row * normed_grad
    mean_term = jnp.mean(widened * gained, axis=1, keepdims=True)
    cubed = inverse * inverse * inverse
    return (upstream.astype(f32) + inverse * gained - widened * cubed * mean_term).astype(bf16)


def turn_kernel(
    inputs_ref, next_ref, gain_ref, shard_ref, down_hbm, turned_ref, shard_out, down, sem
):
    shard_out[...] = shard_ref[...]
    fetch = pltpu.make_async_copy(down_hbm, down, sem)
    fetch.start()
    features = inputs_ref.shape[1]
    turned_ref[:features] = normalize(inputs_ref[...], gain_ref[...])[2].T
    turned_ref[features:] = normalize(next_ref[...], gain_ref[...])[2].T
    fetch.wait()


def pass_kernel(value_ref, *rest):
    rest[-1][...] = value_ref[...]


def first_kernel(
    scale_ref, upstream_ref, inputs_ref, gain_ref, down, *refs, partners, sections
):
    pieces = refs[: 2 * partners]
    result_ref, cot_ref, gate_factor_ref, up_factor_ref, gate_full, up_full = refs[-6:]
    rows = pieces[0].shape[0]
    own = lax.axis_index("dp")
    for index in range(2 * partners):
        place = pl.ds(pl.multiple_of((own ^ (index // 2)) * rows, 16), rows)
        full = gate_full if index % 2 == 0 else up_full
        full[place, :] = pieces[index][...]
    upstream = upstream_ref[...]
    last = lax.axis_index("section") == sections - 1
    cot_ref[...] = upstream * jnp.where(last, 1.0, 0.0).astype(bf16)
    normed = normalize(inputs_ref[...], gain_ref[...])[2]
    normed_grad = jnp.zeros(upstream.shape, f32)
    for start, width in column_chunks(gate_full.shape[1]):
        part = slice(start, start + width)
        gate_part, up_part = gate_full[:, part], up_full[:, part]
        gate_factor, up_factor = factors(
            matmul(normed, gate_part) * scale_ref[0], matmul(normed, up_part) * scale_ref[1]
        )
        gate_factor = (gate_factor * scale_ref[0]).astype(bf16)
        up_factor = (up_factor * scale_ref[1]).astype(bf16)
        gate_factor_ref[:, part] = gate_factor
        up_factor_ref[:, part] = up_factor
        hidden_grad = transposed(upstream, down[part, :])
        normed_grad += transposed((hidden_grad * gate_factor).astype(bf16), gate_part)
        normed_grad += transposed((hidden_grad * up_factor).astype(bf16), up_part)
    result_ref[...] = finish_stage(
        upstream, normed_grad, inputs_ref[...].astype(f32), gain_ref[...]
    )


def stage_kernel(
    upstream_ref, inputs_ref, gain_ref, down, gate_full, up_full, gate_factor, up_factor, *rest
):
    passed = len(rest) // 2
    result_ref = rest[passed]
    for place in range(passed):
        rest[passed + 1 + place][...] = rest[place][...]
    upstream = upstream_ref[...]
    normed_grad = jnp.zeros(upstream.shape, f32)
    for start, width in column_chunks(gate_full.shape[1]):
        part = slice(start, start + width)
        hidden_grad = transposed(upstream, down[part, :])
        gate_grad = (hidden_grad * gate_factor[:, part]).astype(bf16)
        up_grad = (hidden_grad * up_factor[:, part]).astype(bf16)
        normed_grad += transposed(gate_grad, gate_full[:, part])
        normed_grad += transposed(up_grad, up_full[:, part])
    result_ref[...] = finish_stage(
        upstream, normed_grad, inputs_ref[...].astype(f32), gain_ref[...]
    )


def factors_kernel(scale_ref, gate_full, up_full, cot_ref, *refs, partners):
    pieces = refs[:partners]
    out_gate, out_up, cot_out, gate, up, normed, stack = refs[-7:]
    cot_out[...] = cot_ref[...]
    features, columns = gate.shape
    tokens = pieces[0].shape[1]
    group = normed.shape[0] // tokens
    own = lax.axis_index("dp")
    for k in range(partners):
        part = slice(k * columns, (k + 1) * columns)

        @pl.when(own == k)
        def pick():
            gate[...] = gate_full[:, part]
            up[...] = up_full[:, part]

    for k in range(partners):
        stack[k] = pieces[k][:features]

    def one_group(index, carry):
        for k in range(group):
            normed[k * tokens : (k + 1) * tokens, :] = stack[index * group + k].T
        rows = pl.ds(pl.multiple_of(index * (group * tokens), 16), group * tokens)
        gate_factor, up_factor = factors(
            matmul(normed[...], gate[...]) * scale_ref[0],
            matmul(normed[...], up[...]) * scale_ref[1],
        )
        out_gate[rows, :] = gate_factor.astype(bf16)
        out_up[rows, :] = up_factor.astype(bf16)
        return carry

    lax.fori_loop(0, partners // group, one_group, 0)


def weight_kernel(down_ref, gate_factor, up_factor, *refs, distances, first):
    count = len(distances)
    pieces, turned = refs[:count], refs[count : 2 * count]
    if first:
        out_ref, zero_ref = refs[-5:-3]
        zero_ref[...] = jnp.zeros(zero_ref.shape, bf16)
    else:
        start_ref = refs[2 * count]
        outs = refs[2 * count + 1 : -3]
    upstream, normed, total = refs[-3:]
    own = lax.axis_index("dp")
    tokens, features = pieces[0].shape
    columns = gate_factor.shape[1]
    factor_rows = []
    for place, distance in enumerate(distances):
        block = slice(place * tokens, (place + 1) * tokens)
        upstream[block, :] = pieces[place][...]
        normed[:, block] = turned[place][:features]
        factor_rows.append(slice(distance * tokens, (distance + 1) * tokens))
    down_cols = down_ref[pl.ds(pl.multiple_of(own * columns, 16), columns), :]
    hidden_grad = transposed(upstream[...], down_cols)
    gate_grad = hidden_grad * jnp.concatenate([gate_factor[rows, :] for rows in factor_rows], axis=0)
    up_grad = hidden_grad * jnp.concatenate([up_factor[rows, :] for rows in factor_rows], axis=0)
    grads = jnp.concatenate([gate_grad, up_grad], axis=1).astype(bf16)
    product = matmul(normed[...], grads)
    if first:
        out_ref[...] = product
        return
    total[...] = (start_ref[...] + product).astype(bf16)
    rows = outs[0].shape[0]
    for distance in range(len(outs)):
        place = pl.ds(pl.multiple_of((own ^ distance) * rows, 16), rows)
        outs[distance][...] = total[place, :]


def next_kernel(peak_ref, *refs, partners):
    rows_in, turned_parts = refs[:partners], refs[partners : 2 * partners]
    outs = refs[-3 - partners : -3]
    weights, turned, joined = refs[-3:]
    features = weights.shape[0]
    tokens = turned_parts[0].shape[1]
    columns = turned.shape[0] // 2
    group = joined.shape[1] // tokens
    own = lax.axis_index("dp")
    rows = rows_in[0].shape[0]
    for distance in range(partners):
        place = pl.ds(pl.multiple_of((own ^ distance) * rows, 16), rows)
        weights[place, :] = rows_in[distance][...]
    for start in range(0, features, 128):
        turned[:, start : start + 128] = weights[start : start + 128, :].T
    for first in range(0, partners, group):
        for k in range(group):
            joined[:, k * tokens : (k + 1) * tokens] = turned_parts[first + k][features:]
        both = matmul(turned[...], joined[...])
        gate, up = both[:columns], both[columns:]
        hidden = (gate * jax.nn.sigmoid(gate) * up).astype(bf16)
        for k in range(group):
            outs[first + k][:columns] = hidden[:, k * tokens : (k + 1) * tokens]
    rest = jnp.concatenate([peak_ref[...]] * (tokens // peak_ref.shape[1]), axis=1)
    parts = []
    for unused in range(2):
        parts.append(rest.astype(bf16))
        rest = rest - parts[-1].astype(f32)
    parts.append(rest.astype(bf16))
    extra = jnp.concatenate([part.astype(f32)[2:6] for part in parts + parts[-1:]], axis=0)
    for k in range(partners):
        outs[k][columns:] = extra.astype(bf16)


def join_kernel(*refs, partners):
    pieces = refs[:partners]
    out_ref, peak_ref, held = refs[partners:]
    own = lax.axis_index("dp")
    columns = held.shape[1]
    peaks = None
    for distance in range(partners):
        held[own ^ distance] = pieces[distance][:columns]
        parts = pieces[distance][columns:].astype(f32)
        value = parts[:4] + parts[4:8] + parts[8:12]
        peaks = value if peaks is None else jnp.maximum(peaks, value)
    peak_ref[...] = peaks
    for k in range(partners):
        out_ref[:, k * columns : (k + 1) * columns] = held[k].T


def rows_kernel(*refs, partners, unused_count):
    pieces, sources = refs[:partners], refs[partners : partners + 6]
    outs = refs[partners + 6 + unused_count :]
    targets, news, peak_ref = outs[:6], outs[6 : 6 + partners], outs[6 + partners]
    blocks, gradient = outs[7 + partners :]
    own = lax.axis_index("dp")
    columns = pieces[0].shape[1] // 2
    peaks = []
    for distance in range(partners):
        blocks[own ^ distance] = pieces[distance][...].astype(f32)
    for side in range(2):
        part = slice(side * columns, (side + 1) * columns)
        for k in range(partners):
            gradient[:, k * columns : (k + 1) * columns] = blocks[k, :, part]
        results = adam_update(
            sources[side][...], sources[2 + side][...], sources[4 + side][...], gradient[...]
        )
        for kind in range(3):
            targets[2 * kind + side][...] = results[kind]
        peaks.append(jnp.max(jnp.abs(results[0])))
        gradient[...] = results[0]
        for k in range(partners):
            blocks[k, :, part] = gradient[:, k * columns : (k + 1) * columns]
    for distance in range(partners):
        news[distance][...] = blocks[own ^ distance].astype(bf16)
    shape = (4, peak_ref.shape[1])
    both = jnp.concatenate([jnp.full(shape, peaks[0], f32), jnp.full(shape, peaks[1], f32)], axis=0)

    @pl.when(pl.program_id(0) == 0)
    def begin():
        peak_ref[...] = both

    @pl.when(pl.program_id(0) > 0)
    def further():
        peak_ref[...] = jnp.maximum(peak_ref[...], both)


def cost(flops, accessed):
    return pl.CostEstimate(flops=flops, bytes_accessed=accessed, transcendentals=0)


def smem_space():
    return pl.BlockSpec(memory_space=pltpu.SMEM)


def params(limit):
    return pltpu.CompilerParams(vmem_limit_bytes=limit * mib)


def whole(shape):
    return pl.BlockSpec(shape, lambda *unused: (0,) * len(shape))


def in_any(count):
    return [pl.BlockSpec(memory_space=pl.ANY)] * count


def in_vmem(count):
    return [pl.BlockSpec(memory_space=pltpu.VMEM)] * count


def run_turn(inputs, next_part, gain_row, shard, down):
    tokens, features = inputs.shape
    return pl.pallas_call(
        turn_kernel,
        out_shape=(
            jax.ShapeDtypeStruct((2 * features, tokens), bf16),
            jax.ShapeDtypeStruct(shard.shape, bf16),
            jax.ShapeDtypeStruct(down.shape, bf16),
        ),
        in_specs=in_vmem(4) + in_any(1),
        out_specs=tuple(in_vmem(3)),
        scratch_shapes=[pltpu.SemaphoreType.DMA],
        compiler_params=params(6),
        name="turn",
    )(inputs, next_part, gain_row, shard, down)


def run_pass(value, arrived):
    return pl.pallas_call(
        pass_kernel,
        out_shape=jax.ShapeDtypeStruct(value.shape, bf16),
        in_specs=in_vmem(1) + in_any(len(arrived)),
        out_specs=in_vmem(1)[0],
        compiler_params=params(4),
        name="pass_on",
    )(value, *arrived)


def run_first(scale_pair, upstream, inputs, gain, down, pieces, arrived, sections):
    tokens, features = upstream.shape
    hidden = down.shape[0]
    partners = len(pieces)
    flat = [part for pair in pieces for part in pair]
    return pl.pallas_call(
        functools.partial(first_kernel, partners=partners, sections=sections),
        out_shape=(
            jax.ShapeDtypeStruct((tokens, features), bf16),
            jax.ShapeDtypeStruct((tokens, features), bf16),
            jax.ShapeDtypeStruct((tokens, hidden), bf16),
            jax.ShapeDtypeStruct((tokens, hidden), bf16),
            jax.ShapeDtypeStruct((features, hidden), bf16),
            jax.ShapeDtypeStruct((features, hidden), bf16),
        ),
        in_specs=[smem_space()]
        + in_vmem(4 + len(flat))
        + in_any(len(arrived)),
        out_specs=tuple(in_vmem(6)),
        compiler_params=params(14),
        cost_estimate=cost(10 * tokens * features * hidden, 26 * features * hidden),
        name="first_stage",
    )(scale_pair, upstream, inputs, gain, down, *flat, *arrived)


def run_stage(
    upstream, inputs, gain, down, gate_full, up_full, gate_factor, up_factor, passed
):
    tokens, features = upstream.shape
    hidden = down.shape[0]
    return pl.pallas_call(
        stage_kernel,
        out_shape=(jax.ShapeDtypeStruct((tokens, features), bf16),)
        + tuple(jax.ShapeDtypeStruct(part.shape, bf16) for part in passed),
        in_specs=in_vmem(8 + len(passed)),
        out_specs=tuple(in_vmem(1 + len(passed))),
        compiler_params=params(10),
        cost_estimate=cost(6 * tokens * features * hidden, 8 * features * hidden),
        name="stage",
    )(upstream, inputs, gain, down, gate_full, up_full, gate_factor, up_factor, *passed)


def run_factors(scale_pair, gate_full, up_full, cotangent, pieces):
    partners = len(pieces)
    features, hidden = gate_full.shape
    tokens = pieces[0].shape[1]
    columns = hidden // partners
    shape = jax.ShapeDtypeStruct((partners * tokens, columns), bf16)
    return pl.pallas_call(
        functools.partial(factors_kernel, partners=partners),
        out_shape=(shape, shape, jax.ShapeDtypeStruct(cotangent.shape, bf16)),
        in_specs=[smem_space()] + in_vmem(3 + partners),
        out_specs=tuple(in_vmem(3)),
        scratch_shapes=[
            pltpu.VMEM((features, columns), bf16),
            pltpu.VMEM((features, columns), bf16),
            pltpu.VMEM((partners * tokens // 2, features), bf16),
            pltpu.VMEM((partners, features, tokens), bf16),
        ],
        compiler_params=params(18),
        cost_estimate=cost(4 * partners * tokens * features * columns, 8 * features * columns),
        name="column_factors",
    )(scale_pair, gate_full, up_full, cotangent, *pieces)


def run_weights(down, factor_cols, pieces, turned, distances, partners, start=None):
    tokens, features = pieces[0].shape
    columns = factor_cols[0].shape[1]
    count = len(distances)
    first = start is None
    if first:
        shapes = (
            jax.ShapeDtypeStruct((features, 2 * columns), f32),
            jax.ShapeDtypeStruct((tokens, features), bf16),
        )
        starts = []
    else:
        block = jax.ShapeDtypeStruct((features // partners, 2 * columns), bf16)
        shapes = (block,) * partners
        starts = [start]
    return pl.pallas_call(
        functools.partial(weight_kernel, distances=distances, first=first),
        out_shape=shapes,
        in_specs=in_vmem(3 + 2 * count + len(starts)),
        out_specs=tuple(in_vmem(len(shapes))),
        scratch_shapes=[
            pltpu.VMEM((count * tokens, features), bf16),
            pltpu.VMEM((features, count * tokens), bf16),
            pltpu.VMEM((features, 2 * columns), bf16),
        ],
        compiler_params=params(18),
        cost_estimate=cost(6 * count * tokens * features * columns, 12 * features * columns),
        name="column_gradients",
    )(down, *factor_cols, *pieces, *turned, *starts)


def run_next(peaks, rows_in, turned):
    partners = len(turned)
    rows, both = rows_in[0].shape
    tokens = turned[0].shape[1]
    features = partners * rows
    return pl.pallas_call(
        functools.partial(next_kernel, partners=partners),
        out_shape=(jax.ShapeDtypeStruct((both // 2 + 16, tokens), bf16),) * partners,
        in_specs=in_vmem(1 + 2 * partners),
        out_specs=tuple(in_vmem(partners)),
        scratch_shapes=[
            pltpu.VMEM((features, both), bf16),
            pltpu.VMEM((both, features), bf16),
            pltpu.VMEM((features, partners * tokens // 2), bf16),
        ],
        compiler_params=params(18),
        cost_estimate=cost(2 * partners * tokens * features * both, 16 * features * both),
        name="next_columns",
    )(peaks, *rows_in, *turned)


def run_join(pieces):
    partners = len(pieces)
    columns, tokens = pieces[0].shape[0] - 16, pieces[0].shape[1]
    return pl.pallas_call(
        functools.partial(join_kernel, partners=partners),
        out_shape=(
            jax.ShapeDtypeStruct((tokens, partners * columns), bf16),
            jax.ShapeDtypeStruct((4, tokens), f32),
        ),
        in_specs=in_vmem(partners),
        out_specs=tuple(in_vmem(2)),
        scratch_shapes=[pltpu.VMEM((partners, columns, tokens), bf16)],
        compiler_params=params(8),
        name="next_join",
    )(*pieces)


def run_rows(pieces, sources, arrived):
    partners = len(pieces)
    rows, hidden = sources[0].shape
    both = pieces[0].shape[1]
    step = 16
    row_spec = pl.BlockSpec((step, hidden), lambda i: (i, 0))
    block_spec = pl.BlockSpec((step, both), lambda i: (i, 0))
    return pl.pallas_call(
        functools.partial(rows_kernel, partners=partners, unused_count=len(arrived)),
        grid=(rows // step,),
        out_shape=(jax.ShapeDtypeStruct((rows, hidden), f32),) * 6
        + (jax.ShapeDtypeStruct((rows, both), bf16),) * partners
        + (jax.ShapeDtypeStruct((8, 128), f32),),
        in_specs=[block_spec] * partners + [row_spec] * 6 + in_any(len(arrived)),
        out_specs=(row_spec,) * 6 + (block_spec,) * partners + (whole((8, 128)),),
        scratch_shapes=[
            pltpu.VMEM((partners, step, both), f32),
            pltpu.VMEM((step, hidden), f32),
        ],
        compiler_params=params(10),
        cost_estimate=cost(40 * rows * hidden, 48 * rows * hidden),
        name="row_update",
    )(*pieces, *sources, *arrived)


def down_shift(value, sections):
    return lax.ppermute(value, "section", [(source, source - 1) for source in range(1, sections)])


def columns_plan(
    section_inputs,
    cotangent,
    norm_gain,
    quant_gate,
    quant_up,
    scales,
    down_proj,
    master_gate,
    master_up,
    moment_gate,
    moment_up,
    second_gate,
    second_up,
    next_inputs,
):
    gain_row = norm_gain[0]
    scale_pair = scales[0]
    down_local = down_proj[0]
    inputs = section_inputs[0]
    partners = lax.axis_size("dp")
    sections = lax.axis_size("section")
    gain = gain_row[None]
    sources = [
        part[0]
        for part in (master_gate, master_up, moment_gate, moment_up, second_gate, second_up)
    ]

    turned, gate_again, down_here = run_turn(
        inputs, next_inputs[0], gain, quant_gate[0], down_local
    )
    weight_pieces = spread_weights(quant_gate[0], quant_up[0], gate_again)
    turned = run_pass(turned, weight_pieces[6])
    across_c, across_x, across_y = spread_near(turned)
    result, cotangent_here, gate_factor, up_factor, gate_full, up_full = run_first(
        scale_pair, cotangent, inputs, gain, down_here, weight_pieces, [turned], sections
    )

    def next_stage(upstream, passed):
        return run_stage(
            upstream, inputs, gain, down_here, gate_full, up_full, gate_factor, up_factor, passed
        )

    for turn in range(sections - 1):
        incoming = down_shift(result, sections)
        if turn == sections - 2:
            *factor_cols, cotangent_here = run_factors(
                scale_pair, gate_full, up_full, cotangent_here, turned_all
            )
        upstream = cotangent_here + incoming
        if turn == 0:
            result, across_x, across_y = next_stage(upstream, [across_x, across_y])
            turned_all = spread_far(turned, (across_c, across_x, across_y))
        elif turn < sections - 2:
            (result,) = next_stage(upstream, [])
    (result,) = next_stage(upstream, [])
    near = spread_near(upstream)
    order = (0, 1, 2, 4)
    gradient, zero = run_weights(
        down_here,
        factor_cols,
        [upstream, *near],
        [turned_all[k] for k in order],
        order,
        partners,
    )
    far = spread_far(upstream, near, zero)
    order = (3, 5, 6, 7)
    row_blocks = run_weights(
        down_here,
        factor_cols,
        [far[k] for k in order],
        [turned_all[k] for k in order],
        order,
        partners,
        gradient,
    )
    *updated, peaks = run_rows(exchange(row_blocks), sources, [result])
    updated, new_blocks = updated[:6], updated[6:]
    token_blocks = run_next(peaks, exchange(new_blocks), turned_all)
    next_hidden, peaks = run_join(exchange(token_blocks))
    new_scales = peaks[::2, 0] + scale_eps
    return (
        result[None],
        *(part[None] for part in updated),
        new_scales[None, :],
        next_hidden[None],
    )


def plain_plan(
    section_inputs,
    cotangent,
    norm_gain,
    quant_gate,
    quant_up,
    scales,
    down_proj,
    master_gate,
    master_up,
    moment_gate,
    moment_up,
    second_gate,
    second_up,
    next_inputs,
):
    gain_row = norm_gain[0]
    scale_pair = scales[0]
    down_local = down_proj[0]
    hidden_count = quant_gate.shape[2]
    sections = lax.axis_size("section")
    position = lax.axis_index("section")
    is_last = position == sections - 1
    both_full = lax.all_gather(
        jnp.concatenate([quant_gate[0], quant_up[0]], axis=1), "dp", axis=0, tiled=True
    )
    widened, inverse, normed = normalize(section_inputs[0], gain_row)
    both_pre = jnp.dot(normed, both_full, preferred_element_type=jnp.float32)
    gate_pre = both_pre[:, :hidden_count] * scale_pair[0]
    up_pre = both_pre[:, hidden_count:] * scale_pair[1]
    sigmoid = jax.nn.sigmoid(gate_pre)
    up_factor = gate_pre * sigmoid
    gate_factor = up_pre * (sigmoid * (1.0 + gate_pre * (1.0 - sigmoid)))
    cubed = inverse * inverse * inverse

    def stage(upstream):
        hidden_grad = transposed(upstream, down_local)
        gate_grad = (hidden_grad * gate_factor).astype(jnp.bfloat16)
        up_grad = (hidden_grad * up_factor).astype(jnp.bfloat16)
        normed_grad = (
            transposed(gate_grad, both_full[:, :hidden_count]) * scale_pair[0]
            + transposed(up_grad, both_full[:, hidden_count:]) * scale_pair[1]
        )
        gained = gain_row * normed_grad
        mean_term = jnp.mean(widened * gained, axis=-1, keepdims=True)
        result = upstream.astype(jnp.float32) + inverse * gained - widened * cubed * mean_term
        return (result.astype(jnp.bfloat16), gate_grad, up_grad)

    upstream = cotangent
    for turn in range(sections):
        result, gate_grad, up_grad = stage(upstream)
        if turn < sections - 1:
            incoming = lax.ppermute(
                result, "section", [(source, source - 1) for source in range(1, sections)]
            )
            upstream = jnp.where(is_last, cotangent, incoming)

    grads_all = jnp.concatenate([gate_grad, up_grad], axis=1)
    summed = lax.psum_scatter(
        lax.dot_general(
            normed, grads_all, (((0,), (0,)), ((), ())), preferred_element_type=jnp.float32
        ).astype(jnp.bfloat16),
        "dp",
        scatter_dimension=0,
        tiled=True,
    ).astype(jnp.float32)
    new_gate, mom_gate, sec_gate = adam_update(
        master_gate[0], moment_gate[0], second_gate[0], summed[:, :hidden_count]
    )
    new_up, mom_up, sec_up = adam_update(
        master_up[0], moment_up[0], second_up[0], summed[:, hidden_count:]
    )
    peaks = jnp.stack([jnp.max(jnp.abs(new_gate)), jnp.max(jnp.abs(new_up))])
    new_scales = ring_max(peaks, "dp") + scale_eps
    unused_one, unused_two, next_normed = normalize(next_inputs[0], gain_row)
    stacked = jnp.concatenate([new_gate, new_up], axis=1).astype(jnp.bfloat16)
    both_next = jnp.dot(
        next_normed,
        lax.all_gather(stacked, "dp", axis=0, tiled=True),
        preferred_element_type=jnp.float32,
    )
    next_hidden = (
        jax.nn.silu(both_next[:, :hidden_count]) * both_next[:, hidden_count:]
    ).astype(jnp.bfloat16)
    return (
        result[None],
        new_gate[None],
        new_up[None],
        mom_gate[None],
        mom_up[None],
        sec_gate[None],
        sec_up[None],
        new_scales[None, :],
        next_hidden[None],
    )


def solution(mesh):
    placed = (
        P("section", "dp", None),
        P("dp", None),
        P("section", None),
        P("section", "dp", None),
        P("section", "dp", None),
        P("section", None),
        P("section", None, None),
        P("section", "dp", None),
        P("section", "dp", None),
        P("section", "dp", None),
        P("section", "dp", None),
        P("section", "dp", None),
        P("section", "dp", None),
        P("section", "dp", None),
    )
    fits = mesh.shape["dp"] == 8 and mesh.shape["section"] >= 4
    return jax.shard_map(
        columns_plan if fits else plain_plan,
        mesh=mesh,
        in_specs=placed,
        out_specs=(
            P("section", "dp", None),
            P("section", "dp", None),
            P("section", "dp", None),
            P("section", "dp", None),
            P("section", "dp", None),
            P("section", "dp", None),
            P("section", "dp", None),
            P("section", None),
            P("section", "dp", None),
        ),
        check_vma=False,
    )
```
